32 devices in a mesh: bucket: 4 (over y, core), dp: 8 (over z, x).
Axes of the slice: x: 2, y: 2, z: 4, core: 2. Of those that a mesh axis runs over, the one named last changes fastest.
Arguments:
- filter_bank: bfloat16 [128, 256, 320], P(('bucket', 'dp')), may hold values from -6 to 6
- frame_len: int32 [128], P(('bucket', 'dp')), may hold values from 1 to 256, as said below
- tok_len: int32 [128], P(('bucket', 'dp')), may hold values from 1 to 31, as said below
- targets: int32 [128, 32], P(('bucket', 'dp')), may hold values from 1 to 4998
- w_sub: bfloat16 [320, 256], replicated, may hold values from -0.3125 to 0.3125
- enc_attn: bfloat16 [256, 1024], replicated, may hold values from -0.375 to 0.375
- enc_ff1: bfloat16 [256, 2048], replicated, may hold values from -0.375 to 0.375
- enc_ff2: bfloat16 [2048, 256], replicated, may hold values from -0.125 to 0.125
- dec_self: bfloat16 [256, 1024], replicated, may hold values from -0.375 to 0.375
- dec_cross: bfloat16 [256, 1024], replicated, may hold values from -0.375 to 0.375
- dec_ff1: bfloat16 [256, 2048], replicated, may hold values from -0.375 to 0.375
- dec_ff2: bfloat16 [2048, 256], replicated, may hold values from -0.125 to 0.125
- embed: bfloat16 [5000, 256], replicated, may hold values from -0.375 to 0.375
- ctc_head: bfloat16 [256, 5000], replicated, may hold values from -0.375 to 0.375
- out_head: bfloat16 [256, 5000], replicated, may hold values from -0.375 to 0.375
- norm_gain: bfloat16 [7, 256], replicated, may hold values from 0.5 to 1.5
- norm_bias: bfloat16 [7, 256], replicated, may hold values from -0.29882812 to 0.29882812
- master: float32 [6809088], P(('bucket', 'dp')), may hold values from -0.3 to 0.3
- moment1: float32 [6809088], P(('bucket', 'dp')), may hold values from -0.001532906 to 0.001532906
- moment2: float32 [6809088], P(('bucket', 'dp')), may hold values from 7.343127e-08 to 1.1749004e-06
Outputs:
- loss: float32 [], replicated
- clip_norm: float32 [], replicated
- moment1_new: float32 [6809088], P(('bucket', 'dp'))
- moment2_new: float32 [6809088], P(('bucket', 'dp'))
- master_new: float32 [6809088], P(('bucket', 'dp'))
- weights_new: bfloat16 [6809088], P(('bucket', 'dp'))
- weight_norms: float32 [13], replicated
- update_norms: float32 [13], replicated
The draws below stay inside these ranges and needn't reach their ends.
Inputs may be any that keep to these rules, and one draw needn't show every extreme that they name: `frame_len`: utterance r is of length group g = r % 4, with frames in [256 g // 4 + 1, 256 (g + 1) // 4] but never under 4; some utterance has 256. `tok_len`: at most frame_len // 3; some utterance has 31.
All inputs are finite; a program needn't handle non-finite values.
Results may differ from the reference program's by a relative error of at most 0.0025.
Values may be sent and summed in bfloat16 or wider, within the bound.
A program may use at most 384 MiB of HBM per device.

```python
import math
import jax
import jax.numpy as jnp
from jax import lax

D = 256
HEADS = 4
FF = 2048
VOCAB = 5000
FEAT = 320
FR = 256
TCAP = 32
STEP = 5
UTTS = 128
PARAMS = 6809088
N_BUCKET = 4
N_DP = 8


def length_pair(key):
    places = jnp.arange(UTTS)
    length_group = places % N_BUCKET
    upper = FR * (length_group + 1) // N_BUCKET
    lower = jnp.maximum(FR * length_group // N_BUCKET + 1, jnp.minimum(4, upper))
    frames = lower + jax.random.randint(jax.random.fold_in(key, 101), (UTTS,), 0, 1 << 20) % (upper - lower + 1)
    frames = jnp.where(places == N_BUCKET - 1, FR, frames)
    allowed = jnp.minimum(TCAP - 1, frames // 3)
    tokens = 1 + jax.random.randint(jax.random.fold_in(key, 102), (UTTS,), 0, 1 << 20) % allowed
    tokens = jnp.where(places == N_BUCKET - 1, TCAP - 1, tokens)
    return (frames.astype(jnp.int32), tokens.astype(jnp.int32))


def draw_frame_len(key, part):
    return length_pair(key)[0]


def draw_tok_len(key, part):
    return length_pair(key)[1]


def set_ends(array, own_key, least, largest):
    dims = array.shape
    spot = [jax.random.randint(jax.random.fold_in(own_key, axis), (), 0, dims[axis]) for axis in range(len(dims))]
    array = array.at[tuple(spot)].set(least)
    longest = dims.index(max(dims))
    spot[longest] = (spot[longest] + 1) % dims[longest]
    return array.at[tuple(spot)].set(largest)


def steps_of(stream_key, extent, shards, least, high):
    loudness = 1.0
    for axis_at, blocks in shards:
        heights = jax.random.uniform(jax.random.fold_in(jax.random.fold_in(stream_key, 6), axis_at), (blocks,), jnp.float32, least / len(shards), high / len(shards))
        loudness = loudness * jnp.repeat(jnp.exp(heights), extent[axis_at] // blocks).reshape((-1,) + (1,) * (len(extent) - 1 - axis_at))
    return loudness


def bell_draw(stream_key, extent, scale, limit, cuts=(), kind=jnp.bfloat16):
    values = jax.random.normal(stream_key, extent, jnp.float32) * scale
    if len(cuts) > 0:
        values = steps_of(stream_key, extent, cuts, -0.22, 0.18) * values
    return jnp.clip(values, min=-limit, max=limit).astype(kind)


def setup_inputs(seed: int = 0) -> dict:
    arg_keys = jax.random.split(jax.random.key(seed), 21)
    return {
        "filter_bank": bell_draw(arg_keys[0], (UTTS, FR, FEAT), 1.0, 6.0, ((0, 32),)),
        "frame_len": draw_frame_len(jax.random.fold_in(arg_keys[20], 71), 0),
        "tok_len": draw_tok_len(jax.random.fold_in(arg_keys[20], 71), 0),
        "targets": set_ends(jax.random.randint(arg_keys[3], (UTTS, TCAP), 1, VOCAB - 1), jax.random.fold_in(arg_keys[3], 1), 1, (VOCAB - 1) - 1).astype(jnp.int32),
        "w_sub": bell_draw(arg_keys[4], (FEAT, D), FEAT ** -0.5, 0.3125),
        "enc_attn": bell_draw(arg_keys[5], (D, 4 * D), D ** -0.5, 0.375),
        "enc_ff1": bell_draw(arg_keys[6], (D, FF), D ** -0.5, 0.375),
        "enc_ff2": bell_draw(arg_keys[7], (FF, D), FF ** -0.5, 0.125),
        "dec_self": bell_draw(arg_keys[8], (D, 4 * D), D ** -0.5, 0.375),
        "dec_cross": bell_draw(arg_keys[9], (D, 4 * D), D ** -0.5, 0.375),
        "dec_ff1": bell_draw(arg_keys[10], (D, FF), D ** -0.5, 0.375),
        "dec_ff2": bell_draw(arg_keys[11], (FF, D), FF ** -0.5, 0.125),
        "embed": bell_draw(arg_keys[12], (VOCAB, D), D ** -0.5, 0.375),
        "ctc_head": bell_draw(arg_keys[13], (D, VOCAB), D ** -0.5, 0.375),
        "out_head": bell_draw(arg_keys[14], (D, VOCAB), D ** -0.5, 0.375),
        "norm_gain": jnp.clip(1.0 + 0.1 * jax.random.normal(arg_keys[15], (7, D), jnp.float32), 0.5, 1.5).astype(jnp.bfloat16),
        "norm_bias": jnp.clip(jax.random.uniform(arg_keys[16], (7, D), jnp.float32, -0.29882812, 0.29882812), -0.29882812, 0.29882812).astype(jnp.bfloat16),
        "master": bell_draw(arg_keys[17], (PARAMS,), 0.05, 0.3, ((0, 32),), jnp.float32),
        "moment1": bell_draw(arg_keys[18], (PARAMS,), (PARAMS ** -0.5), 0.001532906, ((0, 32),), jnp.float32),
        "moment2": jnp.clip(jnp.exp(math.log(1.1749003760996857e-06) - 2.7725887 * jax.random.uniform(arg_keys[19], (PARAMS,), jnp.float32) ** steps_of(arg_keys[19], (PARAMS,), ((0, 32),), -0.2, 0.2)), 7.343127350623035e-08, 1.1749003760996857e-06),
    }


@jax.custom_vjp
def low(v):
    return lax.optimization_barrier(v.astype(jnp.bfloat16)).astype(jnp.float32)

@jax.custom_vjp
def low_back(v):
    return v

def low_keep(v):
    return (low(v), None)

def low_pass(kept, grad):
    return (grad,)

def back_keep(v):
    return (v, None)

def back_low(kept, grad):
    return (low(grad),)
low.defvjp(low_keep, low_pass)
low_back.defvjp(back_keep, back_low)
NEG_SCORE = -1000000000.0
NEG_PATH = -100000.0
HIGHEST = lax.Precision.HIGHEST

def positions(length, width):
    place = jnp.arange(length, dtype=jnp.float32)[:, None]
    freqs = jnp.exp(jnp.arange(0, width, 2, dtype=jnp.float32) * (-math.log(10000.0) / width))
    angles = place * freqs[None, :]
    return jnp.stack([jnp.sin(angles), jnp.cos(angles)], axis=-1).reshape(length, width)

def layer_norm(values, gain_row, bias_row):
    centre = values - lax.optimization_barrier(jnp.mean(values, axis=-1, keepdims=True))
    spread = lax.optimization_barrier(jnp.mean(centre * centre, axis=-1, keepdims=True))
    return centre * lax.rsqrt(spread + 1e-05) * gain_row + bias_row

def linear(values, matrix):
    return low_back(jnp.einsum('btk,kn->btn', low(values), matrix, precision=HIGHEST))

def log_softmax(values):
    shifted = values - lax.optimization_barrier(jnp.max(values, axis=-1, keepdims=True))
    return shifted - jnp.log(lax.optimization_barrier(jnp.sum(jnp.exp(shifted), axis=-1, keepdims=True)))

def attention(query, keys, values, allowed):
    batch, rows_q, width = query.shape
    rows_k = keys.shape[1]
    size = width // HEADS
    qpart = low(query).reshape(batch, rows_q, HEADS, size)
    kpart = low(keys).reshape(batch, rows_k, HEADS, size)
    vpart = low(values).reshape(batch, rows_k, HEADS, size)
    scores = low_back(jnp.einsum('bqhe,bkhe->bhqk', qpart, kpart, precision=HIGHEST) / math.sqrt(size))
    scores = jnp.where(allowed[:, None], scores, NEG_SCORE)
    probs = jnp.exp(log_softmax(scores))
    context = low_back(jnp.einsum('bhqk,bkhe->bqhe', low(probs), vpart, precision=HIGHEST))
    return context.reshape(batch, rows_q, width)

def feed_forward(values, first, second):
    inner = linear(values, first)
    return linear(inner * jax.nn.sigmoid(inner), second)

def encode(weights, frames_in, frame_len):
    w_sub, enc_attn, enc_ff1, enc_ff2 = weights[:4]
    gains, biases = (weights[11], weights[12])
    batch, length, _ = frames_in.shape
    width = w_sub.shape[1]
    hidden = linear(frames_in, w_sub) + positions(length, width)[None]
    valid = jnp.arange(length)[None, :] < frame_len[:, None]
    allowed = jnp.broadcast_to(valid[:, None, :], (batch, length, length))
    mixed = linear(layer_norm(hidden, gains[0], biases[0]), enc_attn[:, :3 * width])
    context = attention(mixed[..., :width], mixed[..., width:2 * width], mixed[..., 2 * width:], allowed)
    hidden = hidden + linear(context, enc_attn[:, 3 * width:])
    hidden = hidden + feed_forward(layer_norm(hidden, gains[1], biases[1]), enc_ff1, enc_ff2)
    return low_back(low(layer_norm(hidden, gains[2], biases[2])))

def log_add(first, second, third):
    peak = jnp.maximum(jnp.maximum(first, second), third)
    return peak + jnp.log(jnp.exp(first - peak) + jnp.exp(second - peak) + jnp.exp(third - peak))

def ctc_path(logp, labels, frame_count, token_count):
    length = logp.shape[0]
    states = 2 * labels.shape[0] + 1
    index = jnp.arange(states)
    padded = jnp.concatenate([labels, jnp.zeros((1,), jnp.int32)])
    extended = jnp.where(index % 2 == 1, padded[index // 2], 0).astype(jnp.int32)
    earlier = jnp.concatenate([jnp.full((2,), -1, jnp.int32), extended[:-2]])
    can_skip = (index % 2 == 1) & (extended != earlier) & (index >= 2)
    emitted = jnp.take(logp, extended, axis=1)
    start = jnp.where(index < 2, emitted[0], NEG_PATH)

    def advance(alpha, inputs):
        emit_row, moment = inputs
        filler = jnp.full((2,), NEG_PATH, alpha.dtype)
        single = jnp.concatenate([filler[:1], alpha[:-1]])
        double = jnp.where(can_skip, jnp.concatenate([filler, alpha[:-2]]), NEG_PATH)
        fresh = log_add(alpha, single, double) + emit_row
        return (jnp.where(moment < frame_count, fresh, alpha), None)
    alpha, _ = lax.scan(advance, start, (emitted[1:], jnp.arange(1, length)))
    final = alpha[2 * token_count]
    before = alpha[2 * token_count - 1]
    return -log_add(final, before, jnp.full_like(final, NEG_PATH * 10.0))

def head(weights, encoded, frame_len, tok_len, targets):
    dec_self, dec_cross, dec_ff1, dec_ff2, embed, ctc_head, out_head = weights[4:11]
    gains, biases = (weights[11], weights[12])
    batch, length, width = encoded.shape
    tokens = targets.shape[1]
    vocab = embed.shape[0]
    marker = vocab - 1
    ctc_logp = log_softmax(linear(encoded, ctc_head))
    ctc_loss = jax.vmap(ctc_path)(ctc_logp, targets, frame_len, tok_len)
    inputs = jnp.concatenate([jnp.full((batch, 1), marker, jnp.int32), targets[:, :-1]], axis=1)
    hidden = jnp.take(embed, inputs, axis=0) * math.sqrt(width) + positions(tokens, width)[None]
    causal = jnp.broadcast_to(jnp.tril(jnp.ones((tokens, tokens), bool))[None], (batch, tokens, tokens))
    mixed = linear(layer_norm(hidden, gains[3], biases[3]), dec_self[:, :3 * width])
    context = attention(mixed[..., :width], mixed[..., width:2 * width], mixed[..., 2 * width:], causal)
    hidden = hidden + linear(context, dec_self[:, 3 * width:])
    query = linear(layer_norm(hidden, gains[4], biases[4]), dec_cross[:, :width])
    memory = linear(encoded, dec_cross[:, width:3 * width])
    valid = jnp.arange(length)[None, :] < frame_len[:, None]
    allowed = jnp.broadcast_to(valid[:, None, :], (batch, tokens, length))
    context = attention(query, memory[..., :width], memory[..., width:], allowed)
    hidden = hidden + linear(context, dec_cross[:, 3 * width:])
    hidden = hidden + feed_forward(layer_norm(hidden, gains[5], biases[5]), dec_ff1, dec_ff2)
    logq = log_softmax(linear(layer_norm(hidden, gains[6], biases[6]), out_head))
    place = jnp.arange(tokens)[None, :]
    wanted = jnp.where(place == tok_len[:, None], marker, targets).astype(jnp.int32)
    picked = jnp.take_along_axis(logq, wanted[..., None], axis=-1)[..., 0]
    others = lax.optimization_barrier(jnp.sum(logq, axis=-1)) - picked
    per_token = -(0.9 * picked + 0.1 / (vocab - 1) * others)
    att_loss = lax.optimization_barrier(jnp.sum(jnp.where(place <= tok_len[:, None], per_token, 0.0), axis=1))
    return jnp.sum(0.3 * ctc_loss + 0.7 * att_loss)

def to_rows(matrices, devices):
    return jnp.concatenate([matrix.reshape(devices, -1) for matrix in matrices], axis=1)

def per_matrix(values, widths):
    sums, offset = ([], 0)
    for width in widths:
        sums.append(jnp.sum(values[..., offset:offset + width]))
        offset += width
    return jnp.stack(sums)

def expand(scales, widths):
    return jnp.concatenate([jnp.broadcast_to(scales[place], (width,)) for place, width in enumerate(widths)])

def reference(filter_bank, frame_len, tok_len, targets, w_sub, enc_attn, enc_ff1, enc_ff2, dec_self, dec_cross, dec_ff1, dec_ff2, embed, ctc_head, out_head, norm_gain, norm_bias, master, moment1, moment2):
    weights = tuple((item.astype(jnp.float32) for item in (w_sub, enc_attn, enc_ff1, enc_ff2, dec_self, dec_cross, dec_ff1, dec_ff2, embed, ctc_head, out_head, norm_gain, norm_bias)))
    devices = N_BUCKET * N_DP
    blocks = UTTS // 32
    pieces = (filter_bank.reshape(blocks, 32, FR, FEAT), frame_len.reshape(blocks, 32), tok_len.reshape(blocks, 32), targets.reshape(blocks, 32, TCAP))

    def total(params):

        def block_loss(piece):
            frames_in, lengths, counts, labels = piece
            return head(params, encode(params, frames_in.astype(jnp.float32), lengths), lengths, counts, labels)
        return jnp.sum(lax.map(jax.checkpoint(block_loss), pieces))
    loss_sum, pull = jax.vjp(total, weights)
    grads, = pull(jnp.asarray(1.0 / UTTS, loss_sum.dtype))
    widths = [item.size // devices for item in weights]
    rows = to_rows(grads, devices)
    clip_norm = jnp.sqrt(jnp.sum(rows * rows))
    scaled = rows * jnp.minimum(1.0, 1.0 / clip_norm)
    old_weights = master.reshape(devices, -1)
    first = 0.5 * moment1.reshape(devices, -1) + 0.5 * scaled
    second = 0.5 * moment2.reshape(devices, -1) + 0.5 * scaled * scaled
    correct = 1.0 - 0.5 ** STEP
    direction = first / correct / (jnp.sqrt(second / correct) + 1e-06) + 0.01 * old_weights
    weight_norms = jnp.sqrt(per_matrix(old_weights * old_weights, widths))
    update_norms = jnp.sqrt(per_matrix(direction * direction, widths))
    ratio = expand(0.5 * weight_norms / update_norms, widths)
    fresh = old_weights - ratio[None, :] * direction
    return (loss_sum / UTTS, clip_norm, first.reshape(-1), second.reshape(-1), fresh.reshape(-1), fresh.reshape(-1).astype(jnp.bfloat16), weight_norms, update_norms)
```

```python
import functools
import math

import jax
import jax.numpy as jnp
import numpy as np
from jax import lax
from jax.experimental import pallas as pl
from jax.experimental.pallas import tpu as pltpu
from jax.sharding import PartitionSpec as P

HEADS = 4
STEP = 5
GROUPS = 32
BF = jnp.bfloat16
F32 = jnp.float32
NEG_SCORE = -1e9
NEG_PATH = -1e5
FLOOR = -1e30
LOG2E = 1.4426950408889634
VMEM_LIMIT = 60 * 2**20


def dot(a, b):
    return lax.dot_general(a, b, (((1,), (0,)), ((), ())), preferred_element_type=F32)


def dot_rt(a, b):
    return lax.dot_general(a, b, (((1,), (1,)), ((), ())), preferred_element_type=F32)


def dot_lt(a, b):
    return lax.dot_general(a, b, (((0,), (0,)), ((), ())), preferred_element_type=F32)


def halves(value):
    high = value.astype(BF)
    return high, (value - high.astype(F32)).astype(BF)


def iota(shape, dim):
    return lax.broadcasted_iota(jnp.int32, shape, dim)


def normalised(x):
    mean = jnp.mean(x, axis=-1, keepdims=True)
    centre = x - mean
    rstd = lax.rsqrt(jnp.mean(centre * centre, axis=-1, keepdims=True) + 1e-05)
    return centre * rstd, rstd


def norm_back(dy, unit, rstd, gain):
    dunit = dy * gain
    dx = rstd * (
        dunit
        - jnp.mean(dunit, axis=-1, keepdims=True)
        - unit * jnp.mean(dunit * unit, axis=-1, keepdims=True)
    )
    return dx, jnp.sum(dy * unit, axis=0, keepdims=True), jnp.sum(dy, axis=0, keepdims=True)


def softmax(scores):
    shifted = scores - jnp.max(scores, axis=-1, keepdims=True)
    e = jnp.exp(shifted)
    return e * (1.0 / jnp.sum(e, axis=-1, keepdims=True))


def head_mask(width, h):
    size = width // HEADS
    lane = iota((1, width), 1)
    return (lane >= h * size) & (lane < (h + 1) * size)


def pick_head(value, h):
    return jnp.where(head_mask(value.shape[-1], h), value, jnp.zeros((), value.dtype))


def attend(q, k, v, allowed):
    scale = 1.0 / math.sqrt(q.shape[-1] // HEADS)
    total = None
    for h in range(HEADS):
        s = jnp.where(allowed, dot_rt(q, pick_head(k, h)) * scale, NEG_SCORE)
        c = dot(softmax(s).astype(BF), pick_head(v, h))
        total = c if total is None else total + c
    return total


def attend_back(q, k, v, allowed, dctx):
    scale = 1.0 / math.sqrt(q.shape[-1] // HEADS)
    dq = dk = dv = None
    for h in range(HEADS):
        kh, vh = pick_head(k, h), pick_head(v, h)
        p = softmax(jnp.where(allowed, dot_rt(q, kh) * scale, NEG_SCORE))
        dvh = dot_lt(p.astype(BF), pick_head(dctx, h))
        dp = dot_rt(dctx, vh)
        ds = p * (dp - jnp.sum(p * dp, axis=-1, keepdims=True))
        ds = jnp.where(allowed, ds, 0.0).astype(BF)
        dqh = dot(ds, kh)
        dkh = dot_lt(ds, pick_head(q, h))
        if dq is None:
            dq, dk, dv = dqh, dkh, dvh
        else:
            dq, dk, dv = dq + dqh, dk + dkh, dv + dvh
    return dq * scale, dk * scale, dv


def spans(total, size):
    return [(at, min(size, total - at)) for at in range(0, total, size)]


def put8(ref, base, value, first=0):
    rows, width = value.shape
    deep = rows // GROUPS
    if width % 128:
        value = jnp.pad(value, ((0, 0), (0, 128 - width % 128)))
    for c in range(first, value.shape[1] // 128):
        at = base + deep * c
        ref[:, at:at + deep, :] = value[:, 128 * c:128 * (c + 1)].reshape(GROUPS, deep, 128)


def put_rows(ref, base, value, row, rows):
    deep = rows // GROUPS
    count = value.shape[0] // deep
    for c in range(value.shape[1] // 128):
        at = base + deep * c
        ref[row // deep:row // deep + count, at:at + deep, :] = value[:, 128 * c:128 * (c + 1)].reshape(count, deep, 128)


def put_small(ref, row, value):
    width = value.shape[1]
    part = 7 * width // GROUPS
    line = jnp.concatenate([value[i:i + 1, :] for i in range(8)], axis=1)
    for q in range(GROUPS):
        ref[q, row:row + 1, :] = line[:, part * q:part * q + 128]


class Plan:
    def __init__(self, utts, frames, n_bucket, tokens, width, ff, vocab, feat):
        self.utts, self.frames, self.tokens = utts, frames, tokens
        self.width, self.ff, self.vocab = width, ff, vocab
        if utts % n_bucket == 0:
            self.caps = [frames * (i % n_bucket + 1) // n_bucket for i in range(utts)]
        else:
            self.caps = [frames] * utts
        self.starts = [sum(self.caps[:i]) for i in range(utts)]
        self.rows = sum(self.caps)
        self.drows = utts * tokens
        self.embed_rows = -(-(vocab // GROUPS + 2) // 16) * 16
        tiles = -(-vocab // 128)
        deep = width // GROUPS
        self.out_rows = tiles * deep
        attn, ff = 4 * width // 128 * deep, ff // 128 * deep
        embed = self.embed_rows * width // 128
        ends = np.cumsum([0, self.out_rows, embed, ff, ff, attn, attn])
        self.dec_at, self.dec_rows = [int(x) for x in ends[:-1]], int(ends[-1])
        self.ctc_rows = (tiles + 2) * deep
        self.sub_rows = -(-(feat // GROUPS) // 8) * 8
        ends = np.cumsum([16, self.sub_rows * width // 128, ff, ff, attn])
        self.enc_at, self.enc_rows = [int(x) for x in ends[:-1]], int(ends[-1])


def enc_fwd_kernel(plan, len_ref, fb_ref, pe_ref, w_sub, w_attn, w_ff1, w_ff2, gain, bias,
                   h0_ref, qkv_ref, ctx_ref, h1_ref, h2_ref, enc_ref):
    d = plan.width
    for u in range(plan.utts):
        t, at = plan.caps[u], plan.starts[u]
        h0_ref[at:at + t, :] = dot_lt(fb_ref[u, :, 0:t], w_sub[...]) + pe_ref[0:t, :]
    unit, _ = normalised(h0_ref[...])
    a0 = (unit * gain[0:1, :] + bias[0:1, :]).astype(BF)
    qkv_ref[...] = dot(a0, w_attn[:, : 3 * d]).astype(BF)
    for u in range(plan.utts):
        t, at = plan.caps[u], plan.starts[u]
        allowed = iota((1, t), 1) < len_ref[u]
        piece = qkv_ref[at:at + t, :]
        ctx = attend(piece[:, :d], piece[:, d:2 * d], piece[:, 2 * d:], allowed)
        ctx_ref[at:at + t, :] = ctx.astype(BF)
    h1 = h0_ref[...] + dot(ctx_ref[...], w_attn[:, 3 * d:])
    h1_ref[...] = h1
    unit, _ = normalised(h1)
    a1 = (unit * gain[1:2, :] + bias[1:2, :]).astype(BF)
    h2_ref[...] = h1
    for c, size in spans(plan.ff, 512):
        inner = dot(a1, w_ff1[:, c:c + size])
        act = (inner * jax.nn.sigmoid(inner)).astype(BF)
        h2_ref[...] += dot(act, w_ff2[c:c + size, :])
    unit, _ = normalised(h2_ref[...])
    enc_ref[...] = (unit * gain[2:3, :] + bias[2:3, :]).astype(BF)


def enc_bwd_kernel(plan, len_ref, fb_ref, perm_ref, w_attn, w_ff1, w_ff2, gain, bias,
                   h0_ref, qkv_ref, ctx_ref, h1_ref, h2_ref, denc_ref,
                   gg_dec, gb_dec, g_ref, dh_ref, db_ref, dqkv_ref):
    d, deep = plan.width, plan.width // GROUPS
    at_sub, at_ff2, at_ff1, at_attn = plan.enc_at
    g_ref[:, 0:16, :] = jnp.zeros((GROUPS, 16, 128), F32)
    denc = denc_ref[...].astype(BF).astype(F32)
    unit, rstd = normalised(h2_ref[...])
    dh2, gg2, gb2 = norm_back(denc, unit, rstd, gain[2:3, :])
    dh_ref[...] = dh2
    dout = dh2.astype(BF)
    unit1, rstd1 = normalised(h1_ref[...])
    a1 = (unit1 * gain[1:2, :] + bias[1:2, :]).astype(BF)
    for c, size in spans(plan.ff, 512):
        inner = dot(a1, w_ff1[:, c:c + size])
        sig = jax.nn.sigmoid(inner)
        act = inner * sig
        put_rows(g_ref, at_ff2, dot_lt(act.astype(BF), dout), c, plan.ff)
        dact = dot_rt(dout, w_ff2[c:c + size, :])
        dinner = (dact * (sig + act * (1.0 - sig))).astype(BF)
        put8(g_ref, at_ff1 + c // 128 * deep, dot_lt(a1, dinner))
        part = dot_rt(dinner, w_ff1[:, c:c + size])
        if c == 0:
            db_ref[...] = part
        else:
            db_ref[...] += part
    dx, gg1, gb1 = norm_back(db_ref[...], unit1, rstd1, gain[1:2, :])
    dh1 = dh_ref[...] + dx
    dh_ref[...] = dh1
    dout = dh1.astype(BF)
    put8(g_ref, at_attn + 3 * d // 128 * deep, dot_lt(ctx_ref[...], dout))
    dctx = dot_rt(dout, w_attn[:, 3 * d:]).astype(BF)
    for u in range(plan.utts):
        t, at = plan.caps[u], plan.starts[u]
        allowed = iota((1, t), 1) < len_ref[u]
        piece = qkv_ref[at:at + t, :]
        dq, dk, dv = attend_back(piece[:, :d], piece[:, d:2 * d], piece[:, 2 * d:], allowed, dctx[at:at + t, :])
        dqkv_ref[at:at + t, :d] = dq.astype(BF)
        dqkv_ref[at:at + t, d:2 * d] = dk.astype(BF)
        dqkv_ref[at:at + t, 2 * d:] = dv.astype(BF)
    unit, rstd = normalised(h0_ref[...])
    a0 = (unit * gain[0:1, :] + bias[0:1, :]).astype(BF)
    dqkv = dqkv_ref[...]
    put8(g_ref, at_attn, dot_lt(a0, dqkv))
    da0 = dot_rt(dqkv, w_attn[:, :3 * d])
    dx, gg0, gb0 = norm_back(da0, unit, rstd, gain[0:1, :])
    dh0 = (dh_ref[...] + dx).astype(BF)
    g = None
    for u in range(plan.utts):
        t, at = plan.caps[u], plan.starts[u]
        part = dot(fb_ref[u, :, 0:t], dh0[at:at + t, :])
        g = part if g is None else g + part
    high, low = halves(g)
    lower = (g - high.astype(F32) - low.astype(F32)).astype(BF)
    perm = perm_ref[...]
    put_rows(g_ref, at_sub, dot(perm, high) + dot(perm, low) + dot(perm, lower), 0, perm.shape[0])
    put_small(g_ref, 0, gg_dec[...] + jnp.concatenate([gg0, gg1, gg2, jnp.zeros((5, d), F32)], axis=0))
    put_small(g_ref, 1, gb_dec[...] + jnp.concatenate([gb0, gb1, gb2, jnp.zeros((5, d), F32)], axis=0))


def dec_kernel(plan, utterances, len_ref, tok_col, want_col, live_col, tok_row, pe_ref, enc_ref, w_self, w_cross, w_ff1,
               w_ff2, embed, w_out, gain, bias,
               loss_ref, g_ref, g_gain, g_bias, denc_ref, kv_ref):
    d, rows, vocab = plan.width, plan.drows, plan.vocab
    deep = d // GROUPS
    at_out, at_embed, at_ff1, at_ff2, at_cross, at_self = plan.dec_at
    chunks = spans(vocab, 1024)
    place = iota((1, 1024), 1)
    tok = tok_col[...]
    y = None
    for c, size in chunks:
        hot = jnp.where(tok == place[:, :size] + c, 1.0, 0.0).astype(BF)
        part = dot(hot, embed[c:c + size, :])
        y = part if y is None else y + part
    y0 = y * math.sqrt(d) + pe_ref[...]
    unit3, rstd3 = normalised(y0)
    a3 = (unit3 * gain[3:4, :] + bias[3:4, :]).astype(BF)
    mixed = dot(a3, w_self[:, : 3 * d]).astype(BF)
    q, k, v = mixed[:, :d], mixed[:, d:2 * d], mixed[:, 2 * d:]
    row, col = iota((rows, rows), 0), iota((rows, rows), 1)
    causal = (row // plan.tokens == col // plan.tokens) & (col <= row)
    ctx = attend(q, k, v, causal).astype(BF)
    y1 = y0 + dot(ctx, w_self[:, 3 * d:])
    unit4, rstd4 = normalised(y1)
    a4 = (unit4 * gain[4:5, :] + bias[4:5, :]).astype(BF)
    cq = dot(a4, w_cross[:, :d]).astype(BF)
    kv_ref[...] = dot(enc_ref[...], w_cross[:, d:3 * d]).astype(BF)
    owner = iota((rows, 1), 0) // plan.tokens
    frame = iota((1, plan.rows), 1)
    valid = None
    for u in range(plan.utts):
        here = (owner == u) & (frame >= plan.starts[u]) & (frame < plan.starts[u] + len_ref[u])
        valid = here if valid is None else valid | here
    ck, cv = kv_ref[:, :d], kv_ref[:, d:]
    cctx = attend(cq, ck, cv, valid).astype(BF)
    y2 = y1 + dot(cctx, w_cross[:, 3 * d:])
    unit5, rstd5 = normalised(y2)
    a5 = (unit5 * gain[5:6, :] + bias[5:6, :]).astype(BF)
    y3 = y2
    for c, size in spans(plan.ff, 1024):
        inner = dot(a5, w_ff1[:, c:c + size])
        act = (inner * jax.nn.sigmoid(inner)).astype(BF)
        y3 = y3 + dot(act, w_ff2[c:c + size, :])
    unit6, rstd6 = normalised(y3)
    a6 = (unit6 * gain[6:7, :] + bias[6:7, :]).astype(BF)
    want = want_col[...]
    live = live_col[...]
    peak = jnp.full((rows, 1), FLOOR, F32)
    mass = jnp.zeros((rows, 1), F32)
    picked = jnp.zeros((rows, 1), F32)
    summed = jnp.zeros((rows, 1), F32)
    for c, size in chunks:
        z = dot_rt(a6, w_out[c:c + size, :])
        top = jnp.maximum(peak, jnp.max(z, axis=-1, keepdims=True))
        mass = mass * jnp.exp(peak - top) + jnp.sum(jnp.exp(z - top), axis=-1, keepdims=True)
        peak = top
        picked = picked + jnp.sum(jnp.where(want == place[:, :size] + c, z, 0.0), axis=-1, keepdims=True)
        summed = summed + jnp.sum(z, axis=-1, keepdims=True)
    lse = peak + jnp.log(mass)
    rest = 0.1 / (vocab - 1)
    others = (summed - vocab * lse) - (picked - lse)
    per_token = -(0.9 * (picked - lse) + rest * others)
    loss_ref[...] = jnp.full((8, 128), 0.7 * jnp.sum(live * per_token), F32)
    weight = live * (0.7 / utterances)
    da6 = None
    for c, size in chunks:
        z = dot_rt(a6, w_out[c:c + size, :])
        share = jnp.exp(z - lse) * (0.9 + rest * (vocab - 1))
        dz = share - jnp.where(want == place[:, :size] + c, 0.9, rest)
        dz = (dz * weight).astype(BF)
        put8(g_ref, at_out + c // 128 * deep, dot_lt(a6, dz))
        part = dot(dz, w_out[c:c + size, :])
        da6 = part if da6 is None else da6 + part
    dy, gg6, gb6 = norm_back(da6, unit6, rstd6, gain[6:7, :])
    dout = dy.astype(BF)
    da5 = None
    for c, size in spans(plan.ff, 1024):
        inner = dot(a5, w_ff1[:, c:c + size])
        sig = jax.nn.sigmoid(inner)
        act = inner * sig
        put_rows(g_ref, at_ff2, dot_lt(act.astype(BF), dout), c, plan.ff)
        dact = dot_rt(dout, w_ff2[c:c + size, :])
        dinner = (dact * (sig + act * (1.0 - sig))).astype(BF)
        put8(g_ref, at_ff1 + c // 128 * deep, dot_lt(a5, dinner))
        part = dot_rt(dinner, w_ff1[:, c:c + size])
        da5 = part if da5 is None else da5 + part
    dx, gg5, gb5 = norm_back(da5, unit5, rstd5, gain[5:6, :])
    dy = dy + dx
    dout = dy.astype(BF)
    tile = d // 128 * deep
    put8(g_ref, at_cross + 3 * tile, dot_lt(cctx, dout))
    dctx = dot_rt(dout, w_cross[:, 3 * d:]).astype(BF)
    dq, dk, dv = attend_back(cq, ck, cv, valid, dctx)
    dq, dk, dv = dq.astype(BF), dk.astype(BF), dv.astype(BF)
    enc = enc_ref[...]
    put8(g_ref, at_cross + tile, dot_lt(enc, dk))
    put8(g_ref, at_cross + 2 * tile, dot_lt(enc, dv))
    denc_ref[...] = dot_rt(dk, w_cross[:, d:2 * d]) + dot_rt(dv, w_cross[:, 2 * d:3 * d])
    put8(g_ref, at_cross, dot_lt(a4, dq))
    da4 = dot_rt(dq, w_cross[:, :d])
    dx, gg4, gb4 = norm_back(da4, unit4, rstd4, gain[4:5, :])
    dy = dy + dx
    dout = dy.astype(BF)
    put8(g_ref, at_self + 3 * tile, dot_lt(ctx, dout))
    dctx = dot_rt(dout, w_self[:, 3 * d:]).astype(BF)
    dq, dk, dv = attend_back(q, k, v, causal, dctx)
    dq, dk, dv = dq.astype(BF), dk.astype(BF), dv.astype(BF)
    put8(g_ref, at_self, dot_lt(a3, dq))
    put8(g_ref, at_self + tile, dot_lt(a3, dk))
    put8(g_ref, at_self + 2 * tile, dot_lt(a3, dv))
    da3 = dot_rt(dq, w_self[:, :d]) + dot_rt(dk, w_self[:, d:2 * d]) + dot_rt(dv, w_self[:, 2 * d:3 * d])
    dx, gg3, gb3 = norm_back(da3, unit3, rstd3, gain[3:4, :])
    high, low = halves((dy + dx) * math.sqrt(d))
    share_rows, tall = vocab // GROUPS, plan.embed_rows
    toks = tok_row[0:1, :]

    def block(i, carry):
        first = share_rows * i + (vocab - share_rows * GROUPS) * i // GROUPS
        hot = jnp.where(iota((tall, rows), 0) + first == toks, 1.0, 0.0).astype(BF)
        value = dot(hot, high) + dot(hot, low)
        for c in range(d // 128):
            g_ref[i, at_embed + tall * c:at_embed + tall * (c + 1), :] = value[:, 128 * c:128 * (c + 1)]
        return carry

    lax.fori_loop(0, GROUPS, block, 0)
    g_gain[...] = jnp.concatenate([jnp.zeros((3, d), F32), gg3, gg4, gg5, gg6, jnp.zeros((1, d), F32)], axis=0)
    g_bias[...] = jnp.concatenate([jnp.zeros((3, d), F32), gb3, gb4, gb5, gb6, jnp.zeros((1, d), F32)], axis=0)


def ctc_kernel(plan, utterances, len_ref, lab_col, skip_ref, last_ref, lens_ref, enc_ref, w_ref, denc_in,
               loss_ref, g_ref, denc_ref,
               peak_ref, mass_ref, sel_ref, em_ref, cum_ref, alpha_ref, beta_ref, gam_hi, gam_lo):
    d, vocab, frames, toks = plan.width, plan.vocab, plan.frames, plan.tokens
    lanes, deep = plan.drows, d // GROUPS
    g_ref[:, deep:2 * deep, :] = jnp.zeros((GROUPS, deep, 128), F32)
    g_ref[:, plan.ctc_rows - deep:, :] = jnp.zeros((GROUPS, deep, 128), F32)
    chunks = spans(vocab, 1024)
    place = iota((1, 1024), 1)
    labels = lab_col[...]
    enc = enc_ref[...]
    peak = jnp.full((plan.rows, 1), FLOOR, F32)
    mass = jnp.zeros((plan.rows, 1), F32)
    sel_ref[...] = jnp.zeros((lanes, d), F32)
    blank = None
    for c, size in chunks:
        wc = w_ref[c:c + size, :]
        z = dot_rt(enc, wc)
        if c == 0:
            blank = z[:, 0:1]
        top = jnp.maximum(peak, jnp.max(z, axis=-1, keepdims=True))
        mass = mass * jnp.exp(peak - top) + jnp.sum(jnp.exp(z - top), axis=-1, keepdims=True)
        peak = top
        hot = jnp.where(labels == place[:, :size] + c, 1.0, 0.0).astype(BF)
        sel_ref[...] += dot(hot, wc)
    lse = peak + jnp.log(mass)
    peak_ref[:, 0:1] = lse
    lane = iota((1, lanes), 1)
    sel = sel_ref[...].astype(BF)
    em_ref[...] = jnp.zeros((frames, lanes), F32)
    mass_ref[...] = jnp.zeros((frames, lanes), F32)
    for u in range(plan.utts):
        t, at = plan.caps[u], plan.starts[u]
        mine = lane // toks == u
        z = dot_rt(enc[at:at + t, :], sel)
        em_ref[0:t, :] += jnp.where(mine, (z - blank[at:at + t, :]) * LOG2E, 0.0)
        mass_ref[0:t, :] += jnp.where(mine, (blank[at:at + t, :] - lse[at:at + t, :]) * LOG2E, 0.0)
    lower = jnp.where(iota((frames, frames), 0) >= iota((frames, frames), 1), 1.0, 0.0).astype(BF)
    drift = mass_ref[...]
    high, mid = halves(drift)
    low = (drift - high.astype(F32) - mid.astype(F32)).astype(BF)
    total = dot(lower, high) + dot(lower, mid) + dot(lower, low)
    neg = NEG_PATH * LOG2E
    cum_ref[...] = neg - total
    first = lane % toks == 0
    final = lane % toks == toks - 1
    skip = skip_ref[0:1, :] > 0
    skip_next = skip_ref[1:2, :] > 0
    ending = last_ref[0:1, :] > 0
    begin_beta = jnp.where(ending, 0.0, FLOOR)
    end_frame = lens_ref[0:1, :] - 1

    def log_sum(a, b, c):
        top = jnp.maximum(jnp.maximum(a, b), c)
        return top, jnp.log2(jnp.exp2(a - top) + jnp.exp2(b - top) + jnp.exp2(c - top))

    def log_pair(a, b):
        top = jnp.maximum(a, b)
        return top + jnp.log2(jnp.exp2(a - top) + jnp.exp2(b - top))

    def step(i, carry):
        la, ba, lb, bb = carry
        fill = cum_ref[pl.ds(jnp.maximum(i - 1, 0), 1), :]
        shifted = jnp.where(first, fill, pltpu.roll(la, 1, 1))
        e = em_ref[pl.ds(i, 1), :]
        top, rest = log_sum(la, ba, jnp.where(skip, shifted, fill))
        la2 = (top + e) + rest
        top, rest = log_sum(ba, shifted, fill)
        ba2 = top + rest
        start = i == 0
        la2 = jnp.where(start, jnp.where(first, e, fill0), la2)
        ba2 = jnp.where(start, jnp.where(first, 0.0, fill0), ba2)
        alpha_ref[pl.ds(i, 1), :] = la2
        t = frames - 1 - i
        e = em_ref[pl.ds(t, 1), :]
        shifted = jnp.where(final, FLOOR, pltpu.roll(lb, lanes - 1, 1))
        top, rest = log_sum(lb, bb, jnp.where(skip_next, shifted, FLOOR))
        lb2 = (top + e) + rest
        bb2 = log_pair(bb, shifted)
        begin = end_frame == t
        lb2 = jnp.where(begin, begin_beta + e, lb2)
        bb2 = jnp.where(begin, begin_beta, bb2)
        beta_ref[pl.ds(t, 1), :] = lb2
        keep = end_frame >= i
        return (jnp.where(keep, la2, la), jnp.where(keep, ba2, ba), lb2, bb2)

    fill0 = cum_ref[0:1, :]
    flat = jnp.full((1, lanes), FLOOR, F32)
    la, ba, _, _ = lax.fori_loop(0, frames, step, (flat, flat, flat, flat), unroll=2)
    after = jnp.where(first, FLOOR, pltpu.roll(jnp.where(ending, 0.0, FLOOR), 1, 1))
    moment = iota((frames, lanes), 0)
    at_end = jnp.sum(jnp.where(moment == end_frame, neg - cum_ref[...], 0.0), axis=0, keepdims=True)
    floor = NEG_PATH * 10.0 * LOG2E - at_end
    tail = jnp.maximum(jnp.where(ending, la, FLOOR), jnp.where(after == 0.0, ba, FLOOR))
    logz = jnp.zeros((1, lanes), F32)
    ctc = jnp.zeros((), F32)
    for u in range(plan.utts):
        mine = lane // toks == u
        top = jnp.max(jnp.where(mine, tail, FLOOR), axis=-1, keepdims=True)
        bottom = jnp.max(jnp.where(mine, floor, FLOOR), axis=-1, keepdims=True)
        top = jnp.maximum(top, bottom)
        weight = jnp.where(mine & ending, jnp.exp2(la - top), 0.0) + jnp.where(mine & (after == 0.0), jnp.exp2(ba - top), 0.0)
        full = top + jnp.log2(jnp.sum(weight, axis=-1, keepdims=True) + jnp.exp2(bottom - top))
        logz = jnp.where(mine, full, logz)
        drift_end = jnp.max(jnp.where(mine, at_end, FLOOR), axis=-1, keepdims=True)
        ctc = ctc - jnp.sum(full + drift_end) / LOG2E
    loss_ref[...] = jnp.full((8, 128), 0.3 * ctc, F32)
    gamma = jnp.exp2(alpha_ref[...] + beta_ref[...] - em_ref[...] - logz)
    gamma = jnp.where(moment <= end_frame, gamma, 0.0)
    for u in range(plan.utts):
        t, at = plan.caps[u], plan.starts[u]
        mine = lane // toks == u
        piece = jnp.where(mine, gamma[0:t, :], 0.0)
        high, low = halves(piece)
        gam_hi[at:at + t, :] = high
        gam_lo[at:at + t, :] = low
        alive = jnp.where(iota((t, 1), 0) < len_ref[u], 1.0, 0.0)
        peak_ref[at:at + t, 1:2] = alive
        peak_ref[at:at + t, 2:3] = alive - jnp.sum(piece, axis=-1, keepdims=True)
    lse = peak_ref[:, 0:1]
    scale = 0.3 / utterances
    live = peak_ref[:, 1:2] * scale
    blank_share = peak_ref[:, 2:3]
    denc_ref[...] = denc_in[...]
    for c, size in chunks:
        wc = w_ref[c:c + size, :]
        p = jnp.exp(dot_rt(enc, wc) - lse) * live
        hot = jnp.where(labels == place[:, :size] + c, 1.0, 0.0).astype(BF)
        post = dot(gam_hi[...], hot) + dot(gam_lo[...], hot)
        dz = p - post * scale
        if c == 0:
            dz = dz - jnp.where(place[:, :size] == 0, blank_share * scale, 0.0)
        dz = dz.astype(BF)
        value = dot_lt(enc, dz)
        if c == 0:
            g_ref[:, 0:deep, :] = value[:, :128].reshape(GROUPS, deep, 128)
        put8(g_ref, deep + c // 128 * deep, value, 1 if c == 0 else 0)
        denc_ref[...] += dot(dz, wc)


VM = pl.BlockSpec(memory_space=pltpu.VMEM)
SM = pl.BlockSpec(memory_space=pltpu.SMEM)


def shape(*dims, dtype=F32):
    return jax.ShapeDtypeStruct(dims, dtype)


def call(kernel, name, outs, scratch, *args, scalars=1):
    return pl.pallas_call(
        kernel,
        out_shape=outs,
        in_specs=[SM] * scalars + [VM] * (len(args) - scalars),
        out_specs=[VM] * len(outs),
        scratch_shapes=scratch,
        name=name,
        compiler_params=pltpu.CompilerParams(vmem_limit_bytes=VMEM_LIMIT),
    )(*args)


def positions(length, width):
    place = np.arange(length, dtype=np.float64)[:, None]
    angles = place * np.exp(np.arange(0, width, 2, dtype=np.float64) * (-math.log(10000.0) / width))[None, :]
    return np.stack([np.sin(angles), np.cos(angles)], axis=-1).reshape(length, width).astype(np.float32)


def gradients(n_bucket, utterances, filter_bank, frame_len, tok_len, targets, weights):
    (w_sub, enc_attn, enc_ff1, enc_ff2, dec_self, dec_cross, dec_ff1, dec_ff2, embed, ctc_head, out_head,
     norm_gain, norm_bias) = weights
    utts, frames, feat = filter_bank.shape
    toks, (vocab, d), ff = targets.shape[1], embed.shape, enc_ff1.shape[1]
    plan = Plan(utts, frames, n_bucket, toks, d, ff, vocab, feat)
    rows, drows = plan.rows, plan.drows
    gain = jnp.pad(norm_gain.astype(F32), ((0, 1), (0, 0)))
    bias = jnp.pad(norm_bias.astype(F32), ((0, 1), (0, 0)))
    bank = jnp.swapaxes(filter_bank, 1, 2)
    pe = positions(frames, d)
    pe_tok = np.tile(pe[:toks], (utts, 1))
    h0, qkv, ctx, h1, h2, enc = call(
        functools.partial(enc_fwd_kernel, plan), "enc_fwd",
        [shape(rows, d), shape(rows, 3 * d, dtype=BF), shape(rows, d, dtype=BF), shape(rows, d), shape(rows, d), shape(rows, d, dtype=BF)],
        [], frame_len, bank, jnp.asarray(pe), w_sub, enc_attn, enc_ff1, enc_ff2, gain, bias)
    place = jnp.arange(toks)[None, :]
    inputs = jnp.concatenate([jnp.full((utts, 1), vocab - 1, jnp.int32), targets[:, :-1]], axis=1)
    want = jnp.where(place == tok_len[:, None], vocab - 1, targets)
    live = (place <= tok_len[:, None]).astype(F32)
    att, g_dec, gg_dec, gb_dec, denc = call(
        functools.partial(dec_kernel, plan, utterances), "decoder",
        [shape(8, 128), shape(GROUPS, plan.dec_rows, 128), shape(8, d), shape(8, d), shape(rows, d)],
        [pltpu.VMEM((rows, 2 * d), BF)],
        frame_len, inputs.reshape(drows, 1), want.reshape(drows, 1), live.reshape(drows, 1),
        jnp.broadcast_to(inputs.reshape(1, drows), (8, drows)), jnp.asarray(pe_tok), enc, dec_self, dec_cross, dec_ff1, dec_ff2,
        embed, out_head.T, gain, bias)
    same = jnp.concatenate([jnp.zeros((utts, 1), bool), targets[:, 1:] != targets[:, :-1]], axis=1).astype(jnp.int32)
    same_next = jnp.concatenate([same[:, 1:], jnp.zeros((utts, 1), jnp.int32)], axis=1)
    last = (place == tok_len[:, None] - 1).astype(jnp.int32)
    lens = jnp.broadcast_to(frame_len[:, None], (utts, toks))
    ctc, g_ctc, denc = call(
        functools.partial(ctc_kernel, plan, utterances), "ctc",
        [shape(8, 128), shape(GROUPS, plan.ctc_rows, 128), shape(rows, d)],
        [pltpu.VMEM((rows, 128), F32), pltpu.VMEM((frames, drows), F32), pltpu.VMEM((drows, d), F32)]
        + [pltpu.VMEM((frames, drows), F32)] * 4 + [pltpu.VMEM((rows, drows), BF)] * 2,
        frame_len, targets.reshape(drows, 1), jnp.stack([same.reshape(-1), same_next.reshape(-1)]), last.reshape(1, drows),
        lens.reshape(1, drows), enc, ctc_head.T, denc)
    per = feat // GROUPS
    perm = np.zeros((GROUPS * plan.sub_rows, feat), np.float32)
    for r in range(feat):
        perm[r // per * plan.sub_rows + r % per, r] = 1.0
    (g_enc,) = call(
        functools.partial(enc_bwd_kernel, plan), "enc_bwd",
        [shape(GROUPS, plan.enc_rows, 128)],
        [pltpu.VMEM((rows, d), F32), pltpu.VMEM((rows, d), F32), pltpu.VMEM((rows, 3 * d), BF)],
        frame_len, bank, jnp.asarray(perm, BF), enc_attn, enc_ff1, enc_ff2, gain, bias, h0, qkv, ctx, h1, h2, denc, gg_dec, gb_dec)
    return plan, att, ctc, g_dec, g_ctc, g_enc


MESH = pl.DeviceIdType.MESH


class Geometry:
    def __init__(self, n_bucket, n_dp):
        self.ny, self.ns = n_bucket // 2, 4
        self.nf = n_dp // self.ns
        self.share = n_bucket * n_dp // GROUPS
        self.gf = self.nf // self.share
        if self.ny * 2 * self.ns * self.gf != GROUPS:
            raise ValueError("mesh size")

    def size(self, axis):
        return {"c": 2, "y": self.ny, "s": self.ns, "f": self.nf}[axis]


class Here:
    def __init__(self, geo):
        self.geo = geo
        bucket, dp = lax.axis_index("bucket"), lax.axis_index("dp")
        self.at = {"y": bucket // 2, "c": bucket % 2, "s": dp // geo.nf, "f": dp % geo.nf}

    def step(self, axis, p):
        return lax.rem(self.at[axis] + 1 + p, self.geo.size(axis))

    def device(self, axis, p):
        at = dict(self.at)
        at[axis] = self.step(axis, p)
        return (at["y"] * 2 + at["c"], at["s"] * self.geo.nf + at["f"])

    def greet(self):
        barrier = pltpu.get_barrier_semaphore()
        count = 0
        for axis in "cyfs":
            for p in range(self.geo.size(axis) - 1):
                pl.semaphore_signal(barrier, inc=1, device_id=self.device(axis, p), device_id_type=MESH)
                count += 1
        pl.semaphore_wait(barrier, count)


class Stream:
    def __init__(self, geo, array, a, b, order, dtype):
        self.geo, self.array, self.a, self.n, self.order, self.dtype = geo, array, a, b - a, order, dtype

    def wire(self, stage):
        geo, n = self.geo, self.n
        done = self.order[:stage]
        axis = self.order[stage]
        if axis == "c":
            return (geo.ny, geo.ns * geo.gf, n, 128)
        dims = []
        for other, size in (("y", geo.ny), ("s", geo.ns), ("f", geo.gf)):
            if other not in done and (other != axis):
                dims.append(size)
        return tuple(dims) + (n, 128)

    def scratch(self):
        geo = self.geo
        sums = pltpu.VMEM((geo.ny, geo.ns * geo.gf, self.n, 128), F32)
        out = [sums, pltpu.VMEM(self.wire(0), F32)]
        sems = [pltpu.SemaphoreType.DMA((3, geo.ny))]
        for stage in (1, 2, 3):
            partners = geo.size(self.order[stage]) - 1
            out += [pltpu.VMEM((partners,) + self.wire(stage), self.dtype)] * 2
            sems += [pltpu.SemaphoreType.DMA((2, partners))]
        return out + sems

    SCRATCH = 12

    def bind(self, here, g_refs, refs, r_ref, r_at):
        self.here, self.g, self.r, self.r_at = here, g_refs[self.array], r_ref, r_at
        self.sums, self.core = refs[0], refs[1]
        self.send = {s: refs[2 * s] for s in (1, 2, 3)}
        self.recv = {s: refs[2 * s + 1] for s in (1, 2, 3)}
        self.sems = refs[8:12]

    def core_copies(self):
        geo, at, sems = self.geo, self.here.at, self.sems[0]
        span = pl.ds(self.a, self.n)
        copies = []
        for y in range(geo.ny):
            copies.append(pltpu.make_async_remote_copy(
                src_ref=self.g.at[2 * y + 1 - at["c"], :, span], dst_ref=self.core.at[y],
                send_sem=sems.at[0, y], recv_sem=sems.at[1, y],
                device_id=self.here.device("c", 0), device_id_type=MESH))
        return copies

    def local_copies(self):
        geo, at, sems = self.geo, self.here.at, self.sems[0]
        span = pl.ds(self.a, self.n)
        return [pltpu.make_async_copy(self.g.at[2 * y + at["c"], :, span], self.sums.at[y], sems.at[2, y])
                for y in range(geo.ny)]

    def wire_copies(self, stage):
        axis, partners = self.order[stage], self.geo.size(self.order[stage]) - 1
        return [pltpu.make_async_remote_copy(
            src_ref=self.send[stage].at[p], dst_ref=self.recv[stage].at[partners - 1 - p],
            send_sem=self.sems[stage].at[0, p], recv_sem=self.sems[stage].at[1, partners - 1 - p],
            device_id=self.here.device(axis, p), device_id_type=MESH) for p in range(partners)]

    def blocks(self, stage):
        geo, at = self.geo, self.here.at
        done = self.order[:stage + 1]
        sizes = [1 if axis in done else size for axis, size in (("y", geo.ny), ("s", geo.ns), ("f", geo.gf))]

        def place(i, swap=None):
            f = i % sizes[2]
            s = i // sizes[2] % sizes[1]
            y = i // (sizes[2] * sizes[1])
            where = {"y": at["y"] if "y" in done else y, "s": at["s"] if "s" in done else s,
                     "f": (at["f"] if "f" in done else f) if geo.gf > 1 else 0}
            if swap is not None and not (swap[0] == "f" and geo.gf == 1):
                where[swap[0]] = swap[1]
            wire = []
            for axis, v in (("y", y), ("s", s), ("f", f)):
                if axis not in done:
                    wire.append(v)
            return (where["y"], where["s"] * geo.gf + where["f"]), tuple(wire)

        return math.prod(sizes), place

    def start(self, stage):
        if stage == 0:
            for copy in self.core_copies() + self.local_copies():
                copy.start()
            return
        axis = self.order[stage]
        count, place = self.blocks(stage)
        copies = self.wire_copies(stage)
        for p, copy in enumerate(copies):
            target = self.here.step(axis, p)

            def fill(i, carry, p=p, target=target):
                at, wire = place(i, (axis, target))
                self.send[stage][(p,) + wire] = self.sums[at].astype(self.dtype)
                return carry

            loop(count, fill)
            copy.start()

    def finish(self, stage):
        if stage == 0:
            for copy in self.core_copies() + self.local_copies():
                copy.wait()
            geo = self.geo

            def add(i, carry):
                y, sf = i // (geo.ns * geo.gf), i % (geo.ns * geo.gf)
                self.sums[y, sf] += self.core[y, sf]
                return carry

            loop(geo.ny * geo.ns * geo.gf, add)
            return
        count, place = self.blocks(stage)
        copies = self.wire_copies(stage)
        for copy in copies:
            copy.wait()

        def add(i, carry):
            at, wire = place(i)
            total = self.sums[at]
            for p in range(len(copies)):
                total = total + self.recv[stage][(p,) + wire].astype(F32)
            if stage == 3:
                self.r[self.r_at:self.r_at + self.n, :] = total
            else:
                self.sums[at] = total
            return carry

        loop(count, add)


def loop(count, body):
    if count == 1:
        body(0, 0)
    else:
        lax.fori_loop(0, count, body, 0)


def sum_streams(schedule):
    for slot in range(len(schedule) + 4):
        for i in range(len(schedule)):
            stage = slot - i
            if 1 <= stage <= 4:
                for stream in schedule[i]:
                    stream.finish(stage - 1)
            if 0 <= stage <= 3:
                for stream in schedule[i]:
                    stream.start(stage)


class Layout:
    def __init__(self, plan, geo, sizes):
        self.plan, self.share = plan, geo.share
        self.widths = [size // GROUPS // geo.share for size in sizes]
        self.starts = [int(x) for x in np.cumsum([0] + self.widths)]
        self.part = self.starts[-1]
        self.lines = -(-self.part // 1024) * 8
        self.base_dec, self.base_ctc = 0, plan.dec_rows
        self.base_enc = plan.dec_rows + plan.ctc_rows
        self.rows = self.base_enc + plan.enc_rows
        d, deep = plan.width, plan.width // GROUPS
        e, c = [self.base_enc + x for x in plan.enc_at], plan.dec_at
        long = plan.ff // GROUPS
        attn, ff, two = 4 * d // 128, plan.ff // 128, d // 128
        self.place = [(e[0], plan.sub_rows, two), (e[3], deep, attn), (e[2], deep, ff), (e[1], long, two),
                      (c[5], deep, attn), (c[4], deep, attn), (c[2], deep, ff), (c[3], long, two),
                      (c[1], plan.embed_rows, two), (self.base_ctc, deep, plan.out_rows // deep), (c[0], deep, plan.out_rows // deep)]

    def tile(self, weight, c):
        base, deep, _ = self.place[weight]
        return base + deep * c + (deep if weight == 9 and c > 0 else 0)

    def in_xla(self, r, bucket, dp, n_dp):
        index = bucket * n_dp + dp
        group, within = index // self.share, index % self.share
        pieces = []
        for weight, width in enumerate(self.widths):
            if weight >= 11:
                line, at = r[self.base_enc + weight - 11], 0
            else:
                _, deep, tiles = self.place[weight]
                block = jnp.concatenate([r[self.tile(weight, c):self.tile(weight, c) + deep] for c in range(tiles)], axis=1)
                if weight in (9, 10):
                    block = block[:, : self.plan.vocab]
                line, at = block.reshape(-1), 0
                if weight == 8:
                    at = group * (width * self.share) % self.plan.width
            pieces.append(lax.dynamic_slice(line, (at + within * width,), (width,)))
        flat = jnp.concatenate(pieces)
        return jnp.pad(flat, (0, self.lines * 128 - self.part)).reshape(self.lines, 128)

    def in_kernel(self, r, flat, work, group):
        flat[self.lines - 8:, :] = jnp.zeros((8, 128), F32)
        lane = iota((1, 128), 1)

        def put(value, base, length):
            lines, row, shift = -(-length // 128), base // 128, base % 128
            value = value[:lines]
            if shift == 0 and length % 128 == 0:
                flat[row:row + lines, :] = value
                return
            moved = pltpu.roll(value, shift, 1) if shift else value
            number = 128 * iota((lines, 128), 0) + (lane - shift) % 128
            right = (lane >= shift) & (number < length)
            flat[row:row + lines, :] = jnp.where(right, moved, flat[row:row + lines, :])
            if shift:
                left = (lane < shift) & (number < length)
                flat[row + 1:row + 1 + lines, :] = jnp.where(left, moved, flat[row + 1:row + 1 + lines, :])

        for weight, width in enumerate(self.widths):
            base = self.starts[weight]
            if weight >= 11:
                put(r[self.base_enc + weight - 11:self.base_enc + weight - 10, :], base, width)
                continue
            _, deep, tiles = self.place[weight]
            if weight == 8:
                for c in range(tiles):
                    at = self.tile(weight, c)
                    work[pl.ds(c, deep, stride=tiles), :] = r[at:at + deep, :]
                offset = lax.rem(group * width, self.plan.width)
                need = -(-width // 128)
                value = jnp.where(offset >= 128, work[1:need + 2, :], work[0:need + 1, :])
                turned = pltpu.roll(value, 64, 1)
                after = jnp.where(lane < 64, turned[:need], turned[1:])
                put(jnp.where(lax.rem(offset, 128) >= 64, after, value[:need]), base, width)
            elif weight in (9, 10):
                for c in range(tiles):
                    at = self.tile(weight, c)
                    work[pl.ds(c, deep, stride=tiles), :] = r[at:at + deep, :]
                for i in range(deep):
                    put(work[tiles * i:tiles * (i + 1), :], base + self.plan.vocab * i, self.plan.vocab)
            else:
                count = width // 128 // tiles
                for c in range(tiles):
                    at = self.tile(weight, c)
                    flat[pl.ds(base // 128 + c, count, stride=tiles), :] = r[at:at + count, :]


def sum_kernel(geo, plan, layout, schedule, fused, g_dec, g_ctc, g_enc, out_ref, *scratch):
    here = Here(geo)
    refs = list(scratch)
    r_ref = refs.pop(0) if fused else out_ref
    work = refs.pop(0) if fused else None
    arrays = (g_dec, g_ctc, g_enc)
    bases = (layout.base_dec, layout.base_ctc, layout.base_enc)
    at = 0
    for streams in schedule:
        for stream in streams:
            stream.bind(here, arrays, refs[at:at + stream.SCRATCH], r_ref, bases[stream.array] + stream.a)
            at += stream.SCRATCH
    here.greet()
    sum_streams(schedule)
    if fused:
        group = ((here.at["y"] * 2 + here.at["c"]) * geo.ns + here.at["s"]) * geo.gf + here.at["f"]
        layout.in_kernel(r_ref, out_ref, work, group)


def make_schedule(geo, plan, size=256):
    orders = ("cfys", "cyfs") if geo.share == 1 else ("cysf", "csyf")
    lists = [[Stream(geo, 1, 0, 16, orders[0], F32), Stream(geo, 2, 0, 16, orders[0], F32)]]
    for array, first, rows in ((0, 0, plan.dec_rows), (1, 16, plan.ctc_rows), (2, 16, plan.enc_rows)):
        for a, n in spans(rows - first, size):
            half = -(-n // 32) * 16
            a += first
            lists.append([Stream(geo, array, a, a + half, orders[0], BF), Stream(geo, array, a + half, a + n, orders[1], BF)])
    lists[1] = lists[0] + lists[1]
    return lists[1:]


def sum_over_devices(geo, plan, layout, g_dec, g_ctc, g_enc):
    schedule = make_schedule(geo, plan)
    fused = geo.share == 1
    scratch = [pltpu.VMEM((layout.rows, 128), F32), pltpu.VMEM((plan.embed_rows * plan.width // 128, 128), F32)] if fused else []
    for streams in schedule:
        for stream in streams:
            scratch += stream.scratch()
    arrays = [g.reshape(2 * geo.ny, geo.ns * geo.gf, g.shape[1], 128) for g in (g_dec, g_ctc, g_enc)]
    rows = layout.lines if fused else layout.rows
    out = pl.pallas_call(
        functools.partial(sum_kernel, geo, plan, layout, schedule, fused),
        out_shape=shape(rows, 128),
        in_specs=[pl.BlockSpec(memory_space=pl.ANY)] * 3,
        out_specs=VM,
        scratch_shapes=scratch,
        name="sum_over_devices",
        compiler_params=pltpu.CompilerParams(vmem_limit_bytes=VMEM_LIMIT, collective_id=0, has_side_effects=True),
    )(*arrays)
    if fused:
        return out
    return layout.in_xla(out, lax.axis_index("bucket"), lax.axis_index("dp"), geo.ns * geo.nf)


def share_sum(here, block_ref, recv, sems, start):
    geo = here.geo
    at = start
    for axis in "cyfs":
        size, me = geo.size(axis), here.at[axis]
        copies = []
        recv[at + me] = block_ref[...]
        for p in range(size - 1):
            copies.append(pltpu.make_async_remote_copy(
                src_ref=block_ref, dst_ref=recv.at[at + me], send_sem=sems.at[0, at + p], recv_sem=sems.at[1, at + me],
                device_id=here.device(axis, p), device_id_type=MESH))
        for copy in copies:
            copy.start()
        for p, copy in enumerate(copies):
            copy.wait_send()
            other = here.step(axis, p)
            pltpu.make_async_remote_copy(
                src_ref=block_ref, dst_ref=recv.at[at + other], send_sem=sems.at[0, at + p], recv_sem=sems.at[1, at + other],
                device_id=here.device(axis, p), device_id_type=MESH).wait_recv()
        total = recv[at]
        for i in range(1, size):
            total = total + recv[at + i]
        block_ref[...] = total
        at += size
    return at


def lamb_kernel(geo, layout, utterances, g_ref, master, moment1, moment2, att, ctc,
                loss_ref, clip_ref, first_ref, second_ref, fresh_ref, low_ref, wn_ref, un_ref,
                w2, a2, b2, sq, line, recv, sems):
    here = Here(geo)
    here.greet()
    full = layout.part // 128
    edge = layout.part - full * 128

    def load(source, target):
        target[0:full, :] = source[pl.ds(0, full * 128)].reshape(full, 128)
        if edge:
            target[full:full + 1, :] = jnp.zeros((1, 128), F32)
            target[full:full + 1, 0:edge] = source[pl.ds(full * 128, edge)].reshape(1, edge)

    def store(target, value, last):
        target[pl.ds(0, full * 128)] = value[0:full, :].reshape(full * 128).astype(target.dtype)
        if edge:
            target[pl.ds(full * 128, edge)] = last[:, 0:edge].reshape(edge).astype(target.dtype)

    lane = iota((1, 128), 1)

    def sums(ref):
        out = jnp.zeros((1, 128), F32)
        for m in range(len(layout.widths)):
            lo, hi = layout.starts[m], layout.starts[m + 1]
            r0, r1 = -(-lo // 128), hi // 128
            total = jnp.zeros((1, 1), F32)
            if r1 > r0:
                total = total + jnp.sum(jnp.sum(ref[r0:r1, :], axis=0, keepdims=True), axis=1, keepdims=True)
            for row in {lo // 128, hi // 128}:
                left, right = max(lo, row * 128) - row * 128, min(hi, row * 128 + 128) - row * 128
                if left < right and not (left == 0 and right == 128):
                    part = jnp.where((lane >= left) & (lane < right), ref[row:row + 1, :], 0.0)
                    total = total + jnp.sum(part, axis=1, keepdims=True)
            out = jnp.where(lane == m, total, out)
        return out

    lines = full + (1 if edge else 0)
    load(master, w2)
    load(moment1, a2)
    load(moment2, b2)
    g = g_ref[0:lines, :]
    w = w2[0:lines, :]
    sq[0:lines, :] = w * w
    weight_squares = sums(sq)
    squares = jnp.sum(jnp.sum(g * g, axis=0, keepdims=True), axis=1, keepdims=True)
    loss = att[0:1, :] + ctc[0:1, :]
    row = jnp.where(lane == 120, squares, jnp.where(lane == 121, loss, weight_squares))
    line[0] = jnp.broadcast_to(row, (8, 128))
    end = share_sum(here, line.at[0], recv, sems, 0)
    row = line[0, 0:1, :]
    clip = jnp.sqrt(jnp.sum(jnp.where(lane == 120, row, 0.0), axis=1, keepdims=True))
    loss_ref[0] = jnp.sum(jnp.where(lane == 121, row, 0.0)) / utterances
    weight_norms = jnp.sqrt(row)
    scaled = g * jnp.minimum(1.0, 1.0 / clip)
    first = 0.5 * a2[0:lines, :] + 0.5 * scaled
    second = 0.5 * b2[0:lines, :] + 0.5 * scaled * scaled
    correct = 1.0 - 0.5**STEP
    direction = first / correct / (jnp.sqrt(second / correct) + 1e-06) + 0.01 * w
    a2[0:lines, :] = direction
    sq[0:lines, :] = direction * direction
    store(first_ref, first, first[full:, :])
    store(second_ref, second, second[full:, :])
    line[1] = jnp.broadcast_to(sums(sq), (8, 128))
    share_sum(here, line.at[1], recv, sems, end)
    update_norms = jnp.sqrt(line[1, 0:1, :])
    clip_ref[0] = jnp.sum(clip)
    count = len(layout.widths)
    wn_ref[...] = weight_norms[:, 0:count].reshape(count)
    un_ref[...] = update_norms[:, 0:count].reshape(count)
    ratio = 0.5 * weight_norms / update_norms
    for m in range(count):
        scale = jnp.sum(jnp.where(lane == m, ratio, 0.0), axis=1, keepdims=True)
        lo, hi = layout.starts[m], layout.starts[m + 1]
        r0, r1 = -(-lo // 128), hi // 128
        if r1 > r0:
            w2[r0:r1, :] -= scale * a2[r0:r1, :]
        for at in {lo // 128, hi // 128}:
            left, right = max(lo, at * 128) - at * 128, min(hi, at * 128 + 128) - at * 128
            if left < right and not (left == 0 and right == 128):
                w2[at:at + 1, :] -= jnp.where((lane >= left) & (lane < right), scale * a2[at:at + 1, :], 0.0)
    fresh = w2[0:lines, :]
    store(fresh_ref, fresh, fresh[full:, :])
    store(low_ref, fresh, fresh[full:, :])


def lamb(geo, layout, utterances, g, master, moment1, moment2, att, ctc):
    part, lines, count = layout.part, layout.lines, len(layout.widths)
    slots = 2 * (2 + geo.ny + geo.nf + geo.ns)
    loss, clip, first, second, fresh, low, weight_norms, update_norms = pl.pallas_call(
        functools.partial(lamb_kernel, geo, layout, utterances),
        out_shape=[shape(1), shape(1), shape(part), shape(part), shape(part), shape(part, dtype=BF), shape(count), shape(count)],
        in_specs=[VM] * 6,
        out_specs=[SM, SM] + [VM] * 6,
        scratch_shapes=[pltpu.VMEM((lines, 128), F32)] * 4 + [pltpu.VMEM((2, 8, 128), F32), pltpu.VMEM((slots, 8, 128), F32),
                                                          pltpu.SemaphoreType.DMA((2, slots))],
        name="lamb",
        compiler_params=pltpu.CompilerParams(vmem_limit_bytes=VMEM_LIMIT, collective_id=1, has_side_effects=True),
    )(g, master, moment1, moment2, att, ctc)
    return loss[0], clip[0], first, second, fresh, low, weight_norms, update_norms


def solution(mesh):
    n_bucket, n_dp = mesh.shape["bucket"], mesh.shape["dp"]
    geo = Geometry(n_bucket, n_dp)

    def body(filter_bank, frame_len, tok_len, targets, *rest):
        weights, (master, moment1, moment2) = rest[:13], rest[13:]
        utterances = frame_len.shape[0] * n_bucket * n_dp
        plan, att, ctc, g_dec, g_ctc, g_enc = gradients(n_bucket, utterances, filter_bank, frame_len, tok_len, targets, weights)
        layout = Layout(plan, geo, [w.size for w in weights])
        g = sum_over_devices(geo, plan, layout, g_dec, g_ctc, g_enc)
        return lamb(geo, layout, utterances, g, master, moment1, moment2, att, ctc)

    both = P(("bucket", "dp"))
    in_specs = (P(("bucket", "dp"), None, None), both, both, P(("bucket", "dp"), None)) + (P(),) * 13 + (both,) * 3
    out_specs = (P(), P(), both, both, both, both, P(), P())
    return jax.shard_map(body, mesh=mesh, in_specs=in_specs, out_specs=out_specs, check_vma=False)
```

```python
import functools
import math

import jax
import jax.numpy as jnp
import numpy as np
from jax import lax
from jax.experimental import pallas as pl
from jax.experimental.pallas import tpu as pltpu
from jax.sharding import PartitionSpec as P

HEADS = 4
STEP = 5
GROUPS = 32
BF = jnp.bfloat16
F32 = jnp.float32
NEG_SCORE = -1e9
NEG_PATH = -1e5
FLOOR = -1e30
LOG2E = 1.4426950408889634
VMEM_LIMIT = 63 * 2**20


def dot(a, b):
    return lax.dot_general(a, b, (((1,), (0,)), ((), ())), preferred_element_type=F32)


def dot_rt(a, b):
    return lax.dot_general(a, b, (((1,), (1,)), ((), ())), preferred_element_type=F32)


def dot_lt(a, b):
    return lax.dot_general(a, b, (((0,), (0,)), ((), ())), preferred_element_type=F32)


def halves(value):
    high = value.astype(BF)
    return high, (value - high.astype(F32)).astype(BF)


def iota(shape, dim):
    return lax.broadcasted_iota(jnp.int32, shape, dim)


def normalised(x):
    mean = jnp.mean(x, axis=-1, keepdims=True)
    centre = x - mean
    rstd = lax.rsqrt(jnp.mean(centre * centre, axis=-1, keepdims=True) + 1e-05)
    return centre * rstd, rstd


def norm_back(dy, unit, rstd, gain):
    dunit = dy * gain
    dx = rstd * (
        dunit
        - jnp.mean(dunit, axis=-1, keepdims=True)
        - unit * jnp.mean(dunit * unit, axis=-1, keepdims=True)
    )
    return dx, jnp.sum(dy * unit, axis=0, keepdims=True), jnp.sum(dy, axis=0, keepdims=True)


def softmax(scores):
    shifted = scores - jnp.max(scores, axis=-1, keepdims=True)
    e = jnp.exp(shifted)
    return e * (1.0 / jnp.sum(e, axis=-1, keepdims=True))


def head_mask(width, h):
    size = width // HEADS
    lane = iota((1, width), 1)
    return (lane >= h * size) & (lane < (h + 1) * size)


def pick_head(value, h):
    return jnp.where(head_mask(value.shape[-1], h), value, jnp.zeros((), value.dtype))


def attend(q, k, v, allowed):
    scale = 1.0 / math.sqrt(q.shape[-1] // HEADS)
    total = None
    for h in range(HEADS):
        s = jnp.where(allowed, dot_rt(q, pick_head(k, h)) * scale, NEG_SCORE)
        c = dot(softmax(s).astype(BF), pick_head(v, h))
        total = c if total is None else total + c
    return total


def attend_back(q, k, v, allowed, dctx):
    scale = 1.0 / math.sqrt(q.shape[-1] // HEADS)
    dq = dk = dv = None
    for h in range(HEADS):
        kh, vh = pick_head(k, h), pick_head(v, h)
        p = softmax(jnp.where(allowed, dot_rt(q, kh) * scale, NEG_SCORE))
        dvh = dot_lt(p.astype(BF), pick_head(dctx, h))
        dp = dot_rt(dctx, vh)
        ds = p * (dp - jnp.sum(p * dp, axis=-1, keepdims=True))
        ds = jnp.where(allowed, ds, 0.0).astype(BF)
        dqh = dot(ds, kh)
        dkh = dot_lt(ds, pick_head(q, h))
        if dq is None:
            dq, dk, dv = dqh, dkh, dvh
        else:
            dq, dk, dv = dq + dqh, dk + dkh, dv + dvh
    return dq * scale, dk * scale, dv


def spans(total, size):
    return [(at, min(size, total - at)) for at in range(0, total, size)]


def put8(ref, base, value, first=0):
    rows, width = value.shape
    deep = rows // GROUPS
    if width % 128:
        value = jnp.pad(value, ((0, 0), (0, 128 - width % 128)))
    for c in range(first, value.shape[1] // 128):
        at = base + deep * c
        ref[:, at:at + deep, :] = value[:, 128 * c:128 * (c + 1)].reshape(GROUPS, deep, 128)


def put_rows(ref, base, value, row, rows):
    deep = rows // GROUPS
    count = value.shape[0] // deep
    for c in range(value.shape[1] // 128):
        at = base + deep * c
        ref[row // deep:row // deep + count, at:at + deep, :] = value[:, 128 * c:128 * (c + 1)].reshape(count, deep, 128)


def put_small(ref, row, value):
    width = value.shape[1]
    part = 7 * width // GROUPS
    line = jnp.concatenate([value[i:i + 1, :] for i in range(8)], axis=1)
    for q in range(GROUPS):
        ref[q, row:row + 1, :] = line[:, part * q:part * q + 128]


def token_line(ref):
    return jnp.concatenate([ref[u:u + 1, :] for u in range(ref.shape[0])], axis=1)


def scalar_line(plan, ref):
    owner = iota((1, plan.drows), 1) // plan.tokens
    line = jnp.zeros((1, plan.drows), jnp.int32)
    for u in range(plan.utts):
        line = jnp.where(owner == u, ref[u], line)
    return line


def columns(lines):
    n = lines[0].shape[1]
    block = jnp.concatenate(lines + [jnp.zeros((8 - len(lines), n), lines[0].dtype)], axis=0)
    turned = block.T
    return [turned[:, i:i + 1] for i in range(len(lines))]


class Plan:
    def __init__(self, utts, frames, n_bucket, tokens, width, ff, vocab, feat):
        self.utts, self.frames, self.tokens = utts, frames, tokens
        self.width, self.ff, self.vocab = width, ff, vocab
        if utts % n_bucket == 0:
            self.caps = [frames * (i % n_bucket + 1) // n_bucket for i in range(utts)]
        else:
            self.caps = [frames] * utts
        self.starts = [sum(self.caps[:i]) for i in range(utts)]
        self.rows = sum(self.caps)
        self.drows = utts * tokens
        self.chunk = 1024 if self.rows <= 768 else 512
        self.embed_rows = -(-(vocab // GROUPS + 2) // 16) * 16
        tiles = -(-vocab // 128)
        deep = width // GROUPS
        self.out_rows = tiles * deep
        attn, ff = 4 * width // 128 * deep, ff // 128 * deep
        embed = self.embed_rows * width // 128
        ends = np.cumsum([0, self.out_rows, ff, ff, attn])
        self.early_at, self.early_rows = [int(x) for x in ends[:-1]], int(ends[-1])
        self.late_at, self.late_rows = [0, attn], attn + embed
        self.ctc_rows = (tiles + 2) * deep
        self.sub_rows = -(-(feat // GROUPS) // 8) * 8
        ends = np.cumsum([16, ff, ff, attn, self.sub_rows * width // 128])
        self.enc_at, self.enc_rows = [int(x) for x in ends[:-1]], int(ends[-1])


def enc_fwd_part(plan, tick, len_ref, fb_ref, pe_ref, w_sub, w_attn, w_ff1, w_ff2, gain, bias,
                   h0_ref, qkv_ref, ctx_ref, h1_ref, h2_ref, enc_ref):
    d = plan.width
    gain, bias = gain[...].astype(F32), bias[...].astype(F32)
    for u in range(plan.utts):
        t, at = plan.caps[u], plan.starts[u]
        h0_ref[at:at + t, :] = dot_lt(fb_ref[u, :, 0:t], w_sub[...]) + pe_ref[0:t, :]
    unit, _ = normalised(h0_ref[...])
    a0 = (unit * gain[0:1, :] + bias[0:1, :]).astype(BF)
    qkv_ref[...] = dot(a0, w_attn[:, : 3 * d]).astype(BF)
    for u in range(plan.utts):
        t, at = plan.caps[u], plan.starts[u]
        allowed = iota((1, t), 1) < len_ref[u]
        piece = qkv_ref[at:at + t, :]
        ctx = attend(piece[:, :d], piece[:, d:2 * d], piece[:, 2 * d:], allowed)
        ctx_ref[at:at + t, :] = ctx.astype(BF)
    h1 = h0_ref[...] + dot(ctx_ref[...], w_attn[:, 3 * d:])
    h1_ref[...] = h1
    tick("encoder feed")
    unit, _ = normalised(h1)
    a1 = (unit * gain[1:2, :] + bias[1:2, :]).astype(BF)
    h2_ref[...] = h1
    for c, size in spans(plan.ff, plan.chunk // 2):
        inner = dot(a1, w_ff1[:, c:c + size])
        act = (inner * jax.nn.sigmoid(inner)).astype(BF)
        h2_ref[...] += dot(act, w_ff2[c:c + size, :])
    unit, _ = normalised(h2_ref[...])
    enc_ref[...] = (unit * gain[2:3, :] + bias[2:3, :]).astype(BF)


def enc_bwd_part(plan, tick, len_ref, fb_ref, perm_ref, w_attn, w_ff1, w_ff2, gain, bias,
                   h0_ref, qkv_ref, ctx_ref, h1_ref, h2_ref, denc_ref,
                   gg_dec, gb_dec, g_ref, dh_ref, db_ref, dqkv_ref):
    gain, bias = gain[...].astype(F32), bias[...].astype(F32)
    d, deep = plan.width, plan.width // GROUPS
    at_ff2, at_ff1, at_attn, at_sub = plan.enc_at
    g_ref[:, 0:16, :] = jnp.zeros((GROUPS, 16, 128), F32)
    denc = denc_ref[...].astype(BF).astype(F32)
    unit, rstd = normalised(h2_ref[...])
    dh2, gg2, gb2 = norm_back(denc, unit, rstd, gain[2:3, :])
    dh_ref[...] = dh2
    dout = dh2.astype(BF)
    unit1, rstd1 = normalised(h1_ref[...])
    a1 = (unit1 * gain[1:2, :] + bias[1:2, :]).astype(BF)
    for c, size in spans(plan.ff, plan.chunk // 2):
        inner = dot(a1, w_ff1[:, c:c + size])
        sig = jax.nn.sigmoid(inner)
        act = inner * sig
        put_rows(g_ref, at_ff2, dot_lt(act.astype(BF), dout), c, plan.ff)
        dact = dot_rt(dout, w_ff2[c:c + size, :])
        dinner = (dact * (sig + act * (1.0 - sig))).astype(BF)
        put8(g_ref, at_ff1 + c // 128 * deep, dot_lt(a1, dinner))
        part = dot_rt(dinner, w_ff1[:, c:c + size])
        if c == 0:
            db_ref[...] = part
        else:
            db_ref[...] += part
        if c % 512 == 0:
            tick("ff%d" % (c // 512))
    dx, gg1, gb1 = norm_back(db_ref[...], unit1, rstd1, gain[1:2, :])
    dh1 = dh_ref[...] + dx
    dh_ref[...] = dh1
    dout = dh1.astype(BF)
    put8(g_ref, at_attn + 3 * d // 128 * deep, dot_lt(ctx_ref[...], dout))
    dctx = dot_rt(dout, w_attn[:, 3 * d:]).astype(BF)
    tick("out")
    for u in range(plan.utts):
        t, at = plan.caps[u], plan.starts[u]
        allowed = iota((1, t), 1) < len_ref[u]
        piece = qkv_ref[at:at + t, :]
        dq, dk, dv = attend_back(piece[:, :d], piece[:, d:2 * d], piece[:, 2 * d:], allowed, dctx[at:at + t, :])
        dqkv_ref[at:at + t, :d] = dq.astype(BF)
        dqkv_ref[at:at + t, d:2 * d] = dk.astype(BF)
        dqkv_ref[at:at + t, 2 * d:] = dv.astype(BF)
        tick("attn%d" % u)
    unit, rstd = normalised(h0_ref[...])
    a0 = (unit * gain[0:1, :] + bias[0:1, :]).astype(BF)
    dqkv = dqkv_ref[...]
    put8(g_ref, at_attn, dot_lt(a0, dqkv))
    da0 = dot_rt(dqkv, w_attn[:, :3 * d])
    dx, gg0, gb0 = norm_back(da0, unit, rstd, gain[0:1, :])
    dh0 = (dh_ref[...] + dx).astype(BF)
    g = None
    for u in range(plan.utts):
        t, at = plan.caps[u], plan.starts[u]
        part = dot(fb_ref[u, :, 0:t], dh0[at:at + t, :])
        g = part if g is None else g + part
    high, low = halves(g)
    lower = (g - high.astype(F32) - low.astype(F32)).astype(BF)
    perm = perm_ref[...]
    put_rows(g_ref, at_sub, dot(perm, high) + dot(perm, low) + dot(perm, lower), 0, perm.shape[0])
    put_small(g_ref, 0, gg_dec[...] + jnp.concatenate([gg0, gg1, gg2, jnp.zeros((5, d), F32)], axis=0))
    put_small(g_ref, 1, gb_dec[...] + jnp.concatenate([gb0, gb1, gb2, jnp.zeros((5, d), F32)], axis=0))


def dec_part(plan, utterances, tick, len_ref, count_ref, target_ref, pe_ref, enc_ref, w_self, w_cross, w_ff1,
             w_ff2, embed, w_out, gain, bias, loss_ref, g_ref, late_ref, g_gain, g_bias, denc_ref, kv_ref):
    d, rows, vocab = plan.width, plan.drows, plan.vocab
    deep = d // GROUPS
    at_out, at_ff1, at_ff2, at_cross = plan.early_at
    at_self, at_embed = plan.late_at
    gain, bias = gain[...].astype(F32), bias[...].astype(F32)
    line, counts = token_line(target_ref), scalar_line(plan, count_ref)
    spot = iota((1, rows), 1) % plan.tokens
    toks = jnp.where(spot == 0, vocab - 1, pltpu.roll(line, 1, 1))
    tick("decoder")
    tok, want, live = columns([toks, jnp.where(spot == counts, vocab - 1, line), jnp.where(spot <= counts, 1, 0)])
    live = live.astype(F32)
    chunks = spans(vocab, 1024)
    place = iota((1, 1024), 1)
    y = None
    for c, size in chunks:
        hot = jnp.where(tok == place[:, :size] + c, 1.0, 0.0).astype(BF)
        part = dot(hot, embed[c:c + size, :])
        y = part if y is None else y + part
    y0 = y * math.sqrt(d) + pe_ref[...]
    tick("self")
    unit3, rstd3 = normalised(y0)
    a3 = (unit3 * gain[3:4, :] + bias[3:4, :]).astype(BF)
    mixed = dot(a3, w_self[:, : 3 * d]).astype(BF)
    q, k, v = mixed[:, :d], mixed[:, d:2 * d], mixed[:, 2 * d:]
    row, col = iota((rows, rows), 0), iota((rows, rows), 1)
    causal = (row // plan.tokens == col // plan.tokens) & (col <= row)
    ctx = attend(q, k, v, causal).astype(BF)
    y1 = y0 + dot(ctx, w_self[:, 3 * d:])
    tick("cross")
    unit4, rstd4 = normalised(y1)
    a4 = (unit4 * gain[4:5, :] + bias[4:5, :]).astype(BF)
    cq = dot(a4, w_cross[:, :d]).astype(BF)
    kv_ref[...] = dot(enc_ref[...], w_cross[:, d:3 * d]).astype(BF)
    owner = iota((rows, 1), 0) // plan.tokens
    frame = iota((1, plan.rows), 1)
    valid = None
    for u in range(plan.utts):
        here = (owner == u) & (frame >= plan.starts[u]) & (frame < plan.starts[u] + len_ref[u])
        valid = here if valid is None else valid | here
    ck, cv = kv_ref[:, :d], kv_ref[:, d:]
    cctx = attend(cq, ck, cv, valid).astype(BF)
    y2 = y1 + dot(cctx, w_cross[:, 3 * d:])
    tick("feed")
    unit5, rstd5 = normalised(y2)
    a5 = (unit5 * gain[5:6, :] + bias[5:6, :]).astype(BF)
    y3 = y2
    for c, size in spans(plan.ff, 1024):
        inner = dot(a5, w_ff1[:, c:c + size])
        act = (inner * jax.nn.sigmoid(inner)).astype(BF)
        y3 = y3 + dot(act, w_ff2[c:c + size, :])
    unit6, rstd6 = normalised(y3)
    a6 = (unit6 * gain[6:7, :] + bias[6:7, :]).astype(BF)
    tick("head")
    peak = jnp.full((rows, 1), FLOOR, F32)
    mass = jnp.zeros((rows, 1), F32)
    picked = jnp.zeros((rows, 1), F32)
    summed = jnp.zeros((rows, 1), F32)
    for c, size in chunks:
        z = dot_rt(a6, w_out[c:c + size, :])
        top = jnp.maximum(peak, jnp.max(z, axis=-1, keepdims=True))
        mass = mass * jnp.exp(peak - top) + jnp.sum(jnp.exp(z - top), axis=-1, keepdims=True)
        peak = top
        picked = picked + jnp.sum(jnp.where(want == place[:, :size] + c, z, 0.0), axis=-1, keepdims=True)
        summed = summed + jnp.sum(z, axis=-1, keepdims=True)
    lse = peak + jnp.log(mass)
    rest = 0.1 / (vocab - 1)
    others = (summed - vocab * lse) - (picked - lse)
    per_token = -(0.9 * (picked - lse) + rest * others)
    loss_ref[...] = jnp.full((8, 128), 0.7 * jnp.sum(live * per_token), F32)
    weight = live * (0.7 / utterances)
    da6 = None
    for c, size in chunks:
        z = dot_rt(a6, w_out[c:c + size, :])
        share = jnp.exp(z - lse) * (0.9 + rest * (vocab - 1))
        dz = share - jnp.where(want == place[:, :size] + c, 0.9, rest)
        dz = (dz * weight).astype(BF)
        put8(g_ref, at_out + c // 128 * deep, dot_lt(a6, dz))
        part = dot(dz, w_out[c:c + size, :])
        da6 = part if da6 is None else da6 + part
    dy, gg6, gb6 = norm_back(da6, unit6, rstd6, gain[6:7, :])
    tick("head back")
    dout = dy.astype(BF)
    da5 = None
    for c, size in spans(plan.ff, 1024):
        inner = dot(a5, w_ff1[:, c:c + size])
        sig = jax.nn.sigmoid(inner)
        act = inner * sig
        put_rows(g_ref, at_ff2, dot_lt(act.astype(BF), dout), c, plan.ff)
        dact = dot_rt(dout, w_ff2[c:c + size, :])
        dinner = (dact * (sig + act * (1.0 - sig))).astype(BF)
        put8(g_ref, at_ff1 + c // 128 * deep, dot_lt(a5, dinner))
        part = dot_rt(dinner, w_ff1[:, c:c + size])
        da5 = part if da5 is None else da5 + part
    dx, gg5, gb5 = norm_back(da5, unit5, rstd5, gain[5:6, :])
    dy = dy + dx
    tick("feed back")
    dout = dy.astype(BF)
    tile = d // 128 * deep
    put8(g_ref, at_cross + 3 * tile, dot_lt(cctx, dout))
    dctx = dot_rt(dout, w_cross[:, 3 * d:]).astype(BF)
    dq, dk, dv = attend_back(cq, ck, cv, valid, dctx)
    dq, dk, dv = dq.astype(BF), dk.astype(BF), dv.astype(BF)
    enc = enc_ref[...]
    put8(g_ref, at_cross + tile, dot_lt(enc, dk))
    put8(g_ref, at_cross + 2 * tile, dot_lt(enc, dv))
    denc_ref[...] = dot_rt(dk, w_cross[:, d:2 * d]) + dot_rt(dv, w_cross[:, 2 * d:3 * d])
    put8(g_ref, at_cross, dot_lt(a4, dq))
    da4 = dot_rt(dq, w_cross[:, :d])
    dx, gg4, gb4 = norm_back(da4, unit4, rstd4, gain[4:5, :])
    dy = dy + dx
    tick("cross back")
    dout = dy.astype(BF)
    put8(late_ref, at_self + 3 * tile, dot_lt(ctx, dout))
    dctx = dot_rt(dout, w_self[:, 3 * d:]).astype(BF)
    dq, dk, dv = attend_back(q, k, v, causal, dctx)
    dq, dk, dv = dq.astype(BF), dk.astype(BF), dv.astype(BF)
    put8(late_ref, at_self, dot_lt(a3, dq))
    put8(late_ref, at_self + tile, dot_lt(a3, dk))
    put8(late_ref, at_self + 2 * tile, dot_lt(a3, dv))
    da3 = dot_rt(dq, w_self[:, :d]) + dot_rt(dk, w_self[:, d:2 * d]) + dot_rt(dv, w_self[:, 2 * d:3 * d])
    dx, gg3, gb3 = norm_back(da3, unit3, rstd3, gain[3:4, :])
    high, low = halves((dy + dx) * math.sqrt(d))
    share_rows, tall = vocab // GROUPS, plan.embed_rows

    def block(i, carry):
        first = share_rows * i + (vocab - share_rows * GROUPS) * i // GROUPS
        hot = jnp.where(iota((tall, rows), 0) + first == toks, 1.0, 0.0).astype(BF)
        value = dot(hot, high) + dot(hot, low)
        for c in range(d // 128):
            late_ref[i, at_embed + tall * c:at_embed + tall * (c + 1), :] = value[:, 128 * c:128 * (c + 1)]
        return carry

    tick("self back")
    for i, (at, size) in enumerate(spans(GROUPS, GROUPS // 4)):
        lax.fori_loop(at, at + size, block, 0, unroll=4)
        tick("embed%d" % i)
    g_gain[...] = jnp.concatenate([jnp.zeros((3, d), F32), gg3, gg4, gg5, gg6, jnp.zeros((1, d), F32)], axis=0)
    g_bias[...] = jnp.concatenate([jnp.zeros((3, d), F32), gb3, gb4, gb5, gb6, jnp.zeros((1, d), F32)], axis=0)


def ctc_part(plan, utterances, tick, len_ref, count_ref, target_ref, enc_ref, w_ref, denc_in,
               g_ref, denc_ref,
               peak_ref, mass_ref, sel_ref, em_ref, cum_ref, alpha_ref, beta_ref, gam_hi, gam_lo):
    d, vocab, frames, toks = plan.width, plan.vocab, plan.frames, plan.tokens
    lanes, deep = plan.drows, d // GROUPS
    g_ref[:, deep:2 * deep, :] = jnp.zeros((GROUPS, deep, 128), F32)
    g_ref[:, plan.ctc_rows - deep:, :] = jnp.zeros((GROUPS, deep, 128), F32)
    chunks = spans(vocab, plan.chunk)
    place = iota((1, plan.chunk), 1)
    line, counts, lens = token_line(target_ref), scalar_line(plan, count_ref), scalar_line(plan, len_ref)
    (labels,) = columns([line])
    enc = enc_ref[...]
    peak = jnp.full((plan.rows, 1), FLOOR, F32)
    mass = jnp.zeros((plan.rows, 1), F32)
    sel_ref[...] = jnp.zeros((lanes, d), F32)
    blank = None
    for c, size in chunks:
        wc = w_ref[c:c + size, :]
        z = dot_rt(enc, wc)
        if c == 0:
            blank = z[:, 0:1]
        top = jnp.maximum(peak, jnp.max(z, axis=-1, keepdims=True))
        mass = mass * jnp.exp(peak - top) + jnp.sum(jnp.exp(z - top), axis=-1, keepdims=True)
        peak = top
        hot = jnp.where(labels == place[:, :size] + c, 1.0, 0.0).astype(BF)
        sel_ref[...] += dot(hot, wc)
        if c % 1024 == 0:
            tick("first%d" % (c // 1024))
    lse = peak + jnp.log(mass)
    peak_ref[:, 0:1] = lse
    tick("prep")
    lane = iota((1, lanes), 1)
    sel = sel_ref[...].astype(BF)
    em_ref[...] = jnp.zeros((frames, lanes), F32)
    mass_ref[...] = jnp.zeros((frames, lanes), F32)
    for u in range(plan.utts):
        t, at = plan.caps[u], plan.starts[u]
        mine = lane // toks == u
        z = dot_rt(enc[at:at + t, :], sel)
        em_ref[0:t, :] += jnp.where(mine, (z - blank[at:at + t, :]) * LOG2E, 0.0)
        mass_ref[0:t, :] += jnp.where(mine, (blank[at:at + t, :] - lse[at:at + t, :]) * LOG2E, 0.0)
    lower = jnp.where(iota((frames, frames), 0) >= iota((frames, frames), 1), 1.0, 0.0).astype(BF)
    drift = mass_ref[...]
    high, mid = halves(drift)
    low = (drift - high.astype(F32) - mid.astype(F32)).astype(BF)
    total = dot(lower, high) + dot(lower, mid) + dot(lower, low)
    neg = NEG_PATH * LOG2E
    cum_ref[...] = neg - total
    first = lane % toks == 0
    final = lane % toks == toks - 1
    skip = (line != pltpu.roll(line, 1, 1)) & (lane % toks > 0)
    skip_next = (line != pltpu.roll(line, lanes - 1, 1)) & (lane % toks < toks - 1)
    ending = lane % toks == counts - 1
    begin_beta = jnp.where(ending, 0.0, FLOOR)
    end_frame = lens - 1

    def log_sum(a, b, c):
        top = jnp.maximum(jnp.maximum(a, b), c)
        return top, jnp.log2(jnp.exp2(a - top) + jnp.exp2(b - top) + jnp.exp2(c - top))

    def log_pair(a, b):
        top = jnp.maximum(a, b)
        return top + jnp.log2(jnp.exp2(a - top) + jnp.exp2(b - top))

    def step(i, carry):
        la, ba, lb, bb = carry
        fill = cum_ref[pl.ds(jnp.maximum(i - 1, 0), 1), :]
        shifted = jnp.where(first, fill, pltpu.roll(la, 1, 1))
        e = em_ref[pl.ds(i, 1), :]
        top, rest = log_sum(la, ba, jnp.where(skip, shifted, fill))
        la2 = (top + e) + rest
        top, rest = log_sum(ba, shifted, fill)
        ba2 = top + rest
        start = i == 0
        la2 = jnp.where(start, jnp.where(first, e, fill0), la2)
        ba2 = jnp.where(start, jnp.where(first, 0.0, fill0), ba2)
        alpha_ref[pl.ds(i, 1), :] = la2
        t = frames - 1 - i
        e = em_ref[pl.ds(t, 1), :]
        shifted = jnp.where(final, FLOOR, pltpu.roll(lb, lanes - 1, 1))
        top, rest = log_sum(lb, bb, jnp.where(skip_next, shifted, FLOOR))
        lb2 = (top + e) + rest
        bb2 = log_pair(bb, shifted)
        begin = end_frame == t
        lb2 = jnp.where(begin, begin_beta + e, lb2)
        bb2 = jnp.where(begin, begin_beta, bb2)
        beta_ref[pl.ds(t, 1), :] = lb2
        keep = end_frame >= i
        return (jnp.where(keep, la2, la), jnp.where(keep, ba2, ba), lb2, bb2)

    fill0 = cum_ref[0:1, :]
    flat = jnp.full((1, lanes), FLOOR, F32)
    carry = (flat, flat, flat, flat)
    for i, (at, size) in enumerate(spans(frames, frames // 16)):
        carry = lax.fori_loop(at, at + size, step, carry, unroll=2)
        tick("scan%d" % i)
    la, ba = carry[:2]
    after = jnp.where(first, FLOOR, pltpu.roll(jnp.where(ending, 0.0, FLOOR), 1, 1))
    moment = iota((frames, lanes), 0)
    at_end = jnp.sum(jnp.where(moment == end_frame, neg - cum_ref[...], 0.0), axis=0, keepdims=True)
    floor = NEG_PATH * 10.0 * LOG2E - at_end
    tail = jnp.maximum(jnp.where(ending, la, FLOOR), jnp.where(after == 0.0, ba, FLOOR))
    logz = jnp.zeros((1, lanes), F32)
    ctc = jnp.zeros((), F32)
    for u in range(plan.utts):
        mine = lane // toks == u
        top = jnp.max(jnp.where(mine, tail, FLOOR), axis=-1, keepdims=True)
        bottom = jnp.max(jnp.where(mine, floor, FLOOR), axis=-1, keepdims=True)
        top = jnp.maximum(top, bottom)
        weight = jnp.where(mine & ending, jnp.exp2(la - top), 0.0) + jnp.where(mine & (after == 0.0), jnp.exp2(ba - top), 0.0)
        full = top + jnp.log2(jnp.sum(weight, axis=-1, keepdims=True) + jnp.exp2(bottom - top))
        logz = jnp.where(mine, full, logz)
        drift_end = jnp.max(jnp.where(mine, at_end, FLOOR), axis=-1, keepdims=True)
        ctc = ctc - jnp.sum(full + drift_end) / LOG2E
    gamma = jnp.exp2(alpha_ref[...] + beta_ref[...] - em_ref[...] - logz)
    gamma = jnp.where(moment <= end_frame, gamma, 0.0)
    for u in range(plan.utts):
        t, at = plan.caps[u], plan.starts[u]
        mine = lane // toks == u
        piece = jnp.where(mine, gamma[0:t, :], 0.0)
        high, low = halves(piece)
        gam_hi[at:at + t, :] = high
        gam_lo[at:at + t, :] = low
        alive = jnp.where(iota((t, 1), 0) < len_ref[u], 1.0, 0.0)
        peak_ref[at:at + t, 1:2] = alive
        peak_ref[at:at + t, 2:3] = alive - jnp.sum(piece, axis=-1, keepdims=True)
    lse = peak_ref[:, 0:1]
    scale = 0.3 / utterances
    live = peak_ref[:, 1:2] * scale
    blank_share = peak_ref[:, 2:3]
    denc_ref[...] = denc_in[...]
    for c, size in chunks:
        wc = w_ref[c:c + size, :]
        p = jnp.exp(dot_rt(enc, wc) - lse) * live
        hot = jnp.where(labels == place[:, :size] + c, 1.0, 0.0).astype(BF)
        post = dot(gam_hi[...], hot) + dot(gam_lo[...], hot)
        dz = p - post * scale
        if c == 0:
            dz = dz - jnp.where(place[:, :size] == 0, blank_share * scale, 0.0)
        dz = dz.astype(BF)
        value = dot_lt(enc, dz)
        if c == 0:
            g_ref[:, 0:deep, :] = value[:, :128].reshape(GROUPS, deep, 128)
        put8(g_ref, deep + c // 128 * deep, value, 1 if c == 0 else 0)
        denc_ref[...] += dot(dz, wc)
        if c % 1024 == 0:
            tick("second%d" % (c // 1024))
    return 0.3 * ctc


VM = pl.BlockSpec(memory_space=pltpu.VMEM)
SM = pl.BlockSpec(memory_space=pltpu.SMEM)
ANY = pl.BlockSpec(memory_space=pl.ANY)


def shape(*dims, dtype=F32):
    return jax.ShapeDtypeStruct(dims, dtype)


class Beside:
    def __init__(self, sems):
        self.sems, self.copies = sems, {}

    def start(self, name, source, target):
        copy = pltpu.make_async_copy(source, target, self.sems.at[len(self.copies)])
        self.copies[name] = copy
        copy.start()

    def wait(self, *names):
        for name in names:
            self.copies[name].wait()


class Pair:
    def __init__(self, geo, here, g_ref, recv, out, sems):
        self.geo, self.here, self.g, self.recv, self.out, self.sems = geo, here, g_ref, recv, out, sems

    def copies(self, i, a, b):
        span, at = pl.ds(a, b - a), self.here.at
        return [pltpu.make_async_remote_copy(
            src_ref=self.g.at[2 * y + 1 - at["c"], :, span], dst_ref=self.recv.at[y, :, span],
            send_sem=self.sems.at[0, i, y], recv_sem=self.sems.at[1, i, y],
            device_id=self.here.device("c", 0), device_id_type=MESH) for y in range(self.geo.ny)]

    def keep(self, i, a, b):
        span, at = pl.ds(a, b - a), self.here.at
        return [pltpu.make_async_copy(self.g.at[2 * y + at["c"], :, span], self.out.at[y, :, span], self.sems.at[2, i, y])
                for y in range(self.geo.ny)]

    def start(self, *span):
        for copy in self.copies(*span):
            copy.start()

    def finish(self, i, a, b):
        for copy in self.copies(i, a, b):
            copy.wait()
        many = self.geo.ns * self.geo.gf

        def add(k, carry):
            y, sf = k // many, k % many
            self.g[2 * y + self.here.at["c"], sf, a:b, :] += self.recv[y, sf, a:b, :]
            return carry

        lax.fori_loop(0, self.geo.ny * many, add, 0)
        for copy in self.keep(i, a, b):
            copy.start()

    def end(self, *span):
        for copy in self.keep(*span):
            copy.wait()


def front_kernel(geo, plan, utterances, *refs):
    refs = list(refs)

    def take(count):
        out = refs[:count]
        del refs[:count]
        return out

    len_ref, count_ref, target_ref, bank, pe, pe_tok, w_sub, w_attn, gain, bias = take(10)
    far = take(8)
    h0_out, qkv_out, ctx_out, h1_out, h2_out, early_out, late_out = take(7)
    enc, att, gg, gb, denc = take(5)
    near = take(8)
    w_ff1, w_ff2, embed, w_self, w_cross, d_ff1, d_ff2, w_out = near
    h0, qkv, ctx, h1, h2 = take(5)
    early, late, recv, kv, sems, pair_sems = take(6)
    here = Here(geo)
    beside = Beside(sems)
    names = ("ff1", "ff2", "embed", "self", "cross", "dff1", "dff2", "out")
    for name, source, target in zip(names, far, near):
        beside.start(name, source, target)
    barrier = pltpu.get_barrier_semaphore()
    pl.semaphore_signal(barrier, inc=1, device_id=here.device("c", 0), device_id_type=MESH)
    pl.semaphore_wait(barrier, 1)
    dims = (2 * geo.ny, geo.ns * geo.gf)
    pair = Pair(geo, here, early.reshape(*dims, plan.early_rows, 128), recv, early_out, pair_sems)
    at = plan.early_at
    spans_ = ((0, at[0], at[1]), (1, at[1], at[3]), (2, at[3], plan.early_rows))
    far_late = late_out.reshape(GROUPS, plan.late_rows, 128)

    def tick(name):
        if name == "encoder feed":
            beside.wait("ff1", "ff2")
        elif name == "decoder":
            for label, source, target in (("h0", h0, h0_out), ("qkv", qkv, qkv_out), ("ctx", ctx, ctx_out), ("h1", h1, h1_out),
                                          ("h2", h2, h2_out)):
                beside.start(label, source, target)
            beside.wait("embed")
        elif name in ("self", "cross"):
            beside.wait(name)
        elif name == "feed":
            beside.wait("dff1", "dff2")
        elif name == "head":
            beside.wait("out")
        elif name == "head back":
            pair.start(*spans_[0])
        elif name == "feed back":
            pair.start(*spans_[1])
            pair.finish(*spans_[0])
        elif name == "cross back":
            pair.start(*spans_[2])
            pair.finish(*spans_[1])
        elif name == "self back":
            pair.finish(*spans_[2])
        elif name.startswith("embed"):
            some = pl.ds(int(name[5:]) * (GROUPS // 4), GROUPS // 4)
            beside.start(name, late.at[some], far_late.at[some])

    enc_fwd_part(plan, tick, len_ref, bank, pe, w_sub, w_attn, w_ff1, w_ff2, gain, bias, h0, qkv, ctx, h1, h2, enc)
    dec_part(plan, utterances, tick, len_ref, count_ref, target_ref, pe_tok, enc, w_self, w_cross, d_ff1, d_ff2, embed, w_out,
             gain, bias, att, early, late, gg, gb, denc, kv)
    for span in spans_:
        pair.end(*span)
    beside.wait("h0", "qkv", "ctx", "h1", "h2", "embed0", "embed1", "embed2", "embed3")


def positions(length, width):
    place = np.arange(length, dtype=np.float64)[:, None]
    angles = place * np.exp(np.arange(0, width, 2, dtype=np.float64) * (-math.log(10000.0) / width))[None, :]
    return np.stack([np.sin(angles), np.cos(angles)], axis=-1).reshape(length, width).astype(np.float32)


def front(geo, n_bucket, utterances, filter_bank, frame_len, tok_len, targets, weights):
    (w_sub, enc_attn, enc_ff1, enc_ff2, dec_self, dec_cross, dec_ff1, dec_ff2, embed, ctc_head, out_head,
     norm_gain, norm_bias) = weights
    utts, frames, feat = filter_bank.shape
    toks, (vocab, d), ff = targets.shape[1], embed.shape, enc_ff1.shape[1]
    plan = Plan(utts, frames, n_bucket, toks, d, ff, vocab, feat)
    rows, drows = plan.rows, plan.drows
    bank = jnp.swapaxes(filter_bank, 1, 2)
    pe = positions(frames, d)
    pe_tok = np.tile(pe[:toks], (utts, 1))
    half = (geo.ny, geo.ns * geo.gf, plan.early_rows, 128)
    far = (enc_ff1, enc_ff2, embed, dec_self, dec_cross, dec_ff1, dec_ff2, out_head.T)
    kept = [shape(rows, d), shape(rows, 3 * d, dtype=BF), shape(rows, d, dtype=BF), shape(rows, d), shape(rows, d)]
    outs = kept + [shape(*half), shape(2 * geo.ny, geo.ns * geo.gf, plan.late_rows, 128)]
    outs += [shape(rows, d, dtype=BF), shape(8, 128), shape(8, d), shape(8, d), shape(rows, d)]
    h0, qkv, ctx, h1, h2, early, late, enc, att, gg_dec, gb_dec, denc = pl.pallas_call(
        functools.partial(front_kernel, geo, plan, utterances),
        out_shape=outs,
        in_specs=[SM] * 2 + [VM] * 8 + [ANY] * 8,
        out_specs=[ANY] * 7 + [VM] * 5,
        scratch_shapes=[pltpu.VMEM(x.shape, x.dtype) for x in far + tuple(kept)]
        + [pltpu.VMEM((GROUPS, plan.early_rows, 128), F32), pltpu.VMEM((GROUPS, plan.late_rows, 128), F32), pltpu.VMEM(half, F32),
           pltpu.VMEM((rows, 2 * d), BF), pltpu.SemaphoreType.DMA((17,)), pltpu.SemaphoreType.DMA((3, 3, geo.ny))],
        name="front",
        compiler_params=pltpu.CompilerParams(vmem_limit_bytes=VMEM_LIMIT, collective_id=1, has_side_effects=True),
    )(frame_len, tok_len, targets, bank, jnp.asarray(pe), jnp.asarray(pe_tok), w_sub, enc_attn, norm_gain, norm_bias, *far)
    per = feat // GROUPS
    perm = np.zeros((GROUPS * plan.sub_rows, feat), np.float32)
    for r in range(feat):
        perm[r // per * plan.sub_rows + r % per, r] = 1.0
    now = (frame_len, tok_len, targets, enc, ctc_head.T, denc, norm_gain, norm_bias, gg_dec, gb_dec, att)
    later = (bank, jnp.asarray(perm, BF), enc_attn, enc_ff1, enc_ff2, h0, qkv, ctx, h1, h2)
    ctc_scratch = [pltpu.VMEM((rows, 128), F32), pltpu.VMEM((frames, drows), F32), pltpu.VMEM((drows, d), F32)]
    ctc_scratch += [pltpu.VMEM((frames, drows), F32)] * 4 + [pltpu.VMEM((rows, drows), BF)] * 2
    enc_scratch = [pltpu.VMEM((rows, d), F32), pltpu.VMEM((rows, d), F32), pltpu.VMEM((rows, 3 * d), BF)]
    return plan, now, later, (early, late), ctc_scratch, enc_scratch


MESH = pl.DeviceIdType.MESH


class Geometry:
    def __init__(self, n_bucket, n_dp):
        self.ny, self.ns = n_bucket // 2, 4
        self.nf = n_dp // self.ns
        self.share = n_bucket * n_dp // GROUPS
        self.gf = self.nf // self.share
        if self.ny * 2 * self.ns * self.gf != GROUPS:
            raise ValueError("mesh size")

    def size(self, axis):
        return {"c": 2, "y": self.ny, "s": self.ns, "f": self.nf}[axis]


class Here:
    def __init__(self, geo):
        self.geo = geo
        bucket, dp = lax.axis_index("bucket"), lax.axis_index("dp")
        self.at = {"y": bucket // 2, "c": bucket % 2, "s": dp // geo.nf, "f": dp % geo.nf}

    def step(self, axis, p):
        return lax.rem(self.at[axis] + 1 + p, self.geo.size(axis))

    def device(self, axis, p):
        at = dict(self.at)
        at[axis] = self.step(axis, p)
        return (at["y"] * 2 + at["c"], at["s"] * self.geo.nf + at["f"])

    def greet(self):
        barrier = pltpu.get_barrier_semaphore()
        geo = self.geo
        bucket, dp = self.at["y"] * 2 + self.at["c"], self.at["s"] * geo.nf + self.at["f"]
        for p in range(geo.ns * geo.nf - 1):
            pl.semaphore_signal(barrier, inc=1, device_id=(bucket, lax.rem(dp + 1 + p, geo.ns * geo.nf)), device_id_type=MESH)
        for p in range(2 * geo.ny - 1):
            pl.semaphore_signal(barrier, inc=1, device_id=(lax.rem(bucket + 1 + p, 2 * geo.ny), dp), device_id_type=MESH)
        pl.semaphore_wait(barrier, geo.ns * geo.nf + 2 * geo.ny - 2)


class Stream:
    def __init__(self, geo, array, a, b, order, dtype, resident=False, paired=False):
        self.geo, self.array, self.a, self.n, self.order, self.dtype = geo, array, a, b - a, order, dtype
        self.resident, self.paired = resident, paired

    def wire(self, stage, n):
        geo = self.geo
        done = self.order[:stage]
        axis = self.order[stage]
        if axis == "c":
            return (geo.ny, geo.ns * geo.gf, n, 128)
        dims = [size for other, size in (("y", geo.ny), ("s", geo.ns), ("f", geo.gf)) if other not in done and other != axis]
        return tuple(dims) + (n, 128)

    def buffers(self, stage, n):
        if stage == 0:
            return [pltpu.VMEM(self.wire(0, n), F32)]
        return [pltpu.VMEM((self.geo.size(self.order[stage]) - 1,) + self.wire(stage, n), self.dtype)] * 2

    def own(self):
        geo = self.geo
        sems = [pltpu.SemaphoreType.DMA((3, geo.ny))]
        for stage in (1, 2, 3):
            sems += [pltpu.SemaphoreType.DMA((2, geo.size(self.order[stage]) - 1))]
        if self.resident:
            return sems
        return sems + [pltpu.VMEM((geo.ny, geo.ns * geo.gf, self.n, 128), F32)]

    def bind(self, here, g_refs, shared, own, r_ref, r_at):
        self.here, self.g, self.r, self.r_at = here, g_refs[self.array], r_ref, r_at
        rows = pl.ds(0, self.n)
        cut = [[ref.at[(slice(None),) * (len(ref.shape) - 2) + (rows,)] for ref in refs] for refs in shared]
        self.core = None if self.paired else cut[0][0]
        self.send = {stage: cut[stage][0] for stage in (1, 2, 3)}
        self.recv = {stage: cut[stage][1] for stage in (1, 2, 3)}
        self.sems = own[:4]
        self.sums = None if self.resident else own[4]

    def get(self, y, sf):
        if self.resident:
            return self.g[2 * y + self.here.at["c"], sf, self.a:self.a + self.n, :]
        return self.sums[y, sf]

    def put(self, y, sf, value):
        if self.resident:
            self.g[2 * y + self.here.at["c"], sf, self.a:self.a + self.n, :] = value
        else:
            self.sums[y, sf] = value

    def core_copies(self):
        geo, at, sems = self.geo, self.here.at, self.sems[0]
        span = pl.ds(self.a, self.n)
        if self.paired:
            return [pltpu.make_async_copy(self.g.at[y, :, span], self.sums.at[y], sems.at[2, y]) for y in range(geo.ny)]
        copies = [pltpu.make_async_remote_copy(
            src_ref=self.g.at[2 * y + 1 - at["c"], :, span], dst_ref=self.core.at[y],
            send_sem=sems.at[0, y], recv_sem=sems.at[1, y],
            device_id=self.here.device("c", 0), device_id_type=MESH) for y in range(geo.ny)]
        if not self.resident:
            copies += [pltpu.make_async_copy(self.g.at[2 * y + at["c"], :, span], self.sums.at[y], sems.at[2, y])
                       for y in range(geo.ny)]
        return copies

    def wire_copies(self, stage):
        axis, partners = self.order[stage], self.geo.size(self.order[stage]) - 1
        return [pltpu.make_async_remote_copy(
            src_ref=self.send[stage].at[p], dst_ref=self.recv[stage].at[partners - 1 - p],
            send_sem=self.sems[stage].at[0, p], recv_sem=self.sems[stage].at[1, partners - 1 - p],
            device_id=self.here.device(axis, p), device_id_type=MESH) for p in range(partners)]

    def blocks(self, stage):
        geo, at = self.geo, self.here.at
        done = self.order[:stage + 1]
        sizes = [1 if axis in done else size for axis, size in (("y", geo.ny), ("s", geo.ns), ("f", geo.gf))]

        def place(i, swap=None):
            f = i % sizes[2]
            s = i // sizes[2] % sizes[1]
            y = i // (sizes[2] * sizes[1])
            where = {"y": at["y"] if "y" in done else y, "s": at["s"] if "s" in done else s,
                     "f": (at["f"] if "f" in done else f) if geo.gf > 1 else 0}
            if swap is not None and not (swap[0] == "f" and geo.gf == 1):
                where[swap[0]] = swap[1]
            wire = tuple(v for axis, v in (("y", y), ("s", s), ("f", f)) if axis not in done)
            return (where["y"], where["s"] * geo.gf + where["f"]), wire

        return math.prod(sizes), place

    def start(self, stage):
        if stage == 0:
            for copy in self.core_copies():
                copy.start()
            return
        axis = self.order[stage]
        count, place = self.blocks(stage)
        for p, copy in enumerate(self.wire_copies(stage)):
            target = self.here.step(axis, p)

            def fill(i, carry, p=p, target=target):
                at, wire = place(i, (axis, target))
                self.send[stage][(p,) + wire] = self.get(*at).astype(self.dtype)
                return carry

            loop(count, fill)
            copy.start()

    def finish(self, stage):
        if stage == 0:
            for copy in self.core_copies():
                copy.wait()
            if self.paired:
                return
            geo = self.geo

            def add(i, carry):
                y, sf = i // (geo.ns * geo.gf), i % (geo.ns * geo.gf)
                self.put(y, sf, self.get(y, sf) + self.core[y, sf])
                return carry

            loop(geo.ny * geo.ns * geo.gf, add)
            return
        count, place = self.blocks(stage)
        copies = self.wire_copies(stage)
        for copy in copies:
            copy.wait()

        def add(i, carry):
            at, wire = place(i)
            total = self.get(*at)
            for p in range(len(copies)):
                total = total + self.recv[stage][(p,) + wire].astype(F32)
            if stage == 3:
                self.r[self.r_at:self.r_at + self.n, :] = total
            else:
                self.put(*at, total)
            return carry

        loop(count, add)


def loop(count, body):
    if count == 1:
        body(0, 0)
    else:
        lax.fori_loop(0, count, body, 0)


class Sum:
    SCRIPT = {
        "begin": (0, 1, 2, 3, 4, 5, 6), "first1": (0, 0, 1, 1, 2, 2, 3, 3, 5, 7), "first2": (4, 6), "first4": (7,),
        "prep": (0, 0, 1, 1, 4, 6), "scan2": (2, 2, 3, 3, 5), "scan4": (0, 0, 1, 1), "scan7": (4, 4, 6, 6, 7),
        "scan8": (0,), "scan9": (1, 2, 2, 3, 3), "scan10": (4, 4), "scan12": (5, 5), "scan13": (2,),
        "scan14": (3, 6, 6), "second0": (4, 5, 5), "second1": (6, 7, 7), "second3": (5,), "second4": (7, 7, 8, 9, 10),
        "ff0": (8, 8, 9, 9, 11), "ff1": (7, 10, 10, 12), "ff2": (8, 8, 11, 11), "ff3": (9, 9, 12, 12, 14, 15),
        "out": (8, 8, 10, 10), "attn1": (9, 9, 11, 11, 14, 14), "attn2": (8, 10, 10, 15, 15),
        "attn3": (9, 11, 11, 12, 12), "end": (10, 13, 14, 14, 16, 17),
        "drain": (11, 12, 12, 15, 15, 13, 13, 16, 16, 17, 17, 12, 14, 14, 15, 15, 13, 13, 17, 17, 16, 16, 14, 13, 13, 17, 17, 15, 16, 16, 13, 17, 16),
    }
    CUTS = (5, 3, 4, 2, 2)
    DEPTH = 2

    def __init__(self, geo, plan):
        self.geo = geo
        orders = ("cfys", "cyfs") if geo.share == 1 else ("cysf", "csyf")
        ff = 2 * plan.ff // 128 * (plan.width // GROUPS)
        self.streams = []

        def cut(array, a, b, count):
            size = (b - a) // count // 16 * 16
            for i in range(count):
                end = b if i == count - 1 else a + size
                self.streams.append(Stream(geo, array, a, end, orders[i % 2], BF, array > 1, array == 0))
                a = end

        early, late, ctc, enc, last = self.CUTS
        cut(0, 0, plan.early_rows, early)
        cut(1, 0, plan.late_rows, late)
        self.streams.append(Stream(geo, 2, 0, 16, orders[0], F32, True))
        cut(2, 16, plan.ctc_rows, ctc)
        self.streams.append(Stream(geo, 3, 0, 16, orders[0], F32, True))
        cut(3, 16, 16 + ff, enc)
        cut(3, 16 + ff, plan.enc_rows, last)
        steps = [0] * len(self.streams)
        self.pools = {}
        for name in self.SCRIPT:
            for i in self.SCRIPT[name]:
                if steps[i] % 2 == 0 and self.streams[i].dtype != F32 and not (steps[i] == 0 and self.streams[i].paired):
                    stage = steps[i] // 2
                    self.pools.setdefault((stage, self.streams[i].order if stage else "c"), []).append(i)
                steps[i] += 1
        if any(count != 8 for count in steps):
            raise ValueError("script")
        self.before, self.after, self.slot = {}, {}, {}
        for (stage, _), users in self.pools.items():
            for at, i in enumerate(users):
                self.slot[i, stage] = at % self.DEPTH
                if at >= self.DEPTH:
                    self.before[i, stage] = users[at - self.DEPTH]
                    self.after[users[at - self.DEPTH], stage] = i
        self.tall = max(stream.n for stream in self.streams)

    def scratch(self):
        out = [pltpu.SemaphoreType.REGULAR((len(self.streams), 4))]
        for stage, order in sorted(self.pools):
            stream = next(stream for stream in self.streams if order in ("c", stream.order))
            for _ in range(self.DEPTH):
                out += stream.buffers(stage, self.tall)
        for stream in self.streams:
            out += stream.own()
            if stream.dtype == F32:
                for stage in range(4):
                    out += stream.buffers(stage, stream.n)
        return out

    def bind(self, here, arrays, refs, r_ref, bases):
        refs = list(refs)
        self.here, self.free = here, refs.pop(0)

        def take(count):
            out = refs[:count]
            del refs[:count]
            return out

        sets = {key: [take(2 if key[0] else 1) for _ in range(self.DEPTH)] for key in sorted(self.pools)}
        for i, stream in enumerate(self.streams):
            own = take(4 if stream.resident else 5)
            if stream.dtype == F32:
                buffers = [take(2 if stage else 1) for stage in range(4)]
            else:
                buffers = [sets[stage, stream.order if stage else "c"][self.slot[i, stage]] if (i, stage) in self.slot else []
                           for stage in range(4)]
            stream.bind(here, arrays, buffers, own, r_ref, bases[stream.array] + stream.a)
        self.steps = [0] * len(self.streams)

    def tick(self, name):
        for i in self.SCRIPT.get(name, ()):
            stage, ending = divmod(self.steps[i], 2)
            self.steps[i] += 1
            stream = self.streams[i]
            partners = self.geo.size(stream.order[stage]) - 1
            if ending:
                stream.finish(stage)
                if (i, stage) in self.after:
                    for p in range(partners):
                        pl.semaphore_signal(self.free.at[self.after[i, stage], stage], inc=1,
                                            device_id=self.here.device(stream.order[stage], p), device_id_type=MESH)
            else:
                if (i, stage) in self.before:
                    pl.semaphore_wait(self.free.at[i, stage], partners)
                stream.start(stage)


class Layout:
    def __init__(self, plan, geo, sizes):
        self.plan, self.share = plan, geo.share
        self.widths = [size // GROUPS // geo.share for size in sizes]
        self.starts = [int(x) for x in np.cumsum([0] + self.widths)]
        self.part = self.starts[-1]
        self.lines = -(-self.part // 1024) * 8
        self.base_late = plan.early_rows
        self.base_ctc = self.base_late + plan.late_rows
        self.base_enc = self.base_ctc + plan.ctc_rows
        self.rows = self.base_enc + plan.enc_rows
        d, deep = plan.width, plan.width // GROUPS
        e, c = [self.base_enc + x for x in plan.enc_at], plan.early_at
        at_self, at_embed = [self.base_late + x for x in plan.late_at]
        long = plan.ff // GROUPS
        attn, ff, two = 4 * d // 128, plan.ff // 128, d // 128
        self.place = [(e[3], plan.sub_rows, two), (e[2], deep, attn), (e[1], deep, ff), (e[0], long, two),
                      (at_self, deep, attn), (c[3], deep, attn), (c[1], deep, ff), (c[2], long, two),
                      (at_embed, plan.embed_rows, two), (self.base_ctc, deep, plan.out_rows // deep), (c[0], deep, plan.out_rows // deep)]

    def tile(self, weight, c):
        base, deep, _ = self.place[weight]
        return base + deep * c + (deep if weight == 9 and c > 0 else 0)

    def in_xla(self, r, bucket, dp, n_dp):
        index = bucket * n_dp + dp
        group, within = index // self.share, index % self.share
        pieces = []
        for weight, width in enumerate(self.widths):
            if weight >= 11:
                line, at = r[self.base_enc + weight - 11], 0
            else:
                _, deep, tiles = self.place[weight]
                block = jnp.concatenate([r[self.tile(weight, c):self.tile(weight, c) + deep] for c in range(tiles)], axis=1)
                if weight in (9, 10):
                    block = block[:, : self.plan.vocab]
                line, at = block.reshape(-1), 0
                if weight == 8:
                    at = group * (width * self.share) % self.plan.width
            pieces.append(lax.dynamic_slice(line, (at + within * width,), (width,)))
        flat = jnp.concatenate(pieces)
        return jnp.pad(flat, (0, self.lines * 128 - self.part)).reshape(self.lines, 128)

    def in_kernel(self, r, flat, work, group):
        flat[self.lines - 8:, :] = jnp.zeros((8, 128), F32)
        lane = iota((1, 128), 1)

        def put(value, base, length):
            lines, row, shift = -(-length // 128), base // 128, base % 128
            value = value[:lines]
            if shift == 0 and length % 128 == 0:
                flat[row:row + lines, :] = value
                return
            moved = pltpu.roll(value, shift, 1) if shift else value
            number = 128 * iota((lines, 128), 0) + (lane - shift) % 128
            right = (lane >= shift) & (number < length)
            flat[row:row + lines, :] = jnp.where(right, moved, flat[row:row + lines, :])
            if shift:
                left = (lane < shift) & (number < length)
                flat[row + 1:row + 1 + lines, :] = jnp.where(left, moved, flat[row + 1:row + 1 + lines, :])

        for weight, width in enumerate(self.widths):
            base = self.starts[weight]
            if weight >= 11:
                put(r[self.base_enc + weight - 11:self.base_enc + weight - 10, :], base, width)
                continue
            _, deep, tiles = self.place[weight]
            if weight == 8:
                for c in range(tiles):
                    at = self.tile(weight, c)
                    work[pl.ds(c, deep, stride=tiles), :] = r[at:at + deep, :]
                offset = lax.rem(group * width, self.plan.width)
                need = -(-width // 128)
                value = jnp.where(offset >= 128, work[1:need + 2, :], work[0:need + 1, :])
                turned = pltpu.roll(value, 64, 1)
                after = jnp.where(lane < 64, turned[:need], turned[1:])
                put(jnp.where(lax.rem(offset, 128) >= 64, after, value[:need]), base, width)
            elif weight in (9, 10):
                for c in range(tiles):
                    at = self.tile(weight, c)
                    work[pl.ds(c, deep, stride=tiles), :] = r[at:at + deep, :]
                for i in range(deep):
                    put(work[tiles * i:tiles * (i + 1), :], base + self.plan.vocab * i, self.plan.vocab)
            else:
                count = width // 128 // tiles
                for c in range(tiles):
                    at = self.tile(weight, c)
                    flat[pl.ds(base // 128 + c, count, stride=tiles), :] = r[at:at + count, :]


def tail_kernel(geo, plan, layout, total, utterances, counts, *refs):
    fused = geo.share == 1
    refs = list(refs)

    def take(count):
        out = refs[:count]
        del refs[:count]
        return out

    len_ref, count_ref, target_ref, enc, head, denc_in, gain, bias, gg_dec, gb_dec, att = take(11)
    far = take(13 if fused else 10)
    g_early, g_late = take(2)
    out_ref, info_ref = take(2)
    near = take(len(far))
    sems, g_ctc, g_enc, denc = take(4)
    ctc_scratch, enc_scratch = take(counts[0]), take(counts[1])
    fused_scratch = take(counts[2])
    bank, perm, w_attn, w_ff1, w_ff2, h0, qkv, ctx, h1, h2 = near[:10]
    optimizer = near[10:]
    here = Here(geo)
    r_ref = fused_scratch[0] if fused else out_ref
    dims = (2 * geo.ny, geo.ns * geo.gf)
    total.bind(here, (g_early, g_late, g_ctc.reshape(*dims, plan.ctc_rows, 128), g_enc.reshape(*dims, plan.enc_rows, 128)), refs,
               r_ref, (0, layout.base_late, layout.base_ctc, layout.base_enc))
    here.greet()
    total.tick("begin")
    beside = Beside(sems)
    for i, (source, target) in enumerate(zip(far, near)):
        beside.start(i, source, target)
    loss = ctc_part(plan, utterances, total.tick, len_ref, count_ref, target_ref, enc, head, denc_in, g_ctc, denc, *ctc_scratch)
    beside.wait(*range(len(far)))
    enc_bwd_part(plan, total.tick, len_ref, bank, perm, w_attn, w_ff1, w_ff2, gain, bias, h0, qkv, ctx, h1, h2, denc,
                 gg_dec, gb_dec, g_enc, *enc_scratch)
    if fused:
        weight_squares = square_sums(layout, optimizer, fused_scratch)
    total.tick("end")
    total.tick("drain")
    row = jnp.zeros((1, 128), F32) + (loss + att[0:1, :])
    if fused:
        group = ((here.at["y"] * 2 + here.at["c"]) * geo.ns + here.at["s"]) * geo.gf + here.at["f"]
        layout.in_kernel(r_ref, out_ref, fused_scratch[1], group)
        norms(geo, layout, here, out_ref, weight_squares, row, info_ref, fused_scratch)
    else:
        info_ref[0:1, :] = row
        info_ref[1:2, :] = row


def tail(geo, plan, layout, utterances, now, later, summed, ctc_scratch, enc_scratch, optimizer):
    fused = geo.share == 1
    total = Sum(geo, plan)
    extra = norm_scratch(geo, plan, layout) if fused else []
    later = later + (tuple(optimizer) if fused else ())
    scratch = [pltpu.VMEM(x.shape, x.dtype) for x in later]
    scratch += [pltpu.SemaphoreType.DMA((len(later),)), pltpu.VMEM((GROUPS, plan.ctc_rows, 128), F32),
                pltpu.VMEM((GROUPS, plan.enc_rows, 128), F32), pltpu.VMEM((plan.rows, plan.width), F32)]
    scratch += ctc_scratch + enc_scratch + extra + total.scratch()
    lines = layout.lines if fused else layout.rows
    return pl.pallas_call(
        functools.partial(tail_kernel, geo, plan, layout, total, utterances, (len(ctc_scratch), len(enc_scratch), len(extra))),
        out_shape=[shape(lines, 128), shape(8, 128)],
        in_specs=[SM] * 2 + [VM] * (len(now) - 2) + [ANY] * (len(later) + 2),
        out_specs=[VM] * 2,
        scratch_shapes=scratch,
        name="tail",
        compiler_params=pltpu.CompilerParams(vmem_limit_bytes=VMEM_LIMIT, collective_id=0, has_side_effects=True),
    )(*now, *later, *summed)


def share_sum(here, row, block, recv, sems, at):
    geo = here.geo
    me = {"dp": here.at["s"] * geo.nf + here.at["f"], "bucket": here.at["y"] * 2 + here.at["c"]}
    for axis, size in (("dp", geo.ns * geo.nf), ("bucket", 2 * geo.ny)):
        own = me[axis]
        block[at] = jnp.broadcast_to(row, (8, 128))
        recv[at + own] = block[at]

        def copy(p, sender, at=at, axis=axis, size=size, own=own):
            other = lax.rem(own + 1 + p, size)
            device = (me["bucket"], other) if axis == "dp" else (other, me["dp"])
            slot = own if sender else other
            return pltpu.make_async_remote_copy(
                src_ref=block.at[at], dst_ref=recv.at[at + slot], send_sem=sems.at[0, at + p], recv_sem=sems.at[1, at + slot],
                device_id=device, device_id_type=MESH)

        for p in range(size - 1):
            copy(p, True).start()
        for p in range(size - 1):
            copy(p, False).wait_recv()
        for p in range(size - 1):
            copy(p, True).wait_send()
        total = recv[at, 0:1, :]
        for i in range(1, size):
            total = total + recv[at + i, 0:1, :]
        row = total
        at += size
    return row, at


def edges(layout):
    full = layout.part // 128
    return full, layout.part - full * 128


def load_flat(layout, source, target):
    full, edge = edges(layout)
    target[0:full, :] = source[pl.ds(0, full * 128)].reshape(full, 128)
    if edge:
        target[full:full + 1, :] = jnp.zeros((1, 128), F32)
        target[full:full + 1, 0:edge] = source[pl.ds(full * 128, edge)].reshape(1, edge)


def store_flat(layout, target, value):
    full, edge = edges(layout)
    target[pl.ds(0, full * 128)] = value[0:full, :].reshape(full * 128).astype(target.dtype)
    if edge:
        target[pl.ds(full * 128, edge)] = value[full:full + 1, 0:edge].reshape(edge).astype(target.dtype)


def pieces(layout, m):
    lo, hi = layout.starts[m], layout.starts[m + 1]
    shared = []
    for at in sorted({lo // 128, hi // 128}):
        left, right = max(lo, at * 128) - at * 128, min(hi, at * 128 + 128) - at * 128
        if left < right and not (left == 0 and right == 128):
            shared.append((at, left, right))
    return (-(-lo // 128), hi // 128), shared


def matrix_sums(layout, ref):
    lane = iota((1, 128), 1)
    out = jnp.zeros((1, 128), F32)
    for m in range(len(layout.widths)):
        (r0, r1), shared = pieces(layout, m)
        total = jnp.zeros((1, 128), F32)
        if r1 > r0:
            total = total + jnp.sum(ref[r0:r1, :], axis=0, keepdims=True)
        for at, left, right in shared:
            total = total + jnp.where((lane >= left) & (lane < right), ref[at:at + 1, :], 0.0)
        out = jnp.where(lane == m, jnp.sum(total, axis=1, keepdims=True), out)
    return out


def norm_scratch(geo, plan, layout):
    slots = 2 * (2 * geo.ny + geo.ns * geo.nf)
    flat = pltpu.VMEM((layout.lines, 128), F32)
    return [pltpu.VMEM((layout.rows, 128), F32), pltpu.VMEM((plan.embed_rows * plan.width // 128, 128), F32), flat, flat, flat, flat,
            pltpu.VMEM((slots, 8, 128), F32), pltpu.VMEM((slots, 8, 128), F32), pltpu.SemaphoreType.DMA((2, slots))]


def square_sums(layout, optimizer, scratch):
    w, a, b, sq = scratch[2:6]
    lines = sum(1 if x else 0 for x in edges(layout)[1:]) + edges(layout)[0]
    for source, target in zip(optimizer, (w, a, b)):
        load_flat(layout, source, target)
    sq[0:lines, :] = w[0:lines, :] * w[0:lines, :]
    return matrix_sums(layout, sq)


def adam(g, clip, w, a, b):
    scaled = g * jnp.minimum(1.0, 1.0 / clip)
    first = 0.5 * a + 0.5 * scaled
    second = 0.5 * b + 0.5 * scaled * scaled
    correct = 1.0 - 0.5**STEP
    return first, second, first / correct / (jnp.sqrt(second / correct) + 1e-06) + 0.01 * w


def norms(geo, layout, here, g_ref, weight_squares, loss, info_ref, scratch):
    w, a, b, sq, block, recv, sems = scratch[2:9]
    full, edge = edges(layout)
    lines = full + (1 if edge else 0)
    lane = iota((1, 128), 1)
    g = g_ref[0:lines, :]
    squares = jnp.sum(jnp.sum(g * g, axis=0, keepdims=True), axis=1, keepdims=True)
    row = jnp.where(lane == 120, squares, jnp.where(lane == 121, loss, weight_squares))
    row, at = share_sum(here, row, block, recv, sems, 0)
    info_ref[0:1, :] = row
    clip = jnp.sqrt(jnp.sum(jnp.where(lane == 120, row, 0.0), axis=1, keepdims=True))
    _, _, direction = adam(g, clip, w[0:lines, :], a[0:lines, :], b[0:lines, :])
    sq[0:lines, :] = direction * direction
    row, _ = share_sum(here, matrix_sums(layout, sq), block, recv, sems, at)
    info_ref[1:2, :] = row


def norm_kernel(geo, layout, g_ref, master, moment1, moment2, loss_ref, info_ref, *scratch):
    here = Here(geo)
    here.greet()
    weight_squares = square_sums(layout, (master, moment1, moment2), scratch)
    norms(geo, layout, here, g_ref, weight_squares, loss_ref[0:1, :], info_ref, scratch)


def update_kernel(layout, utterances, g_ref, master, moment1, moment2, info_ref,
                  loss_ref, clip_ref, first_ref, second_ref, fresh_ref, low_ref, wn_ref, un_ref, w, a, b):
    full, edge = edges(layout)
    lines, count = full + (1 if edge else 0), len(layout.widths)
    lane = iota((1, 128), 1)
    for source, target in ((master, w), (moment1, a), (moment2, b)):
        load_flat(layout, source, target)
    row = info_ref[0:1, :]
    clip = jnp.sqrt(jnp.sum(jnp.where(lane == 120, row, 0.0), axis=1, keepdims=True))
    loss_ref[0] = jnp.sum(jnp.where(lane == 121, row, 0.0)) / utterances
    clip_ref[0] = jnp.sum(clip)
    weight_norms, update_norms = jnp.sqrt(row), jnp.sqrt(info_ref[1:2, :])
    wn_ref[...] = weight_norms[:, 0:count].reshape(count)
    un_ref[...] = update_norms[:, 0:count].reshape(count)
    ratio = 0.5 * weight_norms / update_norms
    first, second, direction = adam(g_ref[0:lines, :], clip, w[0:lines, :], a[0:lines, :], b[0:lines, :])
    store_flat(layout, first_ref, first)
    store_flat(layout, second_ref, second)
    a[0:lines, :] = direction
    for m in range(count):
        scale = jnp.sum(jnp.where(lane == m, ratio, 0.0), axis=1, keepdims=True)
        (r0, r1), shared = pieces(layout, m)
        if r1 > r0:
            w[r0:r1, :] -= scale * a[r0:r1, :]
        for at, left, right in shared:
            w[at:at + 1, :] -= jnp.where((lane >= left) & (lane < right), scale * a[at:at + 1, :], 0.0)
    fresh = w[0:lines, :]
    store_flat(layout, fresh_ref, fresh)
    store_flat(layout, low_ref, fresh)


def update(layout, utterances, g, optimizer, info):
    part, lines, count = layout.part, layout.lines, len(layout.widths)
    loss, clip, *rest = pl.pallas_call(
        functools.partial(update_kernel, layout, utterances),
        out_shape=[shape(1), shape(1), shape(part), shape(part), shape(part), shape(part, dtype=BF), shape(count), shape(count)],
        in_specs=[VM] * 5,
        out_specs=[SM, SM] + [VM] * 6,
        scratch_shapes=[pltpu.VMEM((lines, 128), F32)] * 3,
        name="update",
        compiler_params=pltpu.CompilerParams(vmem_limit_bytes=VMEM_LIMIT),
    )(g, *optimizer, info)
    return (loss[0], clip[0], *rest)


def solution(mesh):
    n_bucket, n_dp = mesh.shape["bucket"], mesh.shape["dp"]
    geo = Geometry(n_bucket, n_dp)

    def body(filter_bank, frame_len, tok_len, targets, *rest):
        weights, optimizer = rest[:13], rest[13:]
        utterances = frame_len.shape[0] * n_bucket * n_dp
        plan, *rest = front(geo, n_bucket, utterances, filter_bank, frame_len, tok_len, targets, weights)
        layout = Layout(plan, geo, [w.size for w in weights])
        out, info = tail(geo, plan, layout, utterances, *rest, optimizer)
        if geo.share == 1:
            return update(layout, utterances, out, optimizer, info)
        g = layout.in_xla(out, lax.axis_index("bucket"), lax.axis_index("dp"), n_dp)
        info = pl.pallas_call(
            functools.partial(norm_kernel, geo, layout),
            out_shape=shape(8, 128), in_specs=[VM] * 5, out_specs=VM, scratch_shapes=norm_scratch(geo, plan, layout), name="norms",
            compiler_params=pltpu.CompilerParams(vmem_limit_bytes=VMEM_LIMIT, collective_id=2, has_side_effects=True),
        )(g, *optimizer, info)
        return update(layout, utterances, g, optimizer, info)

    both = P(("bucket", "dp"))
    in_specs = (P(("bucket", "dp"), None, None), both, both, P(("bucket", "dp"), None)) + (P(),) * 13 + (both,) * 3
    out_specs = (P(), P(), both, both, both, both, P(), P())
    return jax.shard_map(body, mesh=mesh, in_specs=in_specs, out_specs=out_specs, check_vma=False)
```

```python
import functools
import math

import jax
import jax.numpy as jnp
import numpy as np
from jax import lax
from jax.experimental import pallas as pl
from jax.experimental.pallas import tpu as pltpu
from jax.sharding import PartitionSpec as P

HEADS = 4
STEP = 5
GROUPS = 32
BF = jnp.bfloat16
F32 = jnp.float32
NEG_SCORE = -1e9
NEG_PATH = -1e5
FLOOR = -1e30
LOG2E = 1.4426950408889634
VMEM_LIMIT = 63 * 2**20


def dot(a, b):
    return lax.dot_general(a, b, (((1,), (0,)), ((), ())), preferred_element_type=F32)


def dot_rt(a, b):
    return lax.dot_general(a, b, (((1,), (1,)), ((), ())), preferred_element_type=F32)


def dot_lt(a, b):
    return lax.dot_general(a, b, (((0,), (0,)), ((), ())), preferred_element_type=F32)


def halves(value):
    high = value.astype(BF)
    return high, (value - high.astype(F32)).astype(BF)


def iota(shape, dim):
    return lax.broadcasted_iota(jnp.int32, shape, dim)


def normalised(x):
    mean = jnp.mean(x, axis=-1, keepdims=True)
    centre = x - mean
    rstd = lax.rsqrt(jnp.mean(centre * centre, axis=-1, keepdims=True) + 1e-05)
    return centre * rstd, rstd


def norm_back(dy, unit, rstd, gain):
    dunit = dy * gain
    dx = rstd * (
        dunit
        - jnp.mean(dunit, axis=-1, keepdims=True)
        - unit * jnp.mean(dunit * unit, axis=-1, keepdims=True)
    )
    return dx, jnp.sum(dy * unit, axis=0, keepdims=True), jnp.sum(dy, axis=0, keepdims=True)


def softmax(scores):
    shifted = scores - jnp.max(scores, axis=-1, keepdims=True)
    e = jnp.exp(shifted)
    return e * (1.0 / jnp.sum(e, axis=-1, keepdims=True))


def head_mask(width, h):
    size = width // HEADS
    lane = iota((1, width), 1)
    return (lane >= h * size) & (lane < (h + 1) * size)


def pick_head(value, h):
    return jnp.where(head_mask(value.shape[-1], h), value, jnp.zeros((), value.dtype))


def attend(q, k, v, allowed):
    scale = 1.0 / math.sqrt(q.shape[-1] // HEADS)
    total = None
    for h in range(HEADS):
        s = jnp.where(allowed, dot_rt(q, pick_head(k, h)) * scale, NEG_SCORE)
        c = dot(softmax(s).astype(BF), pick_head(v, h))
        total = c if total is None else total + c
    return total


def attend_back(q, k, v, allowed, dctx):
    scale = 1.0 / math.sqrt(q.shape[-1] // HEADS)
    dq = dk = dv = None
    for h in range(HEADS):
        kh, vh = pick_head(k, h), pick_head(v, h)
        p = softmax(jnp.where(allowed, dot_rt(q, kh) * scale, NEG_SCORE))
        dvh = dot_lt(p.astype(BF), pick_head(dctx, h))
        dp = dot_rt(dctx, vh)
        ds = p * (dp - jnp.sum(p * dp, axis=-1, keepdims=True))
        ds = jnp.where(allowed, ds, 0.0).astype(BF)
        dqh = dot(ds, kh)
        dkh = dot_lt(ds, pick_head(q, h))
        if dq is None:
            dq, dk, dv = dqh, dkh, dvh
        else:
            dq, dk, dv = dq + dqh, dk + dkh, dv + dvh
    return dq * scale, dk * scale, dv


def spans(total, size):
    return [(at, min(size, total - at)) for at in range(0, total, size)]


def put8(ref, base, value, first=0):
    rows, width = value.shape
    deep = rows // GROUPS
    if width % 128:
        value = jnp.pad(value, ((0, 0), (0, 128 - width % 128)))
    for c in range(first, value.shape[1] // 128):
        at = base + deep * c
        ref[:, at:at + deep, :] = value[:, 128 * c:128 * (c + 1)].reshape(GROUPS, deep, 128)


def put_rows(ref, base, value, row, rows):
    deep = rows // GROUPS
    count = value.shape[0] // deep
    for c in range(value.shape[1] // 128):
        at = base + deep * c
        ref[row // deep:row // deep + count, at:at + deep, :] = value[:, 128 * c:128 * (c + 1)].reshape(count, deep, 128)


def put_small(ref, row, value):
    width = value.shape[1]
    part = 7 * width // GROUPS
    line = jnp.concatenate([value[i:i + 1, :] for i in range(8)], axis=1)
    for q in range(GROUPS):
        ref[q, row:row + 1, :] = line[:, part * q:part * q + 128]


def token_line(ref):
    return jnp.concatenate([ref[u:u + 1, :] for u in range(ref.shape[0])], axis=1)


def scalar_line(plan, ref):
    owner = iota((1, plan.drows), 1) // plan.tokens
    line = jnp.zeros((1, plan.drows), jnp.int32)
    for u in range(plan.utts):
        line = jnp.where(owner == u, ref[u], line)
    return line


def columns(lines):
    n = lines[0].shape[1]
    block = jnp.concatenate(lines + [jnp.zeros((8 - len(lines), n), lines[0].dtype)], axis=0)
    turned = block.T
    return [turned[:, i:i + 1] for i in range(len(lines))]


class Plan:
    def __init__(self, utts, frames, n_bucket, tokens, width, ff, vocab, feat):
        self.utts, self.frames, self.tokens = utts, frames, tokens
        self.width, self.ff, self.vocab = width, ff, vocab
        if utts % n_bucket == 0:
            self.caps = [frames * (i % n_bucket + 1) // n_bucket for i in range(utts)]
        else:
            self.caps = [frames] * utts
        self.starts = [sum(self.caps[:i]) for i in range(utts)]
        self.rows = sum(self.caps)
        self.drows = utts * tokens
        self.chunk = 1024 if self.rows <= 768 else 512
        self.embed_rows = -(-(vocab // GROUPS + 2) // 16) * 16
        tiles = -(-vocab // 128)
        deep = width // GROUPS
        self.out_rows = tiles * deep
        attn, ff = 4 * width // 128 * deep, ff // 128 * deep
        embed = self.embed_rows * width // 128
        ends = np.cumsum([0, ff, ff, attn, attn])
        self.dec_at, self.dec_rows = [int(x) for x in ends[:-1]], int(ends[-1])
        self.embed_lines = embed
        self.ctc_rows = (tiles + 2) * deep
        self.sub_rows = -(-(feat // GROUPS) // 8) * 8
        ends = np.cumsum([16, ff, ff, attn, self.sub_rows * width // 128])
        self.enc_at, self.enc_rows = [int(x) for x in ends[:-1]], int(ends[-1])


def enc_fwd_part(plan, tick, len_ref, fb_ref, pe_ref, w_sub, w_attn, w_ff1, w_ff2, gain, bias,
                   h0_ref, qkv_ref, ctx_ref, h1_ref, h2_ref, enc_ref):
    d = plan.width
    gain, bias = gain[...].astype(F32), bias[...].astype(F32)
    for u in range(plan.utts):
        t, at = plan.caps[u], plan.starts[u]
        h0_ref[at:at + t, :] = dot_lt(fb_ref[u, :, 0:t], w_sub[...]) + pe_ref[0:t, :]
    unit, _ = normalised(h0_ref[...])
    a0 = (unit * gain[0:1, :] + bias[0:1, :]).astype(BF)
    qkv_ref[...] = dot(a0, w_attn[:, : 3 * d]).astype(BF)
    for u in range(plan.utts):
        t, at = plan.caps[u], plan.starts[u]
        allowed = iota((1, t), 1) < len_ref[u]
        piece = qkv_ref[at:at + t, :]
        ctx = attend(piece[:, :d], piece[:, d:2 * d], piece[:, 2 * d:], allowed)
        ctx_ref[at:at + t, :] = ctx.astype(BF)
    h1 = h0_ref[...] + dot(ctx_ref[...], w_attn[:, 3 * d:])
    h1_ref[...] = h1
    tick("encoder feed")
    unit, _ = normalised(h1)
    a1 = (unit * gain[1:2, :] + bias[1:2, :]).astype(BF)
    h2_ref[...] = h1
    for c, size in spans(plan.ff, plan.chunk // 2):
        inner = dot(a1, w_ff1[:, c:c + size])
        act = (inner * jax.nn.sigmoid(inner)).astype(BF)
        h2_ref[...] += dot(act, w_ff2[c:c + size, :])
    unit, _ = normalised(h2_ref[...])
    enc_ref[...] = (unit * gain[2:3, :] + bias[2:3, :]).astype(BF)


def enc_bwd_part(plan, tick, len_ref, fb_ref, perm_ref, w_attn, w_ff1, w_ff2, gain, bias,
                   h0_ref, qkv_ref, ctx_ref, h1_ref, h2_ref, denc_ref,
                   gg_dec, gb_dec, g_ref, dh_ref, db_ref, dqkv_ref):
    gain, bias = gain[...].astype(F32), bias[...].astype(F32)
    d, deep = plan.width, plan.width // GROUPS
    at_ff2, at_ff1, at_attn, at_sub = plan.enc_at
    g_ref[:, 0:16, :] = jnp.zeros((GROUPS, 16, 128), F32)
    denc = denc_ref[...].astype(BF).astype(F32)
    unit, rstd = normalised(h2_ref[...])
    dh2, gg2, gb2 = norm_back(denc, unit, rstd, gain[2:3, :])
    dh_ref[...] = dh2
    dout = dh2.astype(BF)
    unit1, rstd1 = normalised(h1_ref[...])
    a1 = (unit1 * gain[1:2, :] + bias[1:2, :]).astype(BF)
    for c, size in spans(plan.ff, plan.chunk // 2):
        inner = dot(a1, w_ff1[:, c:c + size])
        sig = jax.nn.sigmoid(inner)
        act = inner * sig
        put_rows(g_ref, at_ff2, dot_lt(act.astype(BF), dout), c, plan.ff)
        dact = dot_rt(dout, w_ff2[c:c + size, :])
        dinner = (dact * (sig + act * (1.0 - sig))).astype(BF)
        put8(g_ref, at_ff1 + c // 128 * deep, dot_lt(a1, dinner))
        part = dot_rt(dinner, w_ff1[:, c:c + size])
        if c == 0:
            db_ref[...] = part
        else:
            db_ref[...] += part
        if c % 512 == 0:
            tick("ff%d" % (c // 512))
    dx, gg1, gb1 = norm_back(db_ref[...], unit1, rstd1, gain[1:2, :])
    dh1 = dh_ref[...] + dx
    dh_ref[...] = dh1
    dout = dh1.astype(BF)
    put8(g_ref, at_attn + 3 * d // 128 * deep, dot_lt(ctx_ref[...], dout))
    dctx = dot_rt(dout, w_attn[:, 3 * d:]).astype(BF)
    tick("out")
    for u in range(plan.utts):
        t, at = plan.caps[u], plan.starts[u]
        allowed = iota((1, t), 1) < len_ref[u]
        piece = qkv_ref[at:at + t, :]
        dq, dk, dv = attend_back(piece[:, :d], piece[:, d:2 * d], piece[:, 2 * d:], allowed, dctx[at:at + t, :])
        dqkv_ref[at:at + t, :d] = dq.astype(BF)
        dqkv_ref[at:at + t, d:2 * d] = dk.astype(BF)
        dqkv_ref[at:at + t, 2 * d:] = dv.astype(BF)
        tick("attn%d" % u)
    unit, rstd = normalised(h0_ref[...])
    a0 = (unit * gain[0:1, :] + bias[0:1, :]).astype(BF)
    dqkv = dqkv_ref[...]
    put8(g_ref, at_attn, dot_lt(a0, dqkv))
    da0 = dot_rt(dqkv, w_attn[:, :3 * d])
    dx, gg0, gb0 = norm_back(da0, unit, rstd, gain[0:1, :])
    dh0 = (dh_ref[...] + dx).astype(BF)
    g = None
    for u in range(plan.utts):
        t, at = plan.caps[u], plan.starts[u]
        part = dot(fb_ref[u, :, 0:t], dh0[at:at + t, :])
        g = part if g is None else g + part
    high, low = halves(g)
    lower = (g - high.astype(F32) - low.astype(F32)).astype(BF)
    perm = perm_ref[...]
    put_rows(g_ref, at_sub, dot(perm, high) + dot(perm, low) + dot(perm, lower), 0, perm.shape[0])
    put_small(g_ref, 0, gg_dec[...] + jnp.concatenate([gg0, gg1, gg2, jnp.zeros((5, d), F32)], axis=0))
    put_small(g_ref, 1, gb_dec[...] + jnp.concatenate([gb0, gb1, gb2, jnp.zeros((5, d), F32)], axis=0))


def source_masks(plan, len_ref):
    rows = plan.drows
    row, col = iota((rows, rows), 0), iota((rows, rows), 1)
    causal = (row // plan.tokens == col // plan.tokens) & (col <= row)
    owner = iota((rows, 1), 0) // plan.tokens
    frame = iota((1, plan.rows), 1)
    valid = None
    for u in range(plan.utts):
        here = (owner == u) & (frame >= plan.starts[u]) & (frame < plan.starts[u] + len_ref[u])
        valid = here if valid is None else valid | here
    return causal, valid


def input_tokens(plan, target_ref):
    spot = iota((1, plan.drows), 1) % plan.tokens
    return jnp.where(spot == 0, plan.vocab - 1, pltpu.roll(token_line(target_ref), 1, 1))


def keep_shapes(plan):
    line, d = plan.drows, plan.width
    return [shape(line, d)] * 4 + [shape(line, 3 * d, dtype=BF)] + [shape(line, d, dtype=BF)] * 3 + [shape(plan.rows, 2 * d, dtype=BF)]


def dec_fwd_part(plan, utterances, tick, len_ref, count_ref, target_ref, pe_ref, enc_ref, w_self, w_cross, w_ff1,
                 w_ff2, embed, w_out, gain, bias, loss_ref, g_ref, g_gain, g_bias, keep):
    y0_ref, y1_ref, y2_ref, dy_ref, mixed_ref, ctx_ref, cctx_ref, cq_ref, kv_ref = keep
    d, rows, vocab = plan.width, plan.drows, plan.vocab
    deep = d // GROUPS
    gain, bias = gain[...].astype(F32), bias[...].astype(F32)
    line, counts = token_line(target_ref), scalar_line(plan, count_ref)
    spot = iota((1, rows), 1) % plan.tokens
    toks = input_tokens(plan, target_ref)
    tick("decoder")
    tok, want, live = columns([toks, jnp.where(spot == counts, vocab - 1, line), jnp.where(spot <= counts, 1, 0)])
    live = live.astype(F32)
    chunks = spans(vocab, 1024)
    place = iota((1, 1024), 1)
    y = None
    for c, size in chunks:
        hot = jnp.where(tok == place[:, :size] + c, 1.0, 0.0).astype(BF)
        part = dot(hot, embed[c:c + size, :])
        y = part if y is None else y + part
    y0 = y * math.sqrt(d) + pe_ref[...]
    y0_ref[...] = y0
    causal, valid = source_masks(plan, len_ref)
    tick("self")
    unit3, rstd3 = normalised(y0)
    a3 = (unit3 * gain[3:4, :] + bias[3:4, :]).astype(BF)
    mixed = dot(a3, w_self[:, : 3 * d]).astype(BF)
    mixed_ref[...] = mixed
    q, k, v = mixed[:, :d], mixed[:, d:2 * d], mixed[:, 2 * d:]
    ctx = attend(q, k, v, causal).astype(BF)
    ctx_ref[...] = ctx
    y1 = y0 + dot(ctx, w_self[:, 3 * d:])
    y1_ref[...] = y1
    tick("cross")
    unit4, rstd4 = normalised(y1)
    a4 = (unit4 * gain[4:5, :] + bias[4:5, :]).astype(BF)
    cq = dot(a4, w_cross[:, :d]).astype(BF)
    kv_ref[...] = dot(enc_ref[...], w_cross[:, d:3 * d]).astype(BF)
    cq_ref[...] = cq
    ck, cv = kv_ref[:, :d], kv_ref[:, d:]
    cctx = attend(cq, ck, cv, valid).astype(BF)
    cctx_ref[...] = cctx
    y2 = y1 + dot(cctx, w_cross[:, 3 * d:])
    y2_ref[...] = y2
    tick("feed")
    unit5, rstd5 = normalised(y2)
    a5 = (unit5 * gain[5:6, :] + bias[5:6, :]).astype(BF)
    y3 = y2
    for c, size in spans(plan.ff, 1024):
        inner = dot(a5, w_ff1[:, c:c + size])
        act = (inner * jax.nn.sigmoid(inner)).astype(BF)
        y3 = y3 + dot(act, w_ff2[c:c + size, :])
    unit6, rstd6 = normalised(y3)
    a6 = (unit6 * gain[6:7, :] + bias[6:7, :]).astype(BF)
    tick("head")
    peak = jnp.full((rows, 1), FLOOR, F32)
    mass = jnp.zeros((rows, 1), F32)
    picked = jnp.zeros((rows, 1), F32)
    summed = jnp.zeros((rows, 1), F32)
    for c, size in chunks:
        z = dot_rt(a6, w_out[c:c + size, :])
        top = jnp.maximum(peak, jnp.max(z, axis=-1, keepdims=True))
        mass = mass * jnp.exp(peak - top) + jnp.sum(jnp.exp(z - top), axis=-1, keepdims=True)
        peak = top
        picked = picked + jnp.sum(jnp.where(want == place[:, :size] + c, z, 0.0), axis=-1, keepdims=True)
        summed = summed + jnp.sum(z, axis=-1, keepdims=True)
    lse = peak + jnp.log(mass)
    rest = 0.1 / (vocab - 1)
    others = (summed - vocab * lse) - (picked - lse)
    per_token = -(0.9 * (picked - lse) + rest * others)
    loss_ref[...] = jnp.full((8, 128), 0.7 * jnp.sum(live * per_token), F32)
    weight = live * (0.7 / utterances)
    da6 = None
    for c, size in chunks:
        z = dot_rt(a6, w_out[c:c + size, :])
        share = jnp.exp(z - lse) * (0.9 + rest * (vocab - 1))
        dz = share - jnp.where(want == place[:, :size] + c, 0.9, rest)
        dz = (dz * weight).astype(BF)
        put8(g_ref, c // 128 * deep, dot_lt(a6, dz))
        if c == 2048:
            tick("head half")
        part = dot(dz, w_out[c:c + size, :])
        da6 = part if da6 is None else da6 + part
    dy, gg6, gb6 = norm_back(da6, unit6, rstd6, gain[6:7, :])
    dy_ref[...] = dy
    g_gain[...] = jnp.concatenate([jnp.zeros((6, d), F32), gg6, jnp.zeros((1, d), F32)], axis=0)
    g_bias[...] = jnp.concatenate([jnp.zeros((6, d), F32), gb6, jnp.zeros((1, d), F32)], axis=0)
    tick("head back")


def dec_bwd_part(plan, tick, len_ref, target_ref, enc_ref, w_self, w_cross, w_ff1, w_ff2, gain, bias, keep,
                 g_ref, g_gain, g_bias, denc_ref):
    y0_ref, y1_ref, y2_ref, dy_ref, mixed_ref, ctx_ref, cctx_ref, cq_ref, kv_ref = keep
    d = plan.width
    deep = d // GROUPS
    at_ff1, at_ff2, at_cross, at_self = plan.dec_at
    gain, bias = gain[...].astype(F32), bias[...].astype(F32)
    causal, valid = source_masks(plan, len_ref)
    unit5, rstd5 = normalised(y2_ref[...])
    a5 = (unit5 * gain[5:6, :] + bias[5:6, :]).astype(BF)
    unit4, rstd4 = normalised(y1_ref[...])
    a4 = (unit4 * gain[4:5, :] + bias[4:5, :]).astype(BF)
    unit3, rstd3 = normalised(y0_ref[...])
    a3 = (unit3 * gain[3:4, :] + bias[3:4, :]).astype(BF)
    dy = dy_ref[...]
    dout = dy.astype(BF)
    da5 = None
    for c, size in spans(plan.ff, 1024):
        inner = dot(a5, w_ff1[:, c:c + size])
        sig = jax.nn.sigmoid(inner)
        act = inner * sig
        put_rows(g_ref, at_ff2, dot_lt(act.astype(BF), dout), c, plan.ff)
        dact = dot_rt(dout, w_ff2[c:c + size, :])
        dinner = (dact * (sig + act * (1.0 - sig))).astype(BF)
        put8(g_ref, at_ff1 + c // 128 * deep, dot_lt(a5, dinner))
        part = dot_rt(dinner, w_ff1[:, c:c + size])
        da5 = part if da5 is None else da5 + part
        tick("dff%d" % (c // 1024))
    dx, gg5, gb5 = norm_back(da5, unit5, rstd5, gain[5:6, :])
    dy = dy + dx
    tick("cross")
    cctx, cq, ck, cv = cctx_ref[...], cq_ref[...], kv_ref[:, :d], kv_ref[:, d:]
    dout = dy.astype(BF)
    tile = d // 128 * deep
    put8(g_ref, at_cross + 3 * tile, dot_lt(cctx, dout))
    dctx = dot_rt(dout, w_cross[:, 3 * d:]).astype(BF)
    dq, dk, dv = attend_back(cq, ck, cv, valid, dctx)
    dq, dk, dv = dq.astype(BF), dk.astype(BF), dv.astype(BF)
    enc = enc_ref[...]
    put8(g_ref, at_cross + tile, dot_lt(enc, dk))
    put8(g_ref, at_cross + 2 * tile, dot_lt(enc, dv))
    denc_ref[...] = dot_rt(dk, w_cross[:, d:2 * d]) + dot_rt(dv, w_cross[:, 2 * d:3 * d])
    put8(g_ref, at_cross, dot_lt(a4, dq))
    da4 = dot_rt(dq, w_cross[:, :d])
    dx, gg4, gb4 = norm_back(da4, unit4, rstd4, gain[4:5, :])
    dy = dy + dx
    tick("self")
    ctx, mixed = ctx_ref[...], mixed_ref[...]
    q, k, v = mixed[:, :d], mixed[:, d:2 * d], mixed[:, 2 * d:]
    dout = dy.astype(BF)
    put8(g_ref, at_self + 3 * tile, dot_lt(ctx, dout))
    dctx = dot_rt(dout, w_self[:, 3 * d:]).astype(BF)
    dq, dk, dv = attend_back(q, k, v, causal, dctx)
    dq, dk, dv = dq.astype(BF), dk.astype(BF), dv.astype(BF)
    put8(g_ref, at_self, dot_lt(a3, dq))
    put8(g_ref, at_self + tile, dot_lt(a3, dk))
    put8(g_ref, at_self + 2 * tile, dot_lt(a3, dv))
    da3 = dot_rt(dq, w_self[:, :d]) + dot_rt(dk, w_self[:, d:2 * d]) + dot_rt(dv, w_self[:, 2 * d:3 * d])
    dx, gg3, gb3 = norm_back(da3, unit3, rstd3, gain[3:4, :])
    tick("dself")
    g_gain[...] += jnp.concatenate([jnp.zeros((3, d), F32), gg3, gg4, gg5, jnp.zeros((2, d), F32)], axis=0)
    g_bias[...] += jnp.concatenate([jnp.zeros((3, d), F32), gb3, gb4, gb5, jnp.zeros((2, d), F32)], axis=0)
    return ((dy + dx) * math.sqrt(d)).astype(BF)


def ctc_part(plan, utterances, tick, len_ref, count_ref, target_ref, enc_ref, w_ref,
             g_ref, denc_ref,
             peak_ref, mass_ref, sel_ref, em_ref, cum_ref, alpha_ref, beta_ref, gam_hi, gam_lo):
    d, vocab, frames, toks = plan.width, plan.vocab, plan.frames, plan.tokens
    lanes, deep = plan.drows, d // GROUPS
    g_ref[:, deep:2 * deep, :] = jnp.zeros((GROUPS, deep, 128), F32)
    g_ref[:, plan.ctc_rows - deep:, :] = jnp.zeros((GROUPS, deep, 128), F32)
    chunks = spans(vocab, plan.chunk)
    place = iota((1, plan.chunk), 1)
    line, counts, lens = token_line(target_ref), scalar_line(plan, count_ref), scalar_line(plan, len_ref)
    (labels,) = columns([line])
    enc = enc_ref[...]
    peak = jnp.full((plan.rows, 1), FLOOR, F32)
    mass = jnp.zeros((plan.rows, 1), F32)
    sel_ref[...] = jnp.zeros((lanes, d), F32)
    blank = None
    for c, size in chunks:
        wc = w_ref[c:c + size, :]
        z = dot_rt(enc, wc)
        if c == 0:
            blank = z[:, 0:1]
        top = jnp.maximum(peak, jnp.max(z, axis=-1, keepdims=True))
        mass = mass * jnp.exp(peak - top) + jnp.sum(jnp.exp(z - top), axis=-1, keepdims=True)
        peak = top
        hot = jnp.where(labels == place[:, :size] + c, 1.0, 0.0).astype(BF)
        sel_ref[...] += dot(hot, wc)
        if c % 1024 == 0:
            tick("first%d" % (c // 1024))
    lse = peak + jnp.log(mass)
    peak_ref[:, 0:1] = lse
    tick("prep")
    lane = iota((1, lanes), 1)
    sel = sel_ref[...].astype(BF)
    em_ref[...] = jnp.zeros((frames, lanes), F32)
    mass_ref[...] = jnp.zeros((frames, lanes), F32)
    for u in range(plan.utts):
        t, at = plan.caps[u], plan.starts[u]
        mine = lane // toks == u
        z = dot_rt(enc[at:at + t, :], sel)
        em_ref[0:t, :] += jnp.where(mine, (z - blank[at:at + t, :]) * LOG2E, 0.0)
        mass_ref[0:t, :] += jnp.where(mine, (blank[at:at + t, :] - lse[at:at + t, :]) * LOG2E, 0.0)
    lower = jnp.where(iota((frames, frames), 0) >= iota((frames, frames), 1), 1.0, 0.0).astype(BF)
    drift = mass_ref[...]
    high, mid = halves(drift)
    low = (drift - high.astype(F32) - mid.astype(F32)).astype(BF)
    total = dot(lower, high) + dot(lower, mid) + dot(lower, low)
    neg = NEG_PATH * LOG2E
    cum_ref[...] = neg - total
    skip = ((line != pltpu.roll(line, 1, 1)) & (lane % toks > 0)).astype(jnp.int32)
    skip_next = ((line != pltpu.roll(line, lanes - 1, 1)) & (lane % toks < toks - 1)).astype(jnp.int32)
    first, ending = lane % toks == 0, lane % toks == counts - 1
    end_frame = lens - 1
    step8, lane8 = iota((8, 128), 0), iota((8, 128), 1) % toks
    first8, final8 = lane8 == step8, lane8 + 7 - step8 == toks - 1

    def spread(row, shift):
        return pltpu.roll(jnp.broadcast_to(row, (8, 128)), shift, 1, stride=1, stride_axis=0)

    def log_sum(a, b, c):
        top = jnp.maximum(jnp.maximum(b, c), a)
        return top, jnp.log2(jnp.exp2(a - top) + jnp.exp2(b - top) + jnp.exp2(c - top))

    def log_pair(a, b):
        top = jnp.maximum(a, b)
        return top + jnp.log2(jnp.exp2(a - top) + jnp.exp2(b - top))

    cuts = [slice(at, at + 128) for at in range(0, lanes, 128)]
    skip8 = [spread(skip[:, cut], 0) > 0 for cut in cuts]
    skip_next8 = [spread(skip_next[:, cut], 121) > 0 for cut in cuts]
    begin8 = [jnp.where(spread(ending[:, cut].astype(jnp.int32), 121) > 0, 0.0, FLOOR) for cut in cuts]
    fill0 = cum_ref[0:1, :]

    def block(i, carry):
        at, back = pl.multiple_of(8 * i, 8), pl.multiple_of(frames - 8 - 8 * i, 8)
        out = []
        for g, cut in enumerate(cuts):
            la, ba, lb, bb = carry[4 * g:4 * g + 4]
            right, left = spread(la, 1), spread(lb, 120)
            la, ba, lb, bb = spread(la, 0), spread(ba, 0), spread(lb, 121), spread(bb, 121)
            ahead, behind = em_ref[pl.ds(at, 8), cut], em_ref[pl.ds(back, 8), cut]
            fills = cum_ref[pl.ds(at, 8), cut]
            fill = cum_ref[pl.ds(pl.multiple_of(jnp.maximum(at - 8, 0), 8), 8), cut][7:8, :]
            alphas, blanks, betas = (jnp.zeros((8, 128), F32),) * 3
            for k in range(8):
                shifted = jnp.where(first8, fill, right if k == 0 else pltpu.roll(la, 7, 0))
                e = spread(ahead[k:k + 1, :], 0)
                top, rest = log_sum(la, ba, jnp.where(skip8[g], shifted, fill))
                la2 = (top + e) + rest
                top, rest = log_sum(shifted, ba, fill)
                ba2 = top + rest
                if k == 0:
                    start = i == 0
                    la2 = jnp.where(start, jnp.where(first8, e, fill0[:, cut]), la2)
                    ba2 = jnp.where(start, jnp.where(first8, 0.0, fill0[:, cut]), ba2)
                la, ba = la2, ba2
                alphas = jnp.where(step8 == k, la[0:1, :], alphas)
                blanks = jnp.where(step8 == k, ba[0:1, :], blanks)
                fill = fills[k:k + 1, :]
                e = spread(behind[7 - k:8 - k, :], 121)
                shifted = jnp.where(final8, FLOOR, left if k == 0 else pltpu.roll(lb, 1, 0))
                top, rest = log_sum(lb, bb, jnp.where(skip_next8[g], shifted, FLOOR))
                begin = end_frame[:, cut] == back + 7 - k
                bb = jnp.where(begin, begin8[g], log_pair(bb, shifted))
                lb = jnp.where(begin, begin8[g] + e, (top + e) + rest)
                betas = jnp.where(step8 == 7 - k, lb[7:8, :], betas)
            alpha_ref[pl.ds(at, 8), cut], mass_ref[pl.ds(at, 8), cut] = alphas, blanks
            beta_ref[pl.ds(back, 8), cut] = betas
            out += [la[0:1, :], ba[0:1, :], lb[7:8, :], bb[7:8, :]]
        return tuple(out)

    carry = (jnp.full((1, 128), FLOOR, F32),) * (4 * len(cuts))
    for i, (at, size) in enumerate(spans(frames // 8, frames // 64)):
        carry = lax.fori_loop(at, at + size, block, carry)
        tick("scan%d" % i)
    moment = iota((frames, lanes), 0)
    la, ba = [jnp.sum(jnp.where(moment == end_frame, ref[...], 0.0), axis=0, keepdims=True) for ref in (alpha_ref, mass_ref)]
    after = jnp.where(first, FLOOR, pltpu.roll(jnp.where(ending, 0.0, FLOOR), 1, 1))
    at_end = jnp.sum(jnp.where(moment == end_frame, neg - cum_ref[...], 0.0), axis=0, keepdims=True)
    floor = NEG_PATH * 10.0 * LOG2E - at_end
    tail = jnp.maximum(jnp.where(ending, la, FLOOR), jnp.where(after == 0.0, ba, FLOOR))
    logz = jnp.zeros((1, lanes), F32)
    ctc = jnp.zeros((), F32)
    for u in range(plan.utts):
        mine = lane // toks == u
        top = jnp.max(jnp.where(mine, tail, FLOOR), axis=-1, keepdims=True)
        bottom = jnp.max(jnp.where(mine, floor, FLOOR), axis=-1, keepdims=True)
        top = jnp.maximum(top, bottom)
        weight = jnp.where(mine & ending, jnp.exp2(la - top), 0.0) + jnp.where(mine & (after == 0.0), jnp.exp2(ba - top), 0.0)
        full = top + jnp.log2(jnp.sum(weight, axis=-1, keepdims=True) + jnp.exp2(bottom - top))
        logz = jnp.where(mine, full, logz)
        drift_end = jnp.max(jnp.where(mine, at_end, FLOOR), axis=-1, keepdims=True)
        ctc = ctc - jnp.sum(full + drift_end) / LOG2E
    gamma = jnp.exp2(alpha_ref[...] + beta_ref[...] - em_ref[...] - logz)
    gamma = jnp.where(moment <= end_frame, gamma, 0.0)
    for u in range(plan.utts):
        t, at = plan.caps[u], plan.starts[u]
        mine = lane // toks == u
        piece = jnp.where(mine, gamma[0:t, :], 0.0)
        high, low = halves(piece)
        gam_hi[at:at + t, :] = high
        gam_lo[at:at + t, :] = low
        alive = jnp.where(iota((t, 1), 0) < len_ref[u], 1.0, 0.0)
        peak_ref[at:at + t, 1:2] = alive
        peak_ref[at:at + t, 2:3] = alive - jnp.sum(piece, axis=-1, keepdims=True)
    lse = peak_ref[:, 0:1]
    scale = 0.3 / utterances
    live = peak_ref[:, 1:2] * scale
    blank_share = peak_ref[:, 2:3]
    for c, size in chunks:
        wc = w_ref[c:c + size, :]
        p = jnp.exp(dot_rt(enc, wc) - lse) * live
        hot = jnp.where(labels == place[:, :size] + c, 1.0, 0.0).astype(BF)
        post = dot(gam_hi[...], hot) + dot(gam_lo[...], hot)
        dz = p - post * scale
        if c == 0:
            dz = dz - jnp.where(place[:, :size] == 0, blank_share * scale, 0.0)
        dz = dz.astype(BF)
        value = dot_lt(enc, dz)
        if c == 0:
            g_ref[:, 0:deep, :] = value[:, :128].reshape(GROUPS, deep, 128)
        put8(g_ref, deep + c // 128 * deep, value, 1 if c == 0 else 0)
        denc_ref[...] += dot(dz, wc)
        if c % 1024 == 0:
            tick("second%d" % (c // 1024))
    return 0.3 * ctc


VM = pl.BlockSpec(memory_space=pltpu.VMEM)
SM = pl.BlockSpec(memory_space=pltpu.SMEM)
ANY = pl.BlockSpec(memory_space=pl.ANY)


def shape(*dims, dtype=F32):
    return jax.ShapeDtypeStruct(dims, dtype)


class Beside:
    def __init__(self, sems):
        self.sems, self.copies = sems, {}

    def start(self, name, source, target):
        copy = pltpu.make_async_copy(source, target, self.sems.at[len(self.copies)])
        self.copies[name] = copy
        copy.start()

    def wait(self, *names):
        for name in names:
            self.copies[name].wait()


class Pair:
    def __init__(self, geo, here, g_ref, recv, out, sems):
        self.geo, self.here, self.g, self.recv, self.out, self.sems = geo, here, g_ref, recv, out, sems

    def copies(self, i, a, b):
        span, at = pl.ds(a, b - a), self.here.at
        return [pltpu.make_async_remote_copy(
            src_ref=self.g.at[2 * y + 1 - at["c"], :, span], dst_ref=self.recv.at[y, :, span],
            send_sem=self.sems.at[0, i, y], recv_sem=self.sems.at[1, i, y],
            device_id=self.here.device("c", 0), device_id_type=MESH) for y in range(self.geo.ny)]

    def keep(self, i, a, b):
        span, at = pl.ds(a, b - a), self.here.at
        return [pltpu.make_async_copy(self.g.at[2 * y + at["c"], :, span], self.out.at[y, :, span], self.sems.at[2, i, y])
                for y in range(self.geo.ny)]

    def start(self, *span):
        for copy in self.copies(*span):
            copy.start()

    def finish(self, i, a, b):
        for copy in self.copies(i, a, b):
            copy.wait()
        many = self.geo.ns * self.geo.gf

        def add(k, carry):
            y, sf = k // many, k % many
            self.g[2 * y + self.here.at["c"], sf, a:b, :] += self.recv[y, sf, a:b, :]
            return carry

        lax.fori_loop(0, self.geo.ny * many, add, 0)
        for copy in self.keep(i, a, b):
            copy.start()

    def end(self, *span):
        for copy in self.keep(*span):
            copy.wait()


def front_kernel(geo, plan, utterances, *refs):
    whole = geo.share > 1
    refs = list(refs)

    def take(count):
        out = refs[:count]
        del refs[:count]
        return out

    len_ref, count_ref, target_ref, bank, pe, pe_tok, w_sub, w_attn, gain, bias = take(10)
    far = take(8)
    h0_out, qkv_out, ctx_out, h1_out, h2_out, pair_out = take(6)
    enc, att, gg, gb = take(4)
    keep = take(9)
    if whole:
        g_out, denc, rows = take(3)
    near = take(8)
    w_ff1, w_ff2, embed, w_self, w_cross, d_ff1, d_ff2, w_out = near
    h0, qkv, ctx, h1, h2 = take(5)
    head, recv, sems, pair_sems = take(4)
    here = Here(geo)
    beside = Beside(sems)
    names = ("ff1", "ff2", "embed", "self", "cross", "dff1", "dff2", "out")
    for name, source, target in zip(names, far, near):
        beside.start(name, source, target)
    barrier = pltpu.get_barrier_semaphore()
    pl.semaphore_signal(barrier, inc=1, device_id=here.device("c", 0), device_id_type=MESH)
    pl.semaphore_wait(barrier, 1)
    pair = Pair(geo, here, head.reshape(2 * geo.ny, geo.ns * geo.gf, plan.out_rows, 128), recv, pair_out, pair_sems)
    cut = plan.out_rows // 32 * 16
    parts = ((0, 0, cut), (1, cut, plan.out_rows))

    def tick(name):
        if name == "encoder feed":
            beside.wait("ff1", "ff2")
        elif name == "decoder":
            for label, source, target in (("h0", h0, h0_out), ("qkv", qkv, qkv_out), ("ctx", ctx, ctx_out), ("h1", h1, h1_out),
                                          ("h2", h2, h2_out)):
                beside.start(label, source, target)
            beside.wait("embed")
        elif name in ("self", "cross"):
            beside.wait(name)
        elif name == "feed":
            beside.wait("dff1", "dff2")
        elif name == "head":
            beside.wait("out")
        elif name == "head half":
            pair.start(*parts[0])
        elif name == "head back":
            pair.start(*parts[1])
            pair.finish(*parts[0])
            pair.finish(*parts[1])

    enc_fwd_part(plan, tick, len_ref, bank, pe, w_sub, w_attn, w_ff1, w_ff2, gain, bias, h0, qkv, ctx, h1, h2, enc)
    dec_fwd_part(plan, utterances, tick, len_ref, count_ref, target_ref, pe_tok, enc, w_self, w_cross, d_ff1, d_ff2, embed, w_out,
                 gain, bias, att, head, gg, gb, keep)
    if whole:
        g_dec = refs[0]
        rows[...] = dec_bwd_part(plan, lambda name: None, len_ref, target_ref, enc, w_self, w_cross, d_ff1, d_ff2, gain, bias, keep,
                                 g_dec, gg, gb, denc)
        beside.start("dec", g_dec, g_out.reshape(GROUPS, plan.dec_rows, 128))
        beside.wait("dec")
    for part in parts:
        pair.end(*part)
    beside.wait("h0", "qkv", "ctx", "h1", "h2")


def positions(length, width):
    place = np.arange(length, dtype=np.float64)[:, None]
    angles = place * np.exp(np.arange(0, width, 2, dtype=np.float64) * (-math.log(10000.0) / width))[None, :]
    return np.stack([np.sin(angles), np.cos(angles)], axis=-1).reshape(length, width).astype(np.float32)


def front(geo, n_bucket, utterances, filter_bank, frame_len, tok_len, targets, weights):
    (w_sub, enc_attn, enc_ff1, enc_ff2, dec_self, dec_cross, dec_ff1, dec_ff2, embed, ctc_head, out_head,
     norm_gain, norm_bias) = weights
    utts, frames, feat = filter_bank.shape
    toks, (vocab, d), ff = targets.shape[1], embed.shape, enc_ff1.shape[1]
    plan = Plan(utts, frames, n_bucket, toks, d, ff, vocab, feat)
    rows, drows, whole = plan.rows, plan.drows, geo.share > 1
    bank = jnp.swapaxes(filter_bank, 1, 2)
    pe = positions(frames, d)
    pe_tok = np.tile(pe[:toks], (utts, 1))
    half = (geo.ny, geo.ns * geo.gf, plan.out_rows, 128)
    far = (enc_ff1, enc_ff2, embed, dec_self, dec_cross, dec_ff1, dec_ff2, out_head.T)
    kept = [shape(rows, d), shape(rows, 3 * d, dtype=BF), shape(rows, d, dtype=BF), shape(rows, d), shape(rows, d)]
    outs = kept + [shape(*half), shape(rows, d, dtype=BF), shape(8, 128), shape(8, d), shape(8, d)] + keep_shapes(plan)
    specs = [ANY] * 6 + [VM] * 13
    scratch = [pltpu.VMEM(x.shape, x.dtype) for x in far + tuple(kept)]
    scratch += [pltpu.VMEM((GROUPS, plan.out_rows, 128), F32), pltpu.VMEM(half, F32), pltpu.SemaphoreType.DMA((14,)),
                pltpu.SemaphoreType.DMA((3, 2, geo.ny))]
    if whole:
        outs += [shape(2 * geo.ny, geo.ns * geo.gf, plan.dec_rows, 128), shape(rows, d), shape(drows, d, dtype=BF)]
        specs += [ANY, VM, VM]
        scratch += [pltpu.VMEM((GROUPS, plan.dec_rows, 128), F32)]
    results = pl.pallas_call(
        functools.partial(front_kernel, geo, plan, utterances),
        out_shape=outs,
        in_specs=[SM] * 2 + [VM] * 8 + [ANY] * 8,
        out_specs=specs,
        scratch_shapes=scratch,
        name="front",
        compiler_params=pltpu.CompilerParams(vmem_limit_bytes=VMEM_LIMIT, collective_id=1, has_side_effects=True),
    )(frame_len, tok_len, targets, bank, jnp.asarray(pe), jnp.asarray(pe_tok), w_sub, enc_attn, norm_gain, norm_bias, *far)
    h0, qkv, ctx, h1, h2, pair, enc, att, gg_dec, gb_dec = results[:10]
    keep, more = results[10:19], results[19:]
    per = feat // GROUPS
    perm = np.zeros((GROUPS * plan.sub_rows, feat), np.float32)
    for r in range(feat):
        perm[r // per * plan.sub_rows + r % per, r] = 1.0
    now = [frame_len, tok_len, targets, enc, norm_gain, norm_bias, gg_dec, gb_dec, att]
    later = [ctc_head.T, bank, jnp.asarray(perm, BF), enc_attn, enc_ff1, enc_ff2, h0, qkv, ctx, h1, h2]
    if whole:
        now += more[1:]
    else:
        now += keep
        later = [dec_ff1, dec_ff2, dec_cross, dec_self] + later
    ctc_scratch = [pltpu.VMEM((rows, 128), F32), pltpu.VMEM((frames, drows), F32), pltpu.VMEM((drows, d), F32)]
    ctc_scratch += [pltpu.VMEM((frames, drows), F32)] * 4 + [pltpu.VMEM((rows, drows), BF)] * 2
    enc_scratch = [pltpu.VMEM((rows, d), F32), pltpu.VMEM((rows, d), F32), pltpu.VMEM((rows, 3 * d), BF)]
    return plan, now, later, [pair] + (list(more[:1]) if whole else []), ctc_scratch, enc_scratch


MESH = pl.DeviceIdType.MESH


class Geometry:
    def __init__(self, n_bucket, n_dp):
        self.ny, self.ns = n_bucket // 2, 4
        self.nf = n_dp // self.ns
        self.share = n_bucket * n_dp // GROUPS
        self.gf = self.nf // self.share
        if self.ny * 2 * self.ns * self.gf != GROUPS:
            raise ValueError("mesh size")

    def size(self, axis):
        return {"c": 2, "y": self.ny, "s": self.ns, "f": self.nf}[axis]


class Here:
    def __init__(self, geo):
        self.geo = geo
        bucket, dp = lax.axis_index("bucket"), lax.axis_index("dp")
        self.at = {"y": bucket // 2, "c": bucket % 2, "s": dp // geo.nf, "f": dp % geo.nf}
        self.devices, self.index = 2 * geo.ny * geo.ns * geo.nf, bucket * geo.ns * geo.nf + dp

    def other(self, index):
        n_dp = self.geo.ns * self.geo.nf
        return (index // n_dp, lax.rem(index, n_dp))

    def step(self, axis, p):
        return lax.rem(self.at[axis] + 1 + p, self.geo.size(axis))

    def device(self, axis, p):
        at = dict(self.at)
        at[axis] = self.step(axis, p)
        return (at["y"] * 2 + at["c"], at["s"] * self.geo.nf + at["f"])

    def greet(self):
        barrier = pltpu.get_barrier_semaphore()
        for p in range(self.devices - 1):
            device = self.other(lax.rem(self.index + 1 + p, self.devices))
            pl.semaphore_signal(barrier, inc=1, device_id=device, device_id_type=MESH)
        pl.semaphore_wait(barrier, self.devices - 1)


class Stream:
    def __init__(self, geo, array, a, b, order, dtype, resident=False, paired=False):
        self.geo, self.array, self.a, self.n, self.order, self.dtype = geo, array, a, b - a, order, dtype
        self.resident, self.paired = resident, paired

    def wire(self, stage, n):
        geo = self.geo
        done = self.order[:stage]
        axis = self.order[stage]
        if axis == "c":
            return (geo.ny, geo.ns * geo.gf, n, 128)
        dims = [size for other, size in (("y", geo.ny), ("s", geo.ns), ("f", geo.gf)) if other not in done and other != axis]
        return tuple(dims) + (n, 128)

    def buffers(self, stage, n):
        if stage == 0:
            return [pltpu.VMEM(self.wire(0, n), F32)]
        return [pltpu.VMEM((self.geo.size(self.order[stage]) - 1,) + self.wire(stage, n), self.dtype)] * 2

    def own(self):
        geo = self.geo
        sems = [pltpu.SemaphoreType.DMA((3, geo.ny))]
        for stage in (1, 2, 3):
            sems += [pltpu.SemaphoreType.DMA((2, geo.size(self.order[stage]) - 1))]
        if self.resident:
            return sems
        return sems + [pltpu.VMEM((geo.ny, geo.ns * geo.gf, self.n, 128), F32)]

    def bind(self, here, g_refs, shared, own, r_ref, r_at):
        self.here, self.g, self.r, self.r_at = here, g_refs[self.array], r_ref, r_at
        rows = pl.ds(0, self.n)
        cut = [[ref.at[(slice(None),) * (len(ref.shape) - 2) + (rows,)] for ref in refs] for refs in shared]
        self.core = None if self.paired else cut[0][0]
        self.send = {stage: cut[stage][0] for stage in (1, 2, 3)}
        self.recv = {stage: cut[stage][1] for stage in (1, 2, 3)}
        self.sems = own[:4]
        self.sums = None if self.resident else own[4]

    def get(self, y, sf):
        if self.resident:
            return self.g[2 * y + self.here.at["c"], sf, self.a:self.a + self.n, :]
        return self.sums[y, sf]

    def put(self, y, sf, value):
        if self.resident:
            self.g[2 * y + self.here.at["c"], sf, self.a:self.a + self.n, :] = value
        else:
            self.sums[y, sf] = value

    def core_copies(self):
        geo, at, sems = self.geo, self.here.at, self.sems[0]
        span = pl.ds(self.a, self.n)
        if self.paired:
            return [pltpu.make_async_copy(self.g.at[y, :, span], self.sums.at[y], sems.at[2, y]) for y in range(geo.ny)]
        copies = [pltpu.make_async_remote_copy(
            src_ref=self.g.at[2 * y + 1 - at["c"], :, span], dst_ref=self.core.at[y],
            send_sem=sems.at[0, y], recv_sem=sems.at[1, y],
            device_id=self.here.device("c", 0), device_id_type=MESH) for y in range(geo.ny)]
        if not self.resident:
            copies += [pltpu.make_async_copy(self.g.at[2 * y + at["c"], :, span], self.sums.at[y], sems.at[2, y])
                       for y in range(geo.ny)]
        return copies

    def wire_copies(self, stage):
        axis, partners = self.order[stage], self.geo.size(self.order[stage]) - 1
        return [pltpu.make_async_remote_copy(
            src_ref=self.send[stage].at[p], dst_ref=self.recv[stage].at[partners - 1 - p],
            send_sem=self.sems[stage].at[0, p], recv_sem=self.sems[stage].at[1, partners - 1 - p],
            device_id=self.here.device(axis, p), device_id_type=MESH) for p in range(partners)]

    def blocks(self, stage):
        geo, at = self.geo, self.here.at
        done = self.order[:stage + 1]
        sizes = [1 if axis in done else size for axis, size in (("y", geo.ny), ("s", geo.ns), ("f", geo.gf))]

        def place(i, swap=None):
            f = i % sizes[2]
            s = i // sizes[2] % sizes[1]
            y = i // (sizes[2] * sizes[1])
            where = {"y": at["y"] if "y" in done else y, "s": at["s"] if "s" in done else s,
                     "f": (at["f"] if "f" in done else f) if geo.gf > 1 else 0}
            if swap is not None and not (swap[0] == "f" and geo.gf == 1):
                where[swap[0]] = swap[1]
            wire = tuple(v for axis, v in (("y", y), ("s", s), ("f", f)) if axis not in done)
            return (where["y"], where["s"] * geo.gf + where["f"]), wire

        return math.prod(sizes), place

    def start(self, stage):
        if stage == 0:
            for copy in self.core_copies():
                copy.start()
            return
        axis = self.order[stage]
        count, place = self.blocks(stage)
        for p, copy in enumerate(self.wire_copies(stage)):
            target = self.here.step(axis, p)

            def fill(i, carry, p=p, target=target):
                at, wire = place(i, (axis, target))
                self.send[stage][(p,) + wire] = self.get(*at).astype(self.dtype)
                return carry

            loop(count, fill)
            copy.start()

    def finish(self, stage):
        if stage == 0:
            for copy in self.core_copies():
                copy.wait()
            if self.paired:
                return
            geo = self.geo

            def add(i, carry):
                y, sf = i // (geo.ns * geo.gf), i % (geo.ns * geo.gf)
                self.put(y, sf, self.get(y, sf) + self.core[y, sf])
                return carry

            loop(geo.ny * geo.ns * geo.gf, add)
            return
        count, place = self.blocks(stage)
        copies = self.wire_copies(stage)
        for copy in copies:
            copy.wait()

        def add(i, carry):
            at, wire = place(i)
            total = self.get(*at)
            for p in range(len(copies)):
                total = total + self.recv[stage][(p,) + wire].astype(F32)
            if stage == 3:
                self.r[self.r_at:self.r_at + self.n, :] = total
            else:
                self.put(*at, total)
            return carry

        loop(count, add)


class RowStream(Stream):
    def __init__(self, geo, plan):
        order = "fycs" if geo.share == 1 else "ycsf"
        super().__init__(geo, -1, 0, plan.embed_lines, order, BF, True)
        self.plan, self.gathers = plan, 3 if geo.share == 1 else 2

    def own(self):
        geo, plan = self.geo, self.plan
        size = [geo.size(axis) - 1 for axis in self.order]
        out = [pltpu.SemaphoreType.DMA((2, count)) for count in size]
        out += [pltpu.VMEM((2, geo.ny, geo.gf, plan.drows + 16, plan.width), BF), pltpu.VMEM((geo.ns, self.n, 128), F32)]
        for stage in range(self.gathers, 4):
            out += [pltpu.VMEM((size[stage],) + self.wire(stage, self.n), BF)] * 2
        return out

    def bind(self, here, own, r_ref, r_at):
        self.here, self.r, self.r_at = here, r_ref, r_at
        self.sems, self.rows, self.block = own[:4], own[4], own[5]
        self.send = {stage: own[6 + 2 * (stage - self.gathers)] for stage in range(self.gathers, 4)}
        self.recv = {stage: own[7 + 2 * (stage - self.gathers)] for stage in range(self.gathers, 4)}

    def get(self, y, sf):
        return self.block[sf // self.geo.gf]

    def put(self, y, sf, value):
        self.block[sf // self.geo.gf] = value

    def fill(self, rows, toks):
        at, geo = self.here.at, self.geo
        mine = (at["c"], at["y"], at["f"] if geo.gf > 1 else 0)
        lines, width = self.plan.drows, self.plan.width
        self.rows[mine + (pl.ds(0, lines), slice(None))] = rows
        ids = jnp.concatenate([toks // 64, lax.rem(toks, 64), jnp.zeros((14, lines), jnp.int32)], axis=0).astype(F32)
        if lines < width:
            ids = jnp.concatenate([ids, jnp.zeros((16, width - lines), F32)], axis=1)
        self.rows[mine + (pl.ds(lines, 16), slice(None))] = ids.astype(BF)

    def gather_copies(self, stage, come=False):
        at, axis, geo = self.here.at, self.order[stage], self.geo
        done = self.order[:stage]
        f = at["f"] if geo.gf > 1 else 0
        if axis == "c":
            part = self.rows.at[at["c"]]
        elif "f" in done or geo.gf == 1:
            part = self.rows.at[at["c"], at["y"]]
        else:
            part = self.rows.at[at["c"], at["y"], f]
        partners = geo.size(axis) - 1
        out = []
        for p in range(partners):
            other = dict(at)
            other[axis] = self.here.step(axis, p)
            if axis == "c":
                theirs = self.rows.at[other["c"]]
            elif "f" in done or geo.gf == 1:
                theirs = self.rows.at[other["c"], other["y"]]
            else:
                theirs = self.rows.at[other["c"], other["y"], other["f"]]
            out.append((p, part, theirs))
        return [pltpu.make_async_remote_copy(
            src_ref=part, dst_ref=theirs if come else part, send_sem=self.sems[stage].at[0, p],
            recv_sem=self.sems[stage].at[1, p if come else partners - 1 - p],
            device_id=self.here.device(axis, p), device_id_type=MESH) for p, part, theirs in out]

    def start(self, stage):
        if stage >= self.gathers:
            return super().start(stage)
        for copy in self.gather_copies(stage):
            copy.start()

    def finish(self, stage):
        if stage >= self.gathers:
            return super().finish(stage)
        for copy in self.gather_copies(stage):
            copy.wait_send()
        for copy in self.gather_copies(stage, True):
            copy.wait_recv()
        if stage == self.gathers - 1:
            self.add_up()

    def add_up(self):
        plan, geo, at = self.plan, self.geo, self.here.at
        tall, lines, width = plan.embed_rows, plan.drows, plan.width
        share = plan.vocab // GROUPS
        rows = self.rows[...].reshape(2 * geo.ny * geo.gf, lines + 16, width)
        many = rows.shape[0]
        ids = rows[:, lines:, :].astype(F32)
        toks = jnp.concatenate([ids[i, 0:1, :lines] * 64.0 + ids[i, 1:2, :lines] for i in range(many)], axis=1)
        rows = jnp.concatenate([rows[i, :lines, :] for i in range(many)], axis=0)
        for s in range(geo.ns):
            group = ((at["y"] * 2 + at["c"]) * geo.ns + s) * geo.gf + (at["f"] if geo.gf > 1 else 0)
            first = share * group + (plan.vocab - share * GROUPS) * group // GROUPS
            hot = jnp.where((iota((tall, many * lines), 0) + first).astype(F32) == toks, 1.0, 0.0).astype(BF)
            value = dot(hot, rows)
            for c in range(width // 128):
                self.block[s, tall * c:tall * (c + 1), :] = value[:, 128 * c:128 * (c + 1)]


def loop(count, body):
    if count == 1:
        body(0, 0)
    else:
        lax.fori_loop(0, count, body, 0, unroll=min(count, 4))


class Sum:
    SCRIPT = {
        "begin": (0, 1, 2, 3), "dff1": (0, 0, 1, 1, 2, 2, 4, 5), "cross": (3, 3), "dself": (4, 5, 6, 7),
        "rows": (0, 0, 1, 1, 4, 5, 8), "first2": (6,), "first3": (2, 2, 3, 3, 6, 7, 7), "first4": (0, 0, 1, 1),
        "scan2": (0,), "scan3": (4, 4, 5, 5), "scan4": (1, 2, 2, 8, 8), "scan6": (3, 3, 7, 7),
        "second0": (2, 4, 4, 6, 6, 9), "second1": (3, 5, 5, 7, 7, 10), "second2": (6, 6, 8, 8, 9, 9, 11),
        "second3": (4, 10, 10), "second4": (5, 8, 8, 9, 9, 11, 11, 12, 13), "ff0": (6, 7, 10, 10),
        "ff1": (9, 9, 12, 12, 13, 13), "ff2": (11, 11), "ff3": (10, 10, 15, 16), "attn0": (12, 12),
        "attn1": (8, 13, 13), "attn2": (9, 11, 11, 15, 15), "attn3": (10, 12, 12, 13, 13, 16, 16),
        "end": (11, 14, 17, 18),
        "drain": (12, 15, 15, 14, 14, 17, 17, 18, 18, 13, 16, 16, 17, 17, 15, 15, 14, 14, 16, 16, 18, 18, 14, 14, 17, 17, 15, 18, 18, 16, 14, 17, 18),
    }
    CUTS = (4, 2, 2, 4, 2, 2)
    DEPTH = 2

    def __init__(self, geo, plan):
        self.geo = geo
        orders = ("cfys", "cyfs") if geo.share == 1 else ("cysf", "csyf")
        ff = 2 * plan.ff // 128 * (plan.width // GROUPS)
        self.streams = []

        def cut(array, a, b, count):
            size = (b - a) // count // 16 * 16
            for i in range(count):
                end = b if i == count - 1 else a + size
                here = array > 1 or (array == 1 and geo.share == 1)
                self.streams.append(Stream(geo, array, a, end, orders[i % 2], BF, here, array == 0))
                a = end

        out, dec, rest, ctc, enc, last = self.CUTS
        cut(0, 0, plan.out_rows, out)
        cut(1, 0, ff, dec)
        cut(1, ff, plan.dec_rows, rest)
        self.row_stream = RowStream(geo, plan)
        self.streams.append(self.row_stream)
        self.streams.append(Stream(geo, 2, 0, 16, orders[0], F32, True))
        cut(2, 16, plan.ctc_rows, ctc)
        self.streams.append(Stream(geo, 3, 0, 16, orders[1], F32, True))
        cut(3, 16, 16 + ff, enc)
        cut(3, 16 + ff, plan.enc_rows, last)
        steps = [0] * len(self.streams)
        self.pools = {}
        for name in self.SCRIPT:
            for i in self.SCRIPT[name]:
                stream = self.streams[i]
                if steps[i] % 2 == 0 and self.pooled(stream) and not (steps[i] == 0 and stream.paired):
                    stage = steps[i] // 2
                    self.pools.setdefault((stage, self.streams[i].order if stage else "c"), []).append(i)
                steps[i] += 1
        if any(count != 8 for count in steps):
            raise ValueError("script")
        self.before, self.after, self.slot = {}, {}, {}
        for (stage, _), users in self.pools.items():
            for at, i in enumerate(users):
                self.slot[i, stage] = at % self.DEPTH
                if at >= self.DEPTH:
                    self.before[i, stage] = users[at - self.DEPTH]
                    self.after[users[at - self.DEPTH], stage] = i
        self.tall = max(stream.n for stream in self.streams if self.pooled(stream))

    def pooled(self, stream):
        return stream.dtype != F32 and stream is not self.row_stream

    def scratch(self):
        out = [pltpu.SemaphoreType.REGULAR((len(self.streams), 4))]
        for stage, order in sorted(self.pools):
            stream = next(stream for stream in self.streams if self.pooled(stream) and order in ("c", stream.order))
            for _ in range(self.DEPTH):
                out += stream.buffers(stage, self.tall)
        for stream in self.streams:
            out += stream.own()
            if stream.dtype == F32:
                for stage in range(4):
                    out += stream.buffers(stage, stream.n)
        return out

    def bind(self, here, arrays, refs, r_ref, bases):
        refs = list(refs)
        self.here, self.free = here, refs.pop(0)

        def take(count):
            out = refs[:count]
            del refs[:count]
            return out

        sets = {key: [take(2 if key[0] else 1) for _ in range(self.DEPTH)] for key in sorted(self.pools)}
        for i, stream in enumerate(self.streams):
            if stream is self.row_stream:
                stream.bind(here, take(len(stream.own())), r_ref, bases[-1])
                continue
            own = take(4 if stream.resident else 5)
            if stream.dtype == F32:
                buffers = [take(2 if stage else 1) for stage in range(4)]
            else:
                buffers = [sets[stage, stream.order if stage else "c"][self.slot[i, stage]] if (i, stage) in self.slot else []
                           for stage in range(4)]
            stream.bind(here, arrays, buffers, own, r_ref, bases[stream.array] + stream.a)
        self.steps = [0] * len(self.streams)

    def tick(self, name):
        for i in self.SCRIPT.get(name, ()):
            stage, ending = divmod(self.steps[i], 2)
            self.steps[i] += 1
            stream = self.streams[i]
            partners = self.geo.size(stream.order[stage]) - 1
            if ending:
                stream.finish(stage)
                if (i, stage) in self.after:
                    for p in range(partners):
                        pl.semaphore_signal(self.free.at[self.after[i, stage], stage], inc=1,
                                            device_id=self.here.device(stream.order[stage], p), device_id_type=MESH)
            else:
                if (i, stage) in self.before:
                    pl.semaphore_wait(self.free.at[i, stage], partners)
                stream.start(stage)


class Layout:
    def __init__(self, plan, geo, sizes):
        self.plan, self.share = plan, geo.share
        self.widths = [size // GROUPS // geo.share for size in sizes]
        self.starts = [int(x) for x in np.cumsum([0] + self.widths)]
        self.part = self.starts[-1]
        self.lines = -(-self.part // 1024) * 8
        self.base_dec = plan.out_rows
        self.base_embed = self.base_dec + plan.dec_rows
        self.base_ctc = self.base_embed + plan.embed_lines
        self.base_enc = self.base_ctc + plan.ctc_rows
        self.rows = self.base_enc + plan.enc_rows
        d, deep = plan.width, plan.width // GROUPS
        e, c = [self.base_enc + x for x in plan.enc_at], [self.base_dec + x for x in plan.dec_at]
        long = plan.ff // GROUPS
        attn, ff, two = 4 * d // 128, plan.ff // 128, d // 128
        self.place = [(e[3], plan.sub_rows, two), (e[2], deep, attn), (e[1], deep, ff), (e[0], long, two),
                      (c[3], deep, attn), (c[2], deep, attn), (c[0], deep, ff), (c[1], long, two),
                      (self.base_embed, plan.embed_rows, two), (self.base_ctc, deep, plan.out_rows // deep), (0, deep, plan.out_rows // deep)]

    def tile(self, weight, c):
        base, deep, _ = self.place[weight]
        return base + deep * c + (deep if weight == 9 and c > 0 else 0)

    def in_xla(self, r, bucket, dp, n_dp):
        index = bucket * n_dp + dp
        group, within = index // self.share, index % self.share
        pieces = []
        for weight, width in enumerate(self.widths):
            if weight >= 11:
                line, at = r[self.base_enc + weight - 11], 0
            else:
                _, deep, tiles = self.place[weight]
                block = jnp.concatenate([r[self.tile(weight, c):self.tile(weight, c) + deep] for c in range(tiles)], axis=1)
                if weight in (9, 10):
                    block = block[:, : self.plan.vocab]
                line, at = block.reshape(-1), 0
                if weight == 8:
                    at = group * (width * self.share) % self.plan.width
            pieces.append(lax.dynamic_slice(line, (at + within * width,), (width,)))
        flat = jnp.concatenate(pieces)
        return jnp.pad(flat, (0, self.lines * 128 - self.part)).reshape(self.lines, 128)

    def in_kernel(self, r, flat, work, group):
        flat[self.lines - 8:, :] = jnp.zeros((8, 128), F32)
        lane = iota((1, 128), 1)

        def put(value, base, length):
            lines, row, shift = -(-length // 128), base // 128, base % 128
            value = value[:lines]
            if shift == 0 and length % 128 == 0:
                flat[row:row + lines, :] = value
                return
            moved = pltpu.roll(value, shift, 1) if shift else value
            number = 128 * iota((lines, 128), 0) + (lane - shift) % 128
            right = (lane >= shift) & (number < length)
            flat[row:row + lines, :] = jnp.where(right, moved, flat[row:row + lines, :])
            if shift:
                left = (lane < shift) & (number < length)
                flat[row + 1:row + 1 + lines, :] = jnp.where(left, moved, flat[row + 1:row + 1 + lines, :])

        for weight, width in enumerate(self.widths):
            base = self.starts[weight]
            if weight >= 11:
                put(r[self.base_enc + weight - 11:self.base_enc + weight - 10, :], base, width)
                continue
            _, deep, tiles = self.place[weight]
            if weight == 8:
                for c in range(tiles):
                    at = self.tile(weight, c)
                    work[pl.ds(c, deep, stride=tiles), :] = r[at:at + deep, :]
                offset = lax.rem(group * width, self.plan.width)
                need = -(-width // 128)
                value = jnp.where(offset >= 128, work[1:need + 2, :], work[0:need + 1, :])
                turned = pltpu.roll(value, 64, 1)
                after = jnp.where(lane < 64, turned[:need], turned[1:])
                put(jnp.where(lax.rem(offset, 128) >= 64, after, value[:need]), base, width)
            elif weight in (9, 10):
                for c in range(tiles):
                    at = self.tile(weight, c)
                    work[pl.ds(c, deep, stride=tiles), :] = r[at:at + deep, :]
                for i in range(deep):
                    put(work[tiles * i:tiles * (i + 1), :], base + self.plan.vocab * i, self.plan.vocab)
            else:
                count = width // 128 // tiles
                for c in range(tiles):
                    at = self.tile(weight, c)
                    flat[pl.ds(base // 128 + c, count, stride=tiles), :] = r[at:at + count, :]


def tail_kernel(geo, plan, layout, total, utterances, counts, *refs):
    fused = geo.share == 1
    refs = list(refs)

    def take(count):
        out = refs[:count]
        del refs[:count]
        return out

    len_ref, count_ref, target_ref, enc, gain, bias, gg_in, gb_in, att = take(9)
    if fused:
        keep = take(9)
        names = ["dff1", "dff2", "cross", "self"]
    else:
        denc_in, row_in = take(2)
        names = []
    names += ["head", "bank", "perm", "attn", "ff1", "ff2", "h0", "qkv", "ctx", "h1", "h2"]
    names += ["master", "moment1", "moment2"] if fused else []
    far = take(len(names))
    pair = take(1)[0]
    g_far = None if fused else take(1)[0]
    out_ref, info_ref = take(2)
    near = dict(zip(names, take(len(far))))
    sems, g_ctc, g_enc, denc, gg, gb = take(6)
    g_dec = take(1)[0] if fused else None
    ctc_scratch, enc_scratch = take(counts[0]), take(counts[1])
    fused_scratch = take(counts[2])
    optimizer = [near[name] for name in ("master", "moment1", "moment2")] if fused else None
    here = Here(geo)
    r_ref = fused_scratch[0] if fused else out_ref
    dims = (2 * geo.ny, geo.ns * geo.gf)
    arrays = (pair, g_dec.reshape(*dims, plan.dec_rows, 128) if fused else g_far, g_ctc.reshape(*dims, plan.ctc_rows, 128),
              g_enc.reshape(*dims, plan.enc_rows, 128))
    total.bind(here, arrays, refs, r_ref, (0, layout.base_dec, layout.base_ctc, layout.base_enc, layout.base_embed))
    beside = Beside(sems)
    first = names.index("head")

    def load(some):
        for name in some:
            beside.start(name, far[names.index(name)], near[name])

    load(names[:first])
    here.greet()
    total.tick("begin")
    gg[...], gb[...] = gg_in[...], gb_in[...]
    if fused:
        beside.wait("dff1", "dff2")

        def tick(name):
            if name in ("cross", "self"):
                beside.wait(name)
            total.tick(name)
            if name == "dff1":
                load(names[first:])

        rows = dec_bwd_part(plan, tick, len_ref, target_ref, enc, near["self"], near["cross"], near["dff1"], near["dff2"], gain, bias,
                            keep, g_dec, gg, gb, denc)
    else:
        load(names)
        for name in ("dff0", "dff1", "cross", "self", "dself"):
            total.tick(name)
        rows = row_in[...]
        denc[...] = denc_in[...]
    total.row_stream.fill(rows, input_tokens(plan, target_ref))
    total.tick("rows")
    beside.wait("head")
    loss = ctc_part(plan, utterances, total.tick, len_ref, count_ref, target_ref, enc, near["head"], g_ctc, denc, *ctc_scratch)
    beside.wait(*names[names.index("bank"):])
    enc_bwd_part(plan, total.tick, len_ref, *[near[name] for name in ("bank", "perm", "attn", "ff1", "ff2")], gain, bias,
                 *[near[name] for name in ("h0", "qkv", "ctx", "h1", "h2")], denc, gg, gb, g_enc, *enc_scratch)
    if fused:
        weight_squares = square_sums(layout, optimizer, fused_scratch)
    total.tick("end")
    total.tick("drain")
    row = jnp.zeros((1, 128), F32) + (loss + att[0:1, :])
    if fused:
        group = ((here.at["y"] * 2 + here.at["c"]) * geo.ns + here.at["s"]) * geo.gf + here.at["f"]
        layout.in_kernel(r_ref, out_ref, fused_scratch[1], group)
        norms(geo, layout, here, out_ref, weight_squares, row, info_ref, fused_scratch)
    else:
        info_ref[0:1, :] = row
        info_ref[1:2, :] = row


def tail(geo, plan, layout, utterances, now, later, summed, ctc_scratch, enc_scratch, optimizer):
    fused = geo.share == 1
    total = Sum(geo, plan)
    extra = norm_scratch(geo, plan, layout) if fused else []
    later = list(later) + (list(optimizer) if fused else [])
    scratch = [pltpu.VMEM(x.shape, x.dtype) for x in later]
    scratch += [pltpu.SemaphoreType.DMA((len(later),)), pltpu.VMEM((GROUPS, plan.ctc_rows, 128), F32),
                pltpu.VMEM((GROUPS, plan.enc_rows, 128), F32), pltpu.VMEM((plan.rows, plan.width), F32),
                pltpu.VMEM((8, plan.width), F32), pltpu.VMEM((8, plan.width), F32)]
    scratch += [pltpu.VMEM((GROUPS, plan.dec_rows, 128), F32)] if fused else []
    scratch += ctc_scratch + enc_scratch + extra + total.scratch()
    lines = layout.lines if fused else layout.rows
    return pl.pallas_call(
        functools.partial(tail_kernel, geo, plan, layout, total, utterances, (len(ctc_scratch), len(enc_scratch), len(extra))),
        out_shape=[shape(lines, 128), shape(8, 128)],
        in_specs=[SM] * 2 + [VM] * (len(now) - 2) + [ANY] * (len(later) + len(summed)),
        out_specs=[VM] * 2,
        scratch_shapes=scratch,
        name="tail",
        compiler_params=pltpu.CompilerParams(vmem_limit_bytes=VMEM_LIMIT, collective_id=0, has_side_effects=True),
    )(*now, *later, *summed)


def share_sum(here, row, block, recv, sems, turn):
    devices, own = here.devices, here.index
    block[turn] = row
    recv[turn, pl.ds(own, 1)] = row.reshape(1, 1, 128)

    def copy(p, sender):
        other = lax.rem(own + 1 + p, devices)
        slot = own if sender else other
        return pltpu.make_async_remote_copy(
            src_ref=block.at[turn], dst_ref=recv.at[turn, slot], send_sem=sems.at[turn, 0, p], recv_sem=sems.at[turn, 1, slot],
            device_id=here.other(other), device_id_type=MESH)

    for p in range(devices - 1):
        copy(p, True).start()
    for p in range(devices - 1):
        copy(p, False).wait_recv()
    for p in range(devices - 1):
        copy(p, True).wait_send()
    return jnp.sum(recv[turn].reshape(devices, 128), axis=0, keepdims=True)


def edges(layout):
    full = layout.part // 128
    return full, layout.part - full * 128


def load_flat(layout, source, target):
    full, edge = edges(layout)
    target[0:full, :] = source[pl.ds(0, full * 128)].reshape(full, 128)
    if edge:
        target[full:full + 1, :] = jnp.zeros((1, 128), F32)
        target[full:full + 1, 0:edge] = source[pl.ds(full * 128, edge)].reshape(1, edge)


def store_flat(layout, target, value):
    full, edge = edges(layout)
    target[pl.ds(0, full * 128)] = value[0:full, :].reshape(full * 128).astype(target.dtype)
    if edge:
        target[pl.ds(full * 128, edge)] = value[full:full + 1, 0:edge].reshape(edge).astype(target.dtype)


def pieces(layout, m):
    lo, hi = layout.starts[m], layout.starts[m + 1]
    shared = []
    for at in sorted({lo // 128, hi // 128}):
        left, right = max(lo, at * 128) - at * 128, min(hi, at * 128 + 128) - at * 128
        if left < right and not (left == 0 and right == 128):
            shared.append((at, left, right))
    return (-(-lo // 128), hi // 128), shared


def matrix_sums(layout, ref):
    lane = iota((1, 128), 1)
    out = jnp.zeros((1, 128), F32)
    for m in range(len(layout.widths)):
        (r0, r1), shared = pieces(layout, m)
        total = jnp.zeros((1, 128), F32)
        if r1 > r0:
            total = total + jnp.sum(ref[r0:r1, :], axis=0, keepdims=True)
        for at, left, right in shared:
            total = total + jnp.where((lane >= left) & (lane < right), ref[at:at + 1, :], 0.0)
        out = jnp.where(lane == m, jnp.sum(total, axis=1, keepdims=True), out)
    return out


def norm_scratch(geo, plan, layout):
    devices = 2 * geo.ny * geo.ns * geo.nf
    flat = pltpu.VMEM((layout.lines, 128), F32)
    return [pltpu.VMEM((layout.rows, 128), F32), pltpu.VMEM((plan.embed_rows * plan.width // 128, 128), F32), flat, flat, flat, flat,
            pltpu.VMEM((2, 1, 128), F32), pltpu.VMEM((2, devices, 1, 128), F32), pltpu.SemaphoreType.DMA((2, 2, devices))]


def square_sums(layout, optimizer, scratch):
    w, a, b, sq = scratch[2:6]
    lines = sum(1 if x else 0 for x in edges(layout)[1:]) + edges(layout)[0]
    for source, target in zip(optimizer, (w, a, b)):
        load_flat(layout, source, target)
    sq[0:lines, :] = w[0:lines, :] * w[0:lines, :]
    return matrix_sums(layout, sq)


def adam(g, clip, w, a, b):
    scaled = g * jnp.minimum(1.0, 1.0 / clip)
    first = 0.5 * a + 0.5 * scaled
    second = 0.5 * b + 0.5 * scaled * scaled
    correct = 1.0 - 0.5**STEP
    return first, second, first / correct / (jnp.sqrt(second / correct) + 1e-06) + 0.01 * w


def norms(geo, layout, here, g_ref, weight_squares, loss, info_ref, scratch):
    w, a, b, sq, block, recv, sems = scratch[2:9]
    full, edge = edges(layout)
    lines = full + (1 if edge else 0)
    lane = iota((1, 128), 1)
    g = g_ref[0:lines, :]
    squares = jnp.sum(jnp.sum(g * g, axis=0, keepdims=True), axis=1, keepdims=True)
    row = jnp.where(lane == 120, squares, jnp.where(lane == 121, loss, weight_squares))
    row = share_sum(here, row, block, recv, sems, 0)
    info_ref[0:1, :] = row
    clip = jnp.sqrt(jnp.sum(jnp.where(lane == 120, row, 0.0), axis=1, keepdims=True))
    _, _, direction = adam(g, clip, w[0:lines, :], a[0:lines, :], b[0:lines, :])
    sq[0:lines, :] = direction * direction
    row = share_sum(here, matrix_sums(layout, sq), block, recv, sems, 1)
    info_ref[1:2, :] = row


def norm_kernel(geo, layout, g_ref, master, moment1, moment2, loss_ref, info_ref, *scratch):
    here = Here(geo)
    here.greet()
    weight_squares = square_sums(layout, (master, moment1, moment2), scratch)
    norms(geo, layout, here, g_ref, weight_squares, loss_ref[0:1, :], info_ref, scratch)


def update_kernel(layout, utterances, g_ref, master, moment1, moment2, info_ref,
                  loss_ref, clip_ref, first_ref, second_ref, fresh_ref, low_ref, wn_ref, un_ref, w, a, b):
    full, edge = edges(layout)
    lines, count = full + (1 if edge else 0), len(layout.widths)
    lane = iota((1, 128), 1)
    for source, target in ((master, w), (moment1, a), (moment2, b)):
        load_flat(layout, source, target)
    row = info_ref[0:1, :]
    clip = jnp.sqrt(jnp.sum(jnp.where(lane == 120, row, 0.0), axis=1, keepdims=True))
    loss_ref[0] = jnp.sum(jnp.where(lane == 121, row, 0.0)) / utterances
    clip_ref[0] = jnp.sum(clip)
    weight_norms, update_norms = jnp.sqrt(row), jnp.sqrt(info_ref[1:2, :])
    wn_ref[...] = weight_norms[:, 0:count].reshape(count)
    un_ref[...] = update_norms[:, 0:count].reshape(count)
    ratio = 0.5 * weight_norms / update_norms
    first, second, direction = adam(g_ref[0:lines, :], clip, w[0:lines, :], a[0:lines, :], b[0:lines, :])
    store_flat(layout, first_ref, first)
    store_flat(layout, second_ref, second)
    a[0:lines, :] = direction
    for m in range(count):
        scale = jnp.sum(jnp.where(lane == m, ratio, 0.0), axis=1, keepdims=True)
        (r0, r1), shared = pieces(layout, m)
        if r1 > r0:
            w[r0:r1, :] -= scale * a[r0:r1, :]
        for at, left, right in shared:
            w[at:at + 1, :] -= jnp.where((lane >= left) & (lane < right), scale * a[at:at + 1, :], 0.0)
    fresh = w[0:lines, :]
    store_flat(layout, fresh_ref, fresh)
    store_flat(layout, low_ref, fresh)


def update(layout, utterances, g, optimizer, info):
    part, lines, count = layout.part, layout.lines, len(layout.widths)
    loss, clip, *rest = pl.pallas_call(
        functools.partial(update_kernel, layout, utterances),
        out_shape=[shape(1), shape(1), shape(part), shape(part), shape(part), shape(part, dtype=BF), shape(count), shape(count)],
        in_specs=[VM] * 5,
        out_specs=[SM, SM] + [VM] * 6,
        scratch_shapes=[pltpu.VMEM((lines, 128), F32)] * 3,
        name="update",
        compiler_params=pltpu.CompilerParams(vmem_limit_bytes=VMEM_LIMIT),
    )(g, *optimizer, info)
    return (loss[0], clip[0], *rest)


def solution(mesh):
    n_bucket, n_dp = mesh.shape["bucket"], mesh.shape["dp"]
    geo = Geometry(n_bucket, n_dp)

    def body(filter_bank, frame_len, tok_len, targets, *rest):
        weights, optimizer = rest[:13], rest[13:]
        utterances = frame_len.shape[0] * n_bucket * n_dp
        plan, *rest = front(geo, n_bucket, utterances, filter_bank, frame_len, tok_len, targets, weights)
        layout = Layout(plan, geo, [w.size for w in weights])
        out, info = tail(geo, plan, layout, utterances, *rest, optimizer)
        if geo.share == 1:
            return update(layout, utterances, out, optimizer, info)
        g = layout.in_xla(out, lax.axis_index("bucket"), lax.axis_index("dp"), n_dp)
        info = pl.pallas_call(
            functools.partial(norm_kernel, geo, layout),
            out_shape=shape(8, 128), in_specs=[VM] * 5, out_specs=VM, scratch_shapes=norm_scratch(geo, plan, layout), name="norms",
            compiler_params=pltpu.CompilerParams(vmem_limit_bytes=VMEM_LIMIT, collective_id=2, has_side_effects=True),
        )(g, *optimizer, info)
        return update(layout, utterances, g, optimizer, info)

    both = P(("bucket", "dp"))
    in_specs = (P(("bucket", "dp"), None, None), both, both, P(("bucket", "dp"), None)) + (P(),) * 13 + (both,) * 3
    out_specs = (P(), P(), both, both, both, both, P(), P())
    return jax.shard_map(body, mesh=mesh, in_specs=in_specs, out_specs=out_specs, check_vma=False)
```

```python
import functools
import math

import jax
import jax.numpy as jnp
import numpy as np
from jax import lax
from jax.experimental import pallas as pl
from jax.experimental.pallas import tpu as pltpu
from jax.sharding import PartitionSpec as P

HEADS = 4
STEP = 5
GROUPS = 32
BF = jnp.bfloat16
F32 = jnp.float32
NEG_SCORE = -1e9
NEG_PATH = -1e5
FLOOR = -1e30
LOG2E = 1.4426950408889634
VMEM_LIMIT = 63 * 2**20


def dot(a, b):
    return lax.dot_general(a, b, (((1,), (0,)), ((), ())), preferred_element_type=F32)


def dot_rt(a, b):
    return lax.dot_general(a, b, (((1,), (1,)), ((), ())), preferred_element_type=F32)


def dot_lt(a, b):
    return lax.dot_general(a, b, (((0,), (0,)), ((), ())), preferred_element_type=F32)


def halves(value):
    high = value.astype(BF)
    return high, (value - high.astype(F32)).astype(BF)


def iota(shape, dim):
    return lax.broadcasted_iota(jnp.int32, shape, dim)


def normalised(x):
    mean = jnp.mean(x, axis=-1, keepdims=True)
    centre = x - mean
    rstd = lax.rsqrt(jnp.mean(centre * centre, axis=-1, keepdims=True) + 1e-05)
    return centre * rstd, rstd


def norm_back(dy, unit, rstd, gain):
    dunit = dy * gain
    dx = rstd * (
        dunit
        - jnp.mean(dunit, axis=-1, keepdims=True)
        - unit * jnp.mean(dunit * unit, axis=-1, keepdims=True)
    )
    return dx, jnp.sum(dy * unit, axis=0, keepdims=True), jnp.sum(dy, axis=0, keepdims=True)


def softmax(scores):
    shifted = scores - jnp.max(scores, axis=-1, keepdims=True)
    e = jnp.exp(shifted)
    return e * (1.0 / jnp.sum(e, axis=-1, keepdims=True))


def head_mask(width, h):
    size = width // HEADS
    lane = iota((1, width), 1)
    return (lane >= h * size) & (lane < (h + 1) * size)


def pick_head(value, h):
    return jnp.where(head_mask(value.shape[-1], h), value, jnp.zeros((), value.dtype))


def attend(q, k, v, allowed):
    scale = 1.0 / math.sqrt(q.shape[-1] // HEADS)
    total = None
    for h in range(HEADS):
        s = jnp.where(allowed, dot_rt(q, pick_head(k, h)) * scale, NEG_SCORE)
        c = dot(softmax(s).astype(BF), pick_head(v, h))
        total = c if total is None else total + c
    return total


def attend_back(q, k, v, allowed, dctx):
    scale = 1.0 / math.sqrt(q.shape[-1] // HEADS)
    dq = dk = dv = None
    for h in range(HEADS):
        kh, vh = pick_head(k, h), pick_head(v, h)
        p = softmax(jnp.where(allowed, dot_rt(q, kh) * scale, NEG_SCORE))
        dvh = dot_lt(p.astype(BF), pick_head(dctx, h))
        dp = dot_rt(dctx, vh)
        ds = p * (dp - jnp.sum(p * dp, axis=-1, keepdims=True))
        ds = jnp.where(allowed, ds, 0.0).astype(BF)
        dqh = dot(ds, kh)
        dkh = dot_lt(ds, pick_head(q, h))
        if dq is None:
            dq, dk, dv = dqh, dkh, dvh
        else:
            dq, dk, dv = dq + dqh, dk + dkh, dv + dvh
    return dq * scale, dk * scale, dv


def spans(total, size):
    return [(at, min(size, total - at)) for at in range(0, total, size)]


def put8(ref, base, value, first=0):
    rows, width = value.shape
    deep = rows // GROUPS
    if width % 128:
        value = jnp.pad(value, ((0, 0), (0, 128 - width % 128)))
    for c in range(first, value.shape[1] // 128):
        at = base + deep * c
        ref[:, at:at + deep, :] = value[:, 128 * c:128 * (c + 1)].reshape(GROUPS, deep, 128)


def put_rows(ref, base, value, row, rows):
    deep = rows // GROUPS
    count = value.shape[0] // deep
    for c in range(value.shape[1] // 128):
        at = base + deep * c
        ref[row // deep:row // deep + count, at:at + deep, :] = value[:, 128 * c:128 * (c + 1)].reshape(count, deep, 128)


def put_small(ref, row, value):
    width = value.shape[1]
    part = 7 * width // GROUPS
    line = jnp.concatenate([value[i:i + 1, :] for i in range(8)], axis=1)
    for q in range(GROUPS):
        ref[q, row:row + 1, :] = line[:, part * q:part * q + 128]


def token_line(ref):
    return jnp.concatenate([ref[u:u + 1, :] for u in range(ref.shape[0])], axis=1)


def scalar_line(plan, ref):
    owner = iota((1, plan.drows), 1) // plan.tokens
    line = jnp.zeros((1, plan.drows), jnp.int32)
    for u in range(plan.utts):
        line = jnp.where(owner == u, ref[u], line)
    return line


def columns(lines):
    n = lines[0].shape[1]
    block = jnp.concatenate(lines + [jnp.zeros((8 - len(lines), n), lines[0].dtype)], axis=0)
    turned = block.T
    return [turned[:, i:i + 1] for i in range(len(lines))]


class Plan:
    def __init__(self, utts, frames, n_bucket, tokens, width, ff, vocab, feat):
        self.utts, self.frames, self.tokens = utts, frames, tokens
        self.width, self.ff, self.vocab = width, ff, vocab
        if utts % n_bucket == 0:
            self.caps = [frames * (i % n_bucket + 1) // n_bucket for i in range(utts)]
        else:
            self.caps = [frames] * utts
        self.starts = [sum(self.caps[:i]) for i in range(utts)]
        self.rows = sum(self.caps)
        self.drows = utts * tokens
        self.chunk = 1024 if self.rows <= 768 else 512
        self.embed_rows = -(-(vocab // GROUPS + 2) // 16) * 16
        tiles = -(-vocab // 128)
        deep = width // GROUPS
        self.out_rows = tiles * deep
        attn, ff = 4 * width // 128 * deep, ff // 128 * deep
        embed = self.embed_rows * width // 128
        ends = np.cumsum([0, ff, ff, attn, attn])
        self.dec_at, self.dec_rows = [int(x) for x in ends[:-1]], int(ends[-1])
        self.embed_lines = embed
        self.ctc_rows = (tiles + 2) * deep
        self.sub_rows = -(-(feat // GROUPS) // 8) * 8
        ends = np.cumsum([16, ff, ff, attn, self.sub_rows * width // 128])
        self.enc_at, self.enc_rows = [int(x) for x in ends[:-1]], int(ends[-1])


def enc_fwd_part(plan, tick, len_ref, fb_ref, pe_ref, w_sub, w_attn, w_ff1, w_ff2, gain, bias,
                   h0_ref, qkv_ref, ctx_ref, h1_ref, h2_ref, enc_ref):
    d = plan.width
    gain, bias = gain[...].astype(F32), bias[...].astype(F32)
    for u in range(plan.utts):
        t, at = plan.caps[u], plan.starts[u]
        h0_ref[at:at + t, :] = dot_lt(fb_ref[u, :, 0:t], w_sub[...]) + pe_ref[0:t, :]
    unit, _ = normalised(h0_ref[...])
    a0 = (unit * gain[0:1, :] + bias[0:1, :]).astype(BF)
    qkv_ref[...] = dot(a0, w_attn[:, : 3 * d]).astype(BF)
    for u in range(plan.utts):
        t, at = plan.caps[u], plan.starts[u]
        allowed = iota((1, t), 1) < len_ref[u]
        piece = qkv_ref[at:at + t, :]
        ctx = attend(piece[:, :d], piece[:, d:2 * d], piece[:, 2 * d:], allowed)
        ctx_ref[at:at + t, :] = ctx.astype(BF)
    h1 = h0_ref[...] + dot(ctx_ref[...], w_attn[:, 3 * d:])
    h1_ref[...] = h1
    tick("encoder feed")
    unit, _ = normalised(h1)
    a1 = (unit * gain[1:2, :] + bias[1:2, :]).astype(BF)
    h2_ref[...] = h1
    for c, size in spans(plan.ff, plan.chunk // 2):
        inner = dot(a1, w_ff1[:, c:c + size])
        act = (inner * jax.nn.sigmoid(inner)).astype(BF)
        h2_ref[...] += dot(act, w_ff2[c:c + size, :])
    unit, _ = normalised(h2_ref[...])
    enc_ref[...] = (unit * gain[2:3, :] + bias[2:3, :]).astype(BF)


def enc_bwd_part(plan, tick, len_ref, fb_ref, perm_ref, w_attn, w_ff1, w_ff2, gain, bias,
                   h0_ref, qkv_ref, ctx_ref, h1_ref, h2_ref, denc_ref,
                   gg_dec, gb_dec, g_ref, dh_ref, db_ref, dqkv_ref):
    gain, bias = gain[...].astype(F32), bias[...].astype(F32)
    d, deep = plan.width, plan.width // GROUPS
    at_ff2, at_ff1, at_attn, at_sub = plan.enc_at
    g_ref[:, 0:16, :] = jnp.zeros((GROUPS, 16, 128), F32)
    denc = denc_ref[...].astype(BF).astype(F32)
    unit, rstd = normalised(h2_ref[...])
    dh2, gg2, gb2 = norm_back(denc, unit, rstd, gain[2:3, :])
    dh_ref[...] = dh2
    dout = dh2.astype(BF)
    unit1, rstd1 = normalised(h1_ref[...])
    a1 = (unit1 * gain[1:2, :] + bias[1:2, :]).astype(BF)
    for c, size in spans(plan.ff, plan.chunk // 2):
        inner = dot(a1, w_ff1[:, c:c + size])
        sig = jax.nn.sigmoid(inner)
        act = inner * sig
        put_rows(g_ref, at_ff2, dot_lt(act.astype(BF), dout), c, plan.ff)
        dact = dot_rt(dout, w_ff2[c:c + size, :])
        dinner = (dact * (sig + act * (1.0 - sig))).astype(BF)
        put8(g_ref, at_ff1 + c // 128 * deep, dot_lt(a1, dinner))
        part = dot_rt(dinner, w_ff1[:, c:c + size])
        if c == 0:
            db_ref[...] = part
        else:
            db_ref[...] += part
        if (c + size) % 512 == 0:
            tick("ff%d" % ((c + size - 1) // 512))
    dx, gg1, gb1 = norm_back(db_ref[...], unit1, rstd1, gain[1:2, :])
    dh1 = dh_ref[...] + dx
    dh_ref[...] = dh1
    dout = dh1.astype(BF)
    put8(g_ref, at_attn + 3 * d // 128 * deep, dot_lt(ctx_ref[...], dout))
    dctx = dot_rt(dout, w_attn[:, 3 * d:]).astype(BF)
    tick("out")
    for u in range(plan.utts):
        t, at = plan.caps[u], plan.starts[u]
        allowed = iota((1, t), 1) < len_ref[u]
        piece = qkv_ref[at:at + t, :]
        dq, dk, dv = attend_back(piece[:, :d], piece[:, d:2 * d], piece[:, 2 * d:], allowed, dctx[at:at + t, :])
        dqkv_ref[at:at + t, :d] = dq.astype(BF)
        dqkv_ref[at:at + t, d:2 * d] = dk.astype(BF)
        dqkv_ref[at:at + t, 2 * d:] = dv.astype(BF)
        tick("attn%d" % u)
    unit, rstd = normalised(h0_ref[...])
    a0 = (unit * gain[0:1, :] + bias[0:1, :]).astype(BF)
    dqkv = dqkv_ref[...]
    put8(g_ref, at_attn, dot_lt(a0, dqkv))
    da0 = dot_rt(dqkv, w_attn[:, :3 * d])
    dx, gg0, gb0 = norm_back(da0, unit, rstd, gain[0:1, :])
    dh0 = (dh_ref[...] + dx).astype(BF)
    g = None
    for u in range(plan.utts):
        t, at = plan.caps[u], plan.starts[u]
        part = dot(fb_ref[u, :, 0:t], dh0[at:at + t, :])
        g = part if g is None else g + part
    high, low = halves(g)
    lower = (g - high.astype(F32) - low.astype(F32)).astype(BF)
    perm = perm_ref[...]
    put_rows(g_ref, at_sub, dot(perm, high) + dot(perm, low) + dot(perm, lower), 0, perm.shape[0])
    put_small(g_ref, 0, gg_dec[...] + jnp.concatenate([gg0, gg1, gg2, jnp.zeros((5, d), F32)], axis=0))
    put_small(g_ref, 1, gb_dec[...] + jnp.concatenate([gb0, gb1, gb2, jnp.zeros((5, d), F32)], axis=0))


def source_masks(plan, len_ref):
    rows = plan.drows
    row, col = iota((rows, rows), 0), iota((rows, rows), 1)
    causal = (row // plan.tokens == col // plan.tokens) & (col <= row)
    owner = iota((rows, 1), 0) // plan.tokens
    frame = iota((1, plan.rows), 1)
    valid = None
    for u in range(plan.utts):
        here = (owner == u) & (frame >= plan.starts[u]) & (frame < plan.starts[u] + len_ref[u])
        valid = here if valid is None else valid | here
    return causal, valid


def input_tokens(plan, target_ref):
    spot = iota((1, plan.drows), 1) % plan.tokens
    return jnp.where(spot == 0, plan.vocab - 1, pltpu.roll(token_line(target_ref), 1, 1))


def keep_shapes(plan):
    line, d = plan.drows, plan.width
    return [shape(line, d)] * 4 + [shape(line, 3 * d, dtype=BF)] + [shape(line, d, dtype=BF)] * 3 + [shape(plan.rows, 2 * d, dtype=BF)]


def dec_fwd_part(plan, utterances, tick, len_ref, count_ref, target_ref, pe_ref, enc_ref, w_self, w_cross, w_ff1,
                 w_ff2, embed, w_out, gain, bias, loss_ref, g_ref, g_gain, g_bias, keep):
    y0_ref, y1_ref, y2_ref, dy_ref, mixed_ref, ctx_ref, cctx_ref, cq_ref, kv_ref = keep
    d, rows, vocab = plan.width, plan.drows, plan.vocab
    deep = d // GROUPS
    gain, bias = gain[...].astype(F32), bias[...].astype(F32)
    line, counts = token_line(target_ref), scalar_line(plan, count_ref)
    spot = iota((1, rows), 1) % plan.tokens
    toks = input_tokens(plan, target_ref)
    tick("decoder")
    tok, want, live = columns([toks, jnp.where(spot == counts, vocab - 1, line), jnp.where(spot <= counts, 1, 0)])
    live = live.astype(F32)
    chunks = spans(vocab, 1024)
    place = iota((1, 1024), 1)
    y = None
    for c, size in chunks:
        hot = jnp.where(tok == place[:, :size] + c, 1.0, 0.0).astype(BF)
        part = dot(hot, embed[c:c + size, :])
        y = part if y is None else y + part
    y0 = y * math.sqrt(d) + pe_ref[...]
    y0_ref[...] = y0
    causal, valid = source_masks(plan, len_ref)
    tick("self")
    unit3, rstd3 = normalised(y0)
    a3 = (unit3 * gain[3:4, :] + bias[3:4, :]).astype(BF)
    mixed = dot(a3, w_self[:, : 3 * d]).astype(BF)
    mixed_ref[...] = mixed
    q, k, v = mixed[:, :d], mixed[:, d:2 * d], mixed[:, 2 * d:]
    ctx = attend(q, k, v, causal).astype(BF)
    ctx_ref[...] = ctx
    y1 = y0 + dot(ctx, w_self[:, 3 * d:])
    y1_ref[...] = y1
    tick("cross")
    unit4, rstd4 = normalised(y1)
    a4 = (unit4 * gain[4:5, :] + bias[4:5, :]).astype(BF)
    cq = dot(a4, w_cross[:, :d]).astype(BF)
    kv_ref[...] = dot(enc_ref[...], w_cross[:, d:3 * d]).astype(BF)
    cq_ref[...] = cq
    ck, cv = kv_ref[:, :d], kv_ref[:, d:]
    cctx = attend(cq, ck, cv, valid).astype(BF)
    cctx_ref[...] = cctx
    y2 = y1 + dot(cctx, w_cross[:, 3 * d:])
    y2_ref[...] = y2
    tick("feed")
    unit5, rstd5 = normalised(y2)
    a5 = (unit5 * gain[5:6, :] + bias[5:6, :]).astype(BF)
    y3 = y2
    for c, size in spans(plan.ff, 1024):
        inner = dot(a5, w_ff1[:, c:c + size])
        act = (inner * jax.nn.sigmoid(inner)).astype(BF)
        y3 = y3 + dot(act, w_ff2[c:c + size, :])
    unit6, rstd6 = normalised(y3)
    a6 = (unit6 * gain[6:7, :] + bias[6:7, :]).astype(BF)
    tick("head")
    peak = jnp.full((rows, 1), FLOOR, F32)
    mass = jnp.zeros((rows, 1), F32)
    picked = jnp.zeros((rows, 1), F32)
    summed = jnp.zeros((rows, 1), F32)
    for c, size in chunks:
        z = dot_rt(a6, w_out[c:c + size, :])
        top = jnp.maximum(peak, jnp.max(z, axis=-1, keepdims=True))
        mass = mass * jnp.exp(peak - top) + jnp.sum(jnp.exp(z - top), axis=-1, keepdims=True)
        peak = top
        picked = picked + jnp.sum(jnp.where(want == place[:, :size] + c, z, 0.0), axis=-1, keepdims=True)
        summed = summed + jnp.sum(z, axis=-1, keepdims=True)
    lse = peak + jnp.log(mass)
    rest = 0.1 / (vocab - 1)
    others = (summed - vocab * lse) - (picked - lse)
    per_token = -(0.9 * (picked - lse) + rest * others)
    loss_ref[...] = jnp.full((8, 128), 0.7 * jnp.sum(live * per_token), F32)
    weight = live * (0.7 / utterances)
    da6 = None
    for c, size in chunks:
        z = dot_rt(a6, w_out[c:c + size, :])
        share = jnp.exp(z - lse) * (0.9 + rest * (vocab - 1))
        dz = share - jnp.where(want == place[:, :size] + c, 0.9, rest)
        dz = (dz * weight).astype(BF)
        put8(g_ref, c // 128 * deep, dot_lt(a6, dz))
        if c == 2048:
            tick("head half")
        part = dot(dz, w_out[c:c + size, :])
        da6 = part if da6 is None else da6 + part
    dy, gg6, gb6 = norm_back(da6, unit6, rstd6, gain[6:7, :])
    dy_ref[...] = dy
    g_gain[...] = jnp.concatenate([jnp.zeros((6, d), F32), gg6, jnp.zeros((1, d), F32)], axis=0)
    g_bias[...] = jnp.concatenate([jnp.zeros((6, d), F32), gb6, jnp.zeros((1, d), F32)], axis=0)
    tick("head back")


def dec_bwd_part(plan, tick, len_ref, target_ref, enc_ref, w_self, w_cross, w_ff1, w_ff2, gain, bias, keep,
                 g_ref, g_gain, g_bias, denc_ref):
    y0_ref, y1_ref, y2_ref, dy_ref, mixed_ref, ctx_ref, cctx_ref, cq_ref, kv_ref = keep
    d = plan.width
    deep = d // GROUPS
    at_ff1, at_ff2, at_cross, at_self = plan.dec_at
    gain, bias = gain[...].astype(F32), bias[...].astype(F32)
    causal, valid = source_masks(plan, len_ref)
    unit5, rstd5 = normalised(y2_ref[...])
    a5 = (unit5 * gain[5:6, :] + bias[5:6, :]).astype(BF)
    unit4, rstd4 = normalised(y1_ref[...])
    a4 = (unit4 * gain[4:5, :] + bias[4:5, :]).astype(BF)
    unit3, rstd3 = normalised(y0_ref[...])
    a3 = (unit3 * gain[3:4, :] + bias[3:4, :]).astype(BF)
    dy = dy_ref[...]
    dout = dy.astype(BF)
    da5 = None
    for c, size in spans(plan.ff, 1024):
        inner = dot(a5, w_ff1[:, c:c + size])
        sig = jax.nn.sigmoid(inner)
        act = inner * sig
        put_rows(g_ref, at_ff2, dot_lt(act.astype(BF), dout), c, plan.ff)
        dact = dot_rt(dout, w_ff2[c:c + size, :])
        dinner = (dact * (sig + act * (1.0 - sig))).astype(BF)
        put8(g_ref, at_ff1 + c // 128 * deep, dot_lt(a5, dinner))
        part = dot_rt(dinner, w_ff1[:, c:c + size])
        da5 = part if da5 is None else da5 + part
        tick("dff%d" % (c // 1024))
    dx, gg5, gb5 = norm_back(da5, unit5, rstd5, gain[5:6, :])
    dy = dy + dx
    tick("cross")
    cctx, cq, ck, cv = cctx_ref[...], cq_ref[...], kv_ref[:, :d], kv_ref[:, d:]
    dout = dy.astype(BF)
    tile = d // 128 * deep
    put8(g_ref, at_cross + 3 * tile, dot_lt(cctx, dout))
    dctx = dot_rt(dout, w_cross[:, 3 * d:]).astype(BF)
    dq, dk, dv = attend_back(cq, ck, cv, valid, dctx)
    dq, dk, dv = dq.astype(BF), dk.astype(BF), dv.astype(BF)
    enc = enc_ref[...]
    put8(g_ref, at_cross + tile, dot_lt(enc, dk))
    put8(g_ref, at_cross + 2 * tile, dot_lt(enc, dv))
    denc_ref[...] = dot_rt(dk, w_cross[:, d:2 * d]) + dot_rt(dv, w_cross[:, 2 * d:3 * d])
    put8(g_ref, at_cross, dot_lt(a4, dq))
    da4 = dot_rt(dq, w_cross[:, :d])
    dx, gg4, gb4 = norm_back(da4, unit4, rstd4, gain[4:5, :])
    dy = dy + dx
    tick("self")
    ctx, mixed = ctx_ref[...], mixed_ref[...]
    q, k, v = mixed[:, :d], mixed[:, d:2 * d], mixed[:, 2 * d:]
    dout = dy.astype(BF)
    put8(g_ref, at_self + 3 * tile, dot_lt(ctx, dout))
    dctx = dot_rt(dout, w_self[:, 3 * d:]).astype(BF)
    dq, dk, dv = attend_back(q, k, v, causal, dctx)
    dq, dk, dv = dq.astype(BF), dk.astype(BF), dv.astype(BF)
    put8(g_ref, at_self, dot_lt(a3, dq))
    put8(g_ref, at_self + tile, dot_lt(a3, dk))
    put8(g_ref, at_self + 2 * tile, dot_lt(a3, dv))
    da3 = dot_rt(dq, w_self[:, :d]) + dot_rt(dk, w_self[:, d:2 * d]) + dot_rt(dv, w_self[:, 2 * d:3 * d])
    dx, gg3, gb3 = norm_back(da3, unit3, rstd3, gain[3:4, :])
    tick("dself")
    g_gain[...] += jnp.concatenate([jnp.zeros((3, d), F32), gg3, gg4, gg5, jnp.zeros((2, d), F32)], axis=0)
    g_bias[...] += jnp.concatenate([jnp.zeros((3, d), F32), gb3, gb4, gb5, jnp.zeros((2, d), F32)], axis=0)
    return ((dy + dx) * math.sqrt(d)).astype(BF)


def ctc_part(plan, utterances, tick, len_ref, count_ref, target_ref, enc_ref, w_ref,
             g_ref, denc_ref,
             peak_ref, mass_ref, sel_ref, em_ref, cum_ref, alpha_ref, beta_ref, gam_hi, gam_lo):
    d, vocab, frames, toks = plan.width, plan.vocab, plan.frames, plan.tokens
    lanes, deep = plan.drows, d // GROUPS
    g_ref[:, deep:2 * deep, :] = jnp.zeros((GROUPS, deep, 128), F32)
    g_ref[:, plan.ctc_rows - deep:, :] = jnp.zeros((GROUPS, deep, 128), F32)
    chunks = spans(vocab, plan.chunk)
    place = iota((1, plan.chunk), 1)
    line, counts, lens = token_line(target_ref), scalar_line(plan, count_ref), scalar_line(plan, len_ref)
    (labels,) = columns([line])
    enc = enc_ref[...]
    peak = jnp.full((plan.rows, 1), FLOOR, F32)
    mass = jnp.zeros((plan.rows, 1), F32)
    sel_ref[...] = jnp.zeros((lanes, d), F32)
    blank = None
    for c, size in chunks:
        wc = w_ref[c:c + size, :]
        z = dot_rt(enc, wc)
        if c == 0:
            blank = z[:, 0:1]
        top = jnp.maximum(peak, jnp.max(z, axis=-1, keepdims=True))
        mass = mass * jnp.exp(peak - top) + jnp.sum(jnp.exp(z - top), axis=-1, keepdims=True)
        peak = top
        hot = jnp.where(labels == place[:, :size] + c, 1.0, 0.0).astype(BF)
        sel_ref[...] += dot(hot, wc)
        if (c + size) % 1024 == 0 or c + size == vocab:
            tick("first%d" % ((c + size - 1) // 1024))
    lse = peak + jnp.log(mass)
    peak_ref[:, 0:1] = lse
    tick("prep")
    lane = iota((1, lanes), 1)
    sel = sel_ref[...].astype(BF)
    em_ref[...] = jnp.zeros((frames, lanes), F32)
    mass_ref[...] = jnp.zeros((frames, lanes), F32)
    for u in range(plan.utts):
        t, at = plan.caps[u], plan.starts[u]
        mine = lane // toks == u
        z = dot_rt(enc[at:at + t, :], sel)
        em_ref[0:t, :] += jnp.where(mine, (z - blank[at:at + t, :]) * LOG2E, 0.0)
        mass_ref[0:t, :] += jnp.where(mine, (blank[at:at + t, :] - lse[at:at + t, :]) * LOG2E, 0.0)
    lower = jnp.where(iota((frames, frames), 0) >= iota((frames, frames), 1), 1.0, 0.0).astype(BF)
    drift = mass_ref[...]
    high, mid = halves(drift)
    low = (drift - high.astype(F32) - mid.astype(F32)).astype(BF)
    total = dot(lower, high) + dot(lower, mid) + dot(lower, low)
    neg = NEG_PATH * LOG2E
    cum_ref[...] = neg - total
    skip = ((line != pltpu.roll(line, 1, 1)) & (lane % toks > 0)).astype(jnp.int32)
    skip_next = ((line != pltpu.roll(line, lanes - 1, 1)) & (lane % toks < toks - 1)).astype(jnp.int32)
    first, ending = lane % toks == 0, lane % toks == counts - 1
    end_frame = lens - 1
    step8, lane8 = iota((8, 128), 0), iota((8, 128), 1) % toks
    first8, final8 = lane8 == step8, lane8 + 7 - step8 == toks - 1

    def spread(row, shift):
        return pltpu.roll(jnp.broadcast_to(row, (8, 128)), shift, 1, stride=1, stride_axis=0)

    def log_sum(a, b, c):
        top = jnp.maximum(jnp.maximum(b, c), a)
        return top, jnp.log2(jnp.exp2(a - top) + jnp.exp2(b - top) + jnp.exp2(c - top))

    def log_pair(a, b):
        top = jnp.maximum(a, b)
        return top + jnp.log2(jnp.exp2(a - top) + jnp.exp2(b - top))

    cuts = [slice(at, at + 128) for at in range(0, lanes, 128)]
    skip8 = [spread(skip[:, cut], 0) > 0 for cut in cuts]
    skip_next8 = [spread(skip_next[:, cut], 121) > 0 for cut in cuts]
    begin8 = [jnp.where(spread(ending[:, cut].astype(jnp.int32), 121) > 0, 0.0, FLOOR) for cut in cuts]
    fill0 = cum_ref[0:1, :]

    def block(i, carry):
        at, back = pl.multiple_of(8 * i, 8), pl.multiple_of(frames - 8 - 8 * i, 8)
        out = []
        for g, cut in enumerate(cuts):
            la, ba, lb, bb = carry[4 * g:4 * g + 4]
            right, left = spread(la, 1), spread(lb, 120)
            la, ba, lb, bb = spread(la, 0), spread(ba, 0), spread(lb, 121), spread(bb, 121)
            ahead, behind = em_ref[pl.ds(at, 8), cut], em_ref[pl.ds(back, 8), cut]
            fills = cum_ref[pl.ds(at, 8), cut]
            fill = cum_ref[pl.ds(pl.multiple_of(jnp.maximum(at - 8, 0), 8), 8), cut][7:8, :]
            alphas, blanks, betas = (jnp.zeros((8, 128), F32),) * 3
            for k in range(8):
                shifted = jnp.where(first8, fill, right if k == 0 else pltpu.roll(la, 7, 0))
                e = spread(ahead[k:k + 1, :], 0)
                top, rest = log_sum(la, ba, jnp.where(skip8[g], shifted, fill))
                la2 = (top + e) + rest
                top, rest = log_sum(shifted, ba, fill)
                ba2 = top + rest
                if k == 0:
                    start = i == 0
                    la2 = jnp.where(start, jnp.where(first8, e, fill0[:, cut]), la2)
                    ba2 = jnp.where(start, jnp.where(first8, 0.0, fill0[:, cut]), ba2)
                la, ba = la2, ba2
                alphas = jnp.where(step8 == k, la[0:1, :], alphas)
                blanks = jnp.where(step8 == k, ba[0:1, :], blanks)
                fill = fills[k:k + 1, :]
                e = spread(behind[7 - k:8 - k, :], 121)
                shifted = jnp.where(final8, FLOOR, left if k == 0 else pltpu.roll(lb, 1, 0))
                top, rest = log_sum(lb, bb, jnp.where(skip_next8[g], shifted, FLOOR))
                begin = end_frame[:, cut] == back + 7 - k
                bb = jnp.where(begin, begin8[g], log_pair(bb, shifted))
                lb = jnp.where(begin, begin8[g] + e, (top + e) + rest)
                betas = jnp.where(step8 == 7 - k, lb[7:8, :], betas)
            alpha_ref[pl.ds(at, 8), cut], mass_ref[pl.ds(at, 8), cut] = alphas, blanks
            beta_ref[pl.ds(back, 8), cut] = betas
            out += [la[0:1, :], ba[0:1, :], lb[7:8, :], bb[7:8, :]]
        return tuple(out)

    carry = (jnp.full((1, 128), FLOOR, F32),) * (4 * len(cuts))
    for i, (at, size) in enumerate(spans(frames // 8, frames // 64)):
        carry = lax.fori_loop(at, at + size, block, carry)
        tick("scan%d" % i)
    moment = iota((frames, lanes), 0)
    la, ba = [jnp.sum(jnp.where(moment == end_frame, ref[...], 0.0), axis=0, keepdims=True) for ref in (alpha_ref, mass_ref)]
    after = jnp.where(first, FLOOR, pltpu.roll(jnp.where(ending, 0.0, FLOOR), 1, 1))
    at_end = jnp.sum(jnp.where(moment == end_frame, neg - cum_ref[...], 0.0), axis=0, keepdims=True)
    floor = NEG_PATH * 10.0 * LOG2E - at_end
    tail = jnp.maximum(jnp.where(ending, la, FLOOR), jnp.where(after == 0.0, ba, FLOOR))
    logz = jnp.zeros((1, lanes), F32)
    ctc = jnp.zeros((), F32)
    for u in range(plan.utts):
        mine = lane // toks == u
        top = jnp.max(jnp.where(mine, tail, FLOOR), axis=-1, keepdims=True)
        bottom = jnp.max(jnp.where(mine, floor, FLOOR), axis=-1, keepdims=True)
        top = jnp.maximum(top, bottom)
        weight = jnp.where(mine & ending, jnp.exp2(la - top), 0.0) + jnp.where(mine & (after == 0.0), jnp.exp2(ba - top), 0.0)
        full = top + jnp.log2(jnp.sum(weight, axis=-1, keepdims=True) + jnp.exp2(bottom - top))
        logz = jnp.where(mine, full, logz)
        drift_end = jnp.max(jnp.where(mine, at_end, FLOOR), axis=-1, keepdims=True)
        ctc = ctc - jnp.sum(full + drift_end) / LOG2E
    gamma = jnp.exp2(alpha_ref[...] + beta_ref[...] - em_ref[...] - logz)
    gamma = jnp.where(moment <= end_frame, gamma, 0.0)
    for u in range(plan.utts):
        t, at = plan.caps[u], plan.starts[u]
        mine = lane // toks == u
        piece = jnp.where(mine, gamma[0:t, :], 0.0)
        high, low = halves(piece)
        gam_hi[at:at + t, :] = high
        gam_lo[at:at + t, :] = low
        alive = jnp.where(iota((t, 1), 0) < len_ref[u], 1.0, 0.0)
        peak_ref[at:at + t, 1:2] = alive
        peak_ref[at:at + t, 2:3] = alive - jnp.sum(piece, axis=-1, keepdims=True)
    lse = peak_ref[:, 0:1]
    scale = 0.3 / utterances
    live = peak_ref[:, 1:2] * scale
    blank_share = peak_ref[:, 2:3]
    for c, size in chunks:
        wc = w_ref[c:c + size, :]
        p = jnp.exp(dot_rt(enc, wc) - lse) * live
        hot = jnp.where(labels == place[:, :size] + c, 1.0, 0.0).astype(BF)
        post = dot(gam_hi[...], hot) + dot(gam_lo[...], hot)
        dz = p - post * scale
        if c == 0:
            dz = dz - jnp.where(place[:, :size] == 0, blank_share * scale, 0.0)
        dz = dz.astype(BF)
        value = dot_lt(enc, dz)
        if c == 0:
            g_ref[:, 0:deep, :] = value[:, :128].reshape(GROUPS, deep, 128)
        put8(g_ref, deep + c // 128 * deep, value, 1 if c == 0 else 0)
        denc_ref[...] += dot(dz, wc)
        if (c + size) % 1024 == 0 or c + size == vocab:
            tick("second%d" % ((c + size - 1) // 1024))
    return 0.3 * ctc


VM = pl.BlockSpec(memory_space=pltpu.VMEM)
SM = pl.BlockSpec(memory_space=pltpu.SMEM)
ANY = pl.BlockSpec(memory_space=pl.ANY)


def shape(*dims, dtype=F32):
    return jax.ShapeDtypeStruct(dims, dtype)


class Beside:
    def __init__(self, sems):
        self.sems, self.copies = sems, {}

    def start(self, name, source, target):
        copy = pltpu.make_async_copy(source, target, self.sems.at[len(self.copies)])
        self.copies[name] = copy
        copy.start()

    def wait(self, *names):
        for name in names:
            self.copies[name].wait()


class Pair:
    def __init__(self, geo, here, g_ref, recv, out, sems):
        self.geo, self.here, self.g, self.recv, self.out, self.sems = geo, here, g_ref, recv, out, sems

    def copies(self, i, a, b):
        span, at = pl.ds(a, b - a), self.here.at
        return [pltpu.make_async_remote_copy(
            src_ref=self.g.at[2 * y + 1 - at["c"], :, span], dst_ref=self.recv.at[y, :, span],
            send_sem=self.sems.at[0, i, y], recv_sem=self.sems.at[1, i, y],
            device_id=self.here.device("c", 0), device_id_type=MESH) for y in range(self.geo.ny)]

    def keep(self, i, a, b):
        span, at = pl.ds(a, b - a), self.here.at
        return [pltpu.make_async_copy(self.g.at[2 * y + at["c"], :, span], self.out.at[y, :, span], self.sems.at[2, i, y])
                for y in range(self.geo.ny)]

    def start(self, *span):
        for copy in self.copies(*span):
            copy.start()

    def finish(self, i, a, b):
        for copy in self.copies(i, a, b):
            copy.wait()
        many = self.geo.ns * self.geo.gf

        def add(k, carry):
            y, sf = k // many, k % many
            self.g[2 * y + self.here.at["c"], sf, a:b, :] += self.recv[y, sf, a:b, :]
            return carry

        lax.fori_loop(0, self.geo.ny * many, add, 0)
        for copy in self.keep(i, a, b):
            copy.start()

    def end(self, *span):
        for copy in self.keep(*span):
            copy.wait()


def front_kernel(geo, plan, utterances, *refs):
    whole = geo.share > 1
    refs = list(refs)

    def take(count):
        out = refs[:count]
        del refs[:count]
        return out

    len_ref, count_ref, target_ref, bank, pe, pe_tok, w_sub, w_attn, gain, bias = take(10)
    far = take(8)
    h0_out, qkv_out, ctx_out, h1_out, h2_out, pair_out = take(6)
    enc, att, gg, gb = take(4)
    keep = take(9)
    if whole:
        g_out, denc, rows = take(3)
    near = take(8)
    w_ff1, w_ff2, embed, w_self, w_cross, d_ff1, d_ff2, w_out = near
    h0, qkv, ctx, h1, h2 = take(5)
    head, recv, sems, pair_sems = take(4)
    here = Here(geo)
    beside = Beside(sems)
    names = ("ff1", "ff2", "embed", "self", "cross", "dff1", "dff2", "out")
    for name, source, target in zip(names, far, near):
        beside.start(name, source, target)
    barrier = pltpu.get_barrier_semaphore()
    pl.semaphore_signal(barrier, inc=1, device_id=here.device("c", 0), device_id_type=MESH)
    pl.semaphore_wait(barrier, 1)
    pair = Pair(geo, here, head.reshape(2 * geo.ny, geo.ns * geo.gf, plan.out_rows, 128), recv, pair_out, pair_sems)
    cut = plan.out_rows // 32 * 16
    parts = ((0, 0, cut), (1, cut, plan.out_rows))

    def tick(name):
        if name == "encoder feed":
            beside.wait("ff1", "ff2")
        elif name == "decoder":
            for label, source, target in (("h0", h0, h0_out), ("qkv", qkv, qkv_out), ("ctx", ctx, ctx_out), ("h1", h1, h1_out),
                                          ("h2", h2, h2_out)):
                beside.start(label, source, target)
            beside.wait("embed")
        elif name in ("self", "cross"):
            beside.wait(name)
        elif name == "feed":
            beside.wait("dff1", "dff2")
        elif name == "head":
            beside.wait("out")
        elif name == "head half":
            pair.start(*parts[0])
        elif name == "head back":
            pair.start(*parts[1])
            pair.finish(*parts[0])
            pair.finish(*parts[1])

    enc_fwd_part(plan, tick, len_ref, bank, pe, w_sub, w_attn, w_ff1, w_ff2, gain, bias, h0, qkv, ctx, h1, h2, enc)
    dec_fwd_part(plan, utterances, tick, len_ref, count_ref, target_ref, pe_tok, enc, w_self, w_cross, d_ff1, d_ff2, embed, w_out,
                 gain, bias, att, head, gg, gb, keep)
    if whole:
        g_dec = refs[0]
        rows[...] = dec_bwd_part(plan, lambda name: None, len_ref, target_ref, enc, w_self, w_cross, d_ff1, d_ff2, gain, bias, keep,
                                 g_dec, gg, gb, denc)
        beside.start("dec", g_dec, g_out.reshape(GROUPS, plan.dec_rows, 128))
        beside.wait("dec")
    for part in parts:
        pair.end(*part)
    beside.wait("h0", "qkv", "ctx", "h1", "h2")


def positions(length, width):
    place = np.arange(length, dtype=np.float64)[:, None]
    angles = place * np.exp(np.arange(0, width, 2, dtype=np.float64) * (-math.log(10000.0) / width))[None, :]
    return np.stack([np.sin(angles), np.cos(angles)], axis=-1).reshape(length, width).astype(np.float32)


def front(geo, n_bucket, utterances, filter_bank, frame_len, tok_len, targets, weights):
    (w_sub, enc_attn, enc_ff1, enc_ff2, dec_self, dec_cross, dec_ff1, dec_ff2, embed, ctc_head, out_head,
     norm_gain, norm_bias) = weights
    utts, frames, feat = filter_bank.shape
    toks, (vocab, d), ff = targets.shape[1], embed.shape, enc_ff1.shape[1]
    plan = Plan(utts, frames, n_bucket, toks, d, ff, vocab, feat)
    rows, drows, whole = plan.rows, plan.drows, geo.share > 1
    bank = jnp.swapaxes(filter_bank, 1, 2)
    pe = positions(frames, d)
    pe_tok = np.tile(pe[:toks], (utts, 1))
    half = (geo.ny, geo.ns * geo.gf, plan.out_rows, 128)
    far = (enc_ff1, enc_ff2, embed, dec_self, dec_cross, dec_ff1, dec_ff2, out_head.T)
    kept = [shape(rows, d), shape(rows, 3 * d, dtype=BF), shape(rows, d, dtype=BF), shape(rows, d), shape(rows, d)]
    outs = kept + [shape(*half), shape(rows, d, dtype=BF), shape(8, 128), shape(8, d), shape(8, d)] + keep_shapes(plan)
    specs = [ANY] * 6 + [VM] * 13
    scratch = [pltpu.VMEM(x.shape, x.dtype) for x in far + tuple(kept)]
    scratch += [pltpu.VMEM((GROUPS, plan.out_rows, 128), F32), pltpu.VMEM(half, F32), pltpu.SemaphoreType.DMA((14,)),
                pltpu.SemaphoreType.DMA((3, 2, geo.ny))]
    if whole:
        outs += [shape(2 * geo.ny, geo.ns * geo.gf, plan.dec_rows, 128), shape(rows, d), shape(drows, d, dtype=BF)]
        specs += [ANY, VM, VM]
        scratch += [pltpu.VMEM((GROUPS, plan.dec_rows, 128), F32)]
    results = pl.pallas_call(
        functools.partial(front_kernel, geo, plan, utterances),
        out_shape=outs,
        in_specs=[SM] * 2 + [VM] * 8 + [ANY] * 8,
        out_specs=specs,
        scratch_shapes=scratch,
        name="front",
        compiler_params=pltpu.CompilerParams(vmem_limit_bytes=VMEM_LIMIT, collective_id=1, has_side_effects=True),
    )(frame_len, tok_len, targets, bank, jnp.asarray(pe), jnp.asarray(pe_tok), w_sub, enc_attn, norm_gain, norm_bias, *far)
    h0, qkv, ctx, h1, h2, pair, enc, att, gg_dec, gb_dec = results[:10]
    keep, more = results[10:19], results[19:]
    per = feat // GROUPS
    perm = np.zeros((GROUPS * plan.sub_rows, feat), np.float32)
    for r in range(feat):
        perm[r // per * plan.sub_rows + r % per, r] = 1.0
    now = [frame_len, tok_len, targets, enc, norm_gain, norm_bias, gg_dec, gb_dec, att]
    later = [ctc_head.T, bank, jnp.asarray(perm, BF), enc_attn, enc_ff1, enc_ff2, h0, qkv, ctx, h1, h2]
    if whole:
        now += more[1:]
    else:
        now += keep
        later = [dec_ff1, dec_ff2, dec_cross, dec_self] + later
    ctc_scratch = [pltpu.VMEM((rows, 128), F32), pltpu.VMEM((frames, drows), F32), pltpu.VMEM((drows, d), F32)]
    ctc_scratch += [pltpu.VMEM((frames, drows), F32)] * 4 + [pltpu.VMEM((rows, drows), BF)] * 2
    enc_scratch = [pltpu.VMEM((rows, d), F32), pltpu.VMEM((rows, d), F32), pltpu.VMEM((rows, 3 * d), BF)]
    return plan, now, later, [pair] + (list(more[:1]) if whole else []), ctc_scratch, enc_scratch


MESH = pl.DeviceIdType.MESH


class Geometry:
    def __init__(self, n_bucket, n_dp):
        self.ny, self.ns = n_bucket // 2, 4
        self.nf = n_dp // self.ns
        self.share = n_bucket * n_dp // GROUPS
        self.gf = self.nf // self.share
        if self.ny * 2 * self.ns * self.gf != GROUPS:
            raise ValueError("mesh size")

    def size(self, axis):
        return {"c": 2, "y": self.ny, "s": self.ns, "f": self.nf}[axis]


class Here:
    def __init__(self, geo):
        self.geo = geo
        bucket, dp = lax.axis_index("bucket"), lax.axis_index("dp")
        self.at = {"y": bucket // 2, "c": bucket % 2, "s": dp // geo.nf, "f": dp % geo.nf}
        self.devices, self.index = 2 * geo.ny * geo.ns * geo.nf, bucket * geo.ns * geo.nf + dp

    def other(self, index):
        n_dp = self.geo.ns * self.geo.nf
        return (index // n_dp, lax.rem(index, n_dp))

    def step(self, axis, p):
        return lax.rem(self.at[axis] + 1 + p, self.geo.size(axis))

    def device(self, axis, p):
        at = dict(self.at)
        at[axis] = self.step(axis, p)
        return (at["y"] * 2 + at["c"], at["s"] * self.geo.nf + at["f"])

    def greet(self):
        barrier = pltpu.get_barrier_semaphore()
        for p in range(self.devices - 1):
            device = self.other(lax.rem(self.index + 1 + p, self.devices))
            pl.semaphore_signal(barrier, inc=1, device_id=device, device_id_type=MESH)
        pl.semaphore_wait(barrier, self.devices - 1)


class Stream:
    def __init__(self, geo, array, a, b, order, dtype, resident=False, paired=False):
        self.geo, self.array, self.a, self.n, self.order, self.dtype = geo, array, a, b - a, order, dtype
        self.resident, self.paired = resident, paired

    def wire(self, stage, n):
        geo = self.geo
        done = self.order[:stage]
        axis = self.order[stage]
        if axis == "c":
            return (geo.ny, geo.ns * geo.gf, n, 128)
        dims = [size for other, size in (("y", geo.ny), ("s", geo.ns), ("f", geo.gf)) if other not in done and other != axis]
        return tuple(dims) + (n, 128)

    def buffers(self, stage, n):
        if stage == 0:
            return [pltpu.VMEM(self.wire(0, n), F32)]
        return [pltpu.VMEM((self.geo.size(self.order[stage]) - 1,) + self.wire(stage, n), self.dtype)] * 2

    def own(self):
        geo = self.geo
        sems = [pltpu.SemaphoreType.DMA((3, geo.ny))]
        for stage in (1, 2, 3):
            sems += [pltpu.SemaphoreType.DMA((2, geo.size(self.order[stage]) - 1))]
        if self.resident:
            return sems
        return sems + [pltpu.VMEM((geo.ny, geo.ns * geo.gf, self.n, 128), F32)]

    def bind(self, here, g_refs, shared, own, r_ref, r_at):
        self.here, self.g, self.r, self.r_at = here, g_refs[self.array], r_ref, r_at
        rows = pl.ds(0, self.n)
        cut = [[ref.at[(slice(None),) * (len(ref.shape) - 2) + (rows,)] for ref in refs] for refs in shared]
        self.core = None if self.paired else cut[0][0]
        self.send = {stage: cut[stage][0] for stage in (1, 2, 3)}
        self.recv = {stage: cut[stage][1] for stage in (1, 2, 3)}
        self.sems = own[:4]
        self.sums = None if self.resident else own[4]

    def get(self, y, sf):
        if self.resident:
            return self.g[2 * y + self.here.at["c"], sf, self.a:self.a + self.n, :]
        return self.sums[y, sf]

    def put(self, y, sf, value):
        if self.resident:
            self.g[2 * y + self.here.at["c"], sf, self.a:self.a + self.n, :] = value
        else:
            self.sums[y, sf] = value

    def core_copies(self):
        geo, at, sems = self.geo, self.here.at, self.sems[0]
        span = pl.ds(self.a, self.n)
        if self.paired:
            return [pltpu.make_async_copy(self.g.at[y, :, span], self.sums.at[y], sems.at[2, y]) for y in range(geo.ny)]
        copies = [pltpu.make_async_remote_copy(
            src_ref=self.g.at[2 * y + 1 - at["c"], :, span], dst_ref=self.core.at[y],
            send_sem=sems.at[0, y], recv_sem=sems.at[1, y],
            device_id=self.here.device("c", 0), device_id_type=MESH) for y in range(geo.ny)]
        if not self.resident:
            copies += [pltpu.make_async_copy(self.g.at[2 * y + at["c"], :, span], self.sums.at[y], sems.at[2, y])
                       for y in range(geo.ny)]
        return copies

    def wire_copies(self, stage):
        axis, partners = self.order[stage], self.geo.size(self.order[stage]) - 1
        return [pltpu.make_async_remote_copy(
            src_ref=self.send[stage].at[p], dst_ref=self.recv[stage].at[partners - 1 - p],
            send_sem=self.sems[stage].at[0, p], recv_sem=self.sems[stage].at[1, partners - 1 - p],
            device_id=self.here.device(axis, p), device_id_type=MESH) for p in range(partners)]

    def blocks(self, stage):
        geo, at = self.geo, self.here.at
        done = self.order[:stage + 1]
        sizes = [1 if axis in done else size for axis, size in (("y", geo.ny), ("s", geo.ns), ("f", geo.gf))]

        def place(i, swap=None):
            f = i % sizes[2]
            s = i // sizes[2] % sizes[1]
            y = i // (sizes[2] * sizes[1])
            where = {"y": at["y"] if "y" in done else y, "s": at["s"] if "s" in done else s,
                     "f": (at["f"] if "f" in done else f) if geo.gf > 1 else 0}
            if swap is not None and not (swap[0] == "f" and geo.gf == 1):
                where[swap[0]] = swap[1]
            wire = tuple(v for axis, v in (("y", y), ("s", s), ("f", f)) if axis not in done)
            return (where["y"], where["s"] * geo.gf + where["f"]), wire

        return math.prod(sizes), place

    def start(self, stage):
        if stage == 0:
            for copy in self.core_copies():
                copy.start()
            return
        axis = self.order[stage]
        count, place = self.blocks(stage)
        for p, copy in enumerate(self.wire_copies(stage)):
            target = self.here.step(axis, p)

            def fill(i, carry, p=p, target=target):
                at, wire = place(i, (axis, target))
                self.send[stage][(p,) + wire] = self.get(*at).astype(self.dtype)
                return carry

            loop(count, fill)
            copy.start()

    def finish(self, stage):
        if stage == 0:
            for copy in self.core_copies():
                copy.wait()
            if self.paired:
                return
            geo = self.geo

            def add(i, carry):
                y, sf = i // (geo.ns * geo.gf), i % (geo.ns * geo.gf)
                self.put(y, sf, self.get(y, sf) + self.core[y, sf])
                return carry

            loop(geo.ny * geo.ns * geo.gf, add)
            return
        count, place = self.blocks(stage)
        copies = self.wire_copies(stage)
        for copy in copies:
            copy.wait()

        def add(i, carry):
            at, wire = place(i)
            total = self.get(*at)
            for p in range(len(copies)):
                total = total + self.recv[stage][(p,) + wire].astype(F32)
            if stage == 3:
                self.r[self.r_at:self.r_at + self.n, :] = total
            else:
                self.put(*at, total)
            return carry

        loop(count, add)


class RowStream(Stream):
    def __init__(self, geo, plan):
        order = "fycs" if geo.share == 1 else "ycsf"
        super().__init__(geo, -1, 0, plan.embed_lines, order, BF, True)
        self.plan, self.gathers = plan, 3 if geo.share == 1 else 2

    def own(self):
        geo, plan = self.geo, self.plan
        size = [geo.size(axis) - 1 for axis in self.order]
        out = [pltpu.SemaphoreType.DMA((2, count)) for count in size]
        out += [pltpu.VMEM((2, geo.ny, geo.gf, plan.drows + 16, plan.width), BF), pltpu.VMEM((geo.ns, self.n, 128), F32)]
        for stage in range(self.gathers, 4):
            out += [pltpu.VMEM((size[stage],) + self.wire(stage, self.n), BF)] * 2
        return out

    def bind(self, here, own, r_ref, r_at):
        self.here, self.r, self.r_at = here, r_ref, r_at
        self.sems, self.rows, self.block = own[:4], own[4], own[5]
        self.send = {stage: own[6 + 2 * (stage - self.gathers)] for stage in range(self.gathers, 4)}
        self.recv = {stage: own[7 + 2 * (stage - self.gathers)] for stage in range(self.gathers, 4)}

    def get(self, y, sf):
        return self.block[sf // self.geo.gf]

    def put(self, y, sf, value):
        self.block[sf // self.geo.gf] = value

    def fill(self, rows, toks):
        at, geo = self.here.at, self.geo
        mine = (at["c"], at["y"], at["f"] if geo.gf > 1 else 0)
        lines, width = self.plan.drows, self.plan.width
        self.rows[mine + (pl.ds(0, lines), slice(None))] = rows
        ids = jnp.concatenate([toks // 64, lax.rem(toks, 64), jnp.zeros((14, lines), jnp.int32)], axis=0).astype(F32)
        if lines < width:
            ids = jnp.concatenate([ids, jnp.zeros((16, width - lines), F32)], axis=1)
        self.rows[mine + (pl.ds(lines, 16), slice(None))] = ids.astype(BF)

    def gather_copies(self, stage, come=False):
        at, axis, geo = self.here.at, self.order[stage], self.geo
        done = self.order[:stage]
        f = at["f"] if geo.gf > 1 else 0
        if axis == "c":
            part = self.rows.at[at["c"]]
        elif "f" in done or geo.gf == 1:
            part = self.rows.at[at["c"], at["y"]]
        else:
            part = self.rows.at[at["c"], at["y"], f]
        partners = geo.size(axis) - 1
        out = []
        for p in range(partners):
            other = dict(at)
            other[axis] = self.here.step(axis, p)
            if axis == "c":
                theirs = self.rows.at[other["c"]]
            elif "f" in done or geo.gf == 1:
                theirs = self.rows.at[other["c"], other["y"]]
            else:
                theirs = self.rows.at[other["c"], other["y"], other["f"]]
            out.append((p, part, theirs))
        return [pltpu.make_async_remote_copy(
            src_ref=part, dst_ref=theirs if come else part, send_sem=self.sems[stage].at[0, p],
            recv_sem=self.sems[stage].at[1, p if come else partners - 1 - p],
            device_id=self.here.device(axis, p), device_id_type=MESH) for p, part, theirs in out]

    def start(self, stage):
        if stage >= self.gathers:
            return super().start(stage)
        for copy in self.gather_copies(stage):
            copy.start()

    def finish(self, stage):
        if stage >= self.gathers:
            return super().finish(stage)
        for copy in self.gather_copies(stage):
            copy.wait_send()
        for copy in self.gather_copies(stage, True):
            copy.wait_recv()
        if stage == self.gathers - 1:
            self.add_up()

    def add_up(self):
        plan, geo, at = self.plan, self.geo, self.here.at
        tall, lines, width = plan.embed_rows, plan.drows, plan.width
        share = plan.vocab // GROUPS
        rows = self.rows[...].reshape(2 * geo.ny * geo.gf, lines + 16, width)
        many = rows.shape[0]
        ids = rows[:, lines:, :].astype(F32)
        toks = jnp.concatenate([ids[i, 0:1, :lines] * 64.0 + ids[i, 1:2, :lines] for i in range(many)], axis=1)
        rows = jnp.concatenate([rows[i, :lines, :] for i in range(many)], axis=0)
        for s in range(geo.ns):
            group = ((at["y"] * 2 + at["c"]) * geo.ns + s) * geo.gf + (at["f"] if geo.gf > 1 else 0)
            first = share * group + (plan.vocab - share * GROUPS) * group // GROUPS
            hot = jnp.where((iota((tall, many * lines), 0) + first).astype(F32) == toks, 1.0, 0.0).astype(BF)
            value = dot(hot, rows)
            for c in range(width // 128):
                self.block[s, tall * c:tall * (c + 1), :] = value[:, 128 * c:128 * (c + 1)]


def loop(count, body):
    if count == 1:
        body(0, 0)
    else:
        lax.fori_loop(0, count, body, 0, unroll=min(count, 4))


class Sum:
    SCRIPT = {
        "begin": (0, 1, 2, 3), "dff1": (0, 0, 1, 1, 2, 2, 3, 3, 4, 5), "dself": (0, 0, 1, 1, 4, 4, 5, 5, 6, 7),
        "rows": (8,), "first2": (2, 2, 3, 3, 6, 6, 7, 7), "first4": (0, 0, 1, 1), "scan2": (0, 4, 4, 5, 5),
        "scan4": (1, 2, 2, 8, 8), "scan5": (3, 3), "scan6": (7, 7), "scan7": (6, 6), "second0": (2, 4, 4, 9),
        "second1": (3, 5, 5, 7, 7, 8, 8, 9, 9, 10), "second2": (6, 6, 8, 8, 9, 9, 10, 10, 11),
        "second3": (4, 5, 9, 9), "second4": (7, 11, 11, 12, 13), "ff0": (6, 10, 10, 12, 12), "ff1": (13, 13, 17),
        "ff2": (11, 11), "ff3": (10, 10, 12, 12, 15, 17, 17, 18), "out": (8, 9, 11, 11),
        "attn0": (13, 13, 15, 15, 16), "attn1": (12, 12, 18, 18), "attn2": (10, 16, 16, 17, 17),
        "attn3": (11, 13, 13, 18, 18), "end": (12, 14, 15, 15, 16, 16, 19, 20),
        "drain": (18, 18, 13, 17, 17, 14, 14, 19, 19, 20, 20, 15, 15, 16, 16, 18, 14, 14, 17, 19, 19, 20, 20, 14, 14, 15, 19, 19, 16, 20, 20, 14, 19, 20),
    }
    CUTS = (4, 2, 2, 4, 4, 2)
    DEPTH = 2

    def __init__(self, geo, plan):
        self.geo = geo
        orders = ("cfys", "cyfs") if geo.share == 1 else ("cysf", "csyf")
        ff = 2 * plan.ff // 128 * (plan.width // GROUPS)
        self.streams = []

        def cut(array, a, b, count):
            size = (b - a) // count // 16 * 16
            for i in range(count):
                end = b if i == count - 1 else a + size
                here = array > 1 or (array == 1 and geo.share == 1)
                self.streams.append(Stream(geo, array, a, end, orders[i % 2], BF, here, array == 0))
                a = end

        out, dec, rest, ctc, enc, last = self.CUTS
        cut(0, 0, plan.out_rows, out)
        cut(1, 0, ff, dec)
        cut(1, ff, plan.dec_rows, rest)
        self.row_stream = RowStream(geo, plan)
        self.streams.append(self.row_stream)
        self.streams.append(Stream(geo, 2, 0, 16, orders[0], F32, True))
        cut(2, 16, plan.ctc_rows, ctc)
        self.streams.append(Stream(geo, 3, 0, 16, orders[1], F32, True))
        cut(3, 16, 16 + ff, enc)
        cut(3, 16 + ff, plan.enc_rows, last)
        steps = [0] * len(self.streams)
        self.pools = {}
        for name in self.SCRIPT:
            for i in self.SCRIPT[name]:
                stream = self.streams[i]
                if steps[i] % 2 == 0 and self.pooled(stream) and not (steps[i] == 0 and stream.paired):
                    stage = steps[i] // 2
                    self.pools.setdefault((stage, self.streams[i].order if stage else "c"), []).append(i)
                steps[i] += 1
        if any(count != 8 for count in steps):
            raise ValueError("script")
        self.before, self.after, self.slot = {}, {}, {}
        for (stage, _), users in self.pools.items():
            for at, i in enumerate(users):
                self.slot[i, stage] = at % self.DEPTH
                if at >= self.DEPTH:
                    self.before[i, stage] = users[at - self.DEPTH]
                    self.after[users[at - self.DEPTH], stage] = i
        self.tall = max(stream.n for stream in self.streams if self.pooled(stream))

    def pooled(self, stream):
        return stream.dtype != F32 and stream is not self.row_stream

    def scratch(self):
        out = [pltpu.SemaphoreType.REGULAR((len(self.streams), 4))]
        for stage, order in sorted(self.pools):
            stream = next(stream for stream in self.streams if self.pooled(stream) and order in ("c", stream.order))
            for _ in range(self.DEPTH):
                out += stream.buffers(stage, self.tall)
        for stream in self.streams:
            out += stream.own()
            if stream.dtype == F32:
                for stage in range(4):
                    out += stream.buffers(stage, stream.n)
        return out

    def bind(self, here, arrays, refs, r_ref, bases):
        refs = list(refs)
        self.here, self.free = here, refs.pop(0)

        def take(count):
            out = refs[:count]
            del refs[:count]
            return out

        sets = {key: [take(2 if key[0] else 1) for _ in range(self.DEPTH)] for key in sorted(self.pools)}
        for i, stream in enumerate(self.streams):
            if stream is self.row_stream:
                stream.bind(here, take(len(stream.own())), r_ref, bases[-1])
                continue
            own = take(4 if stream.resident else 5)
            if stream.dtype == F32:
                buffers = [take(2 if stage else 1) for stage in range(4)]
            else:
                buffers = [sets[stage, stream.order if stage else "c"][self.slot[i, stage]] if (i, stage) in self.slot else []
                           for stage in range(4)]
            stream.bind(here, arrays, buffers, own, r_ref, bases[stream.array] + stream.a)
        self.steps = [0] * len(self.streams)

    def tick(self, name):
        for i in self.SCRIPT.get(name, ()):
            stage, ending = divmod(self.steps[i], 2)
            self.steps[i] += 1
            stream = self.streams[i]
            partners = self.geo.size(stream.order[stage]) - 1
            if ending:
                stream.finish(stage)
                if (i, stage) in self.after:
                    for p in range(partners):
                        pl.semaphore_signal(self.free.at[self.after[i, stage], stage], inc=1,
                                            device_id=self.here.device(stream.order[stage], p), device_id_type=MESH)
            else:
                if (i, stage) in self.before:
                    pl.semaphore_wait(self.free.at[i, stage], partners)
                stream.start(stage)


class Layout:
    def __init__(self, plan, geo, sizes):
        self.plan, self.share = plan, geo.share
        self.widths = [size // GROUPS // geo.share for size in sizes]
        self.starts = [int(x) for x in np.cumsum([0] + self.widths)]
        self.part = self.starts[-1]
        self.lines = -(-self.part // 1024) * 8
        self.base_dec = plan.out_rows
        self.base_embed = self.base_dec + plan.dec_rows
        self.base_ctc = self.base_embed + plan.embed_lines
        self.base_enc = self.base_ctc + plan.ctc_rows
        self.rows = self.base_enc + plan.enc_rows
        d, deep = plan.width, plan.width // GROUPS
        e, c = [self.base_enc + x for x in plan.enc_at], [self.base_dec + x for x in plan.dec_at]
        long = plan.ff // GROUPS
        attn, ff, two = 4 * d // 128, plan.ff // 128, d // 128
        self.place = [(e[3], plan.sub_rows, two), (e[2], deep, attn), (e[1], deep, ff), (e[0], long, two),
                      (c[3], deep, attn), (c[2], deep, attn), (c[0], deep, ff), (c[1], long, two),
                      (self.base_embed, plan.embed_rows, two), (self.base_ctc, deep, plan.out_rows // deep), (0, deep, plan.out_rows // deep)]

    def tile(self, weight, c):
        base, deep, _ = self.place[weight]
        return base + deep * c + (deep if weight == 9 and c > 0 else 0)

    def in_xla(self, r, bucket, dp, n_dp):
        index = bucket * n_dp + dp
        group, within = index // self.share, index % self.share
        pieces = []
        for weight, width in enumerate(self.widths):
            if weight >= 11:
                line, at = r[self.base_enc + weight - 11], 0
            else:
                _, deep, tiles = self.place[weight]
                block = jnp.concatenate([r[self.tile(weight, c):self.tile(weight, c) + deep] for c in range(tiles)], axis=1)
                if weight in (9, 10):
                    block = block[:, : self.plan.vocab]
                line, at = block.reshape(-1), 0
                if weight == 8:
                    at = group * (width * self.share) % self.plan.width
            pieces.append(lax.dynamic_slice(line, (at + within * width,), (width,)))
        flat = jnp.concatenate(pieces)
        return jnp.pad(flat, (0, self.lines * 128 - self.part)).reshape(self.lines, 128)

    def in_kernel(self, r, flat, work, group):
        flat[self.lines - 8:, :] = jnp.zeros((8, 128), F32)
        lane = iota((1, 128), 1)

        def put(value, base, length):
            lines, row, shift = -(-length // 128), base // 128, base % 128
            value = value[:lines]
            if shift == 0 and length % 128 == 0:
                flat[row:row + lines, :] = value
                return
            moved = pltpu.roll(value, shift, 1) if shift else value
            number = 128 * iota((lines, 128), 0) + (lane - shift) % 128
            right = (lane >= shift) & (number < length)
            flat[row:row + lines, :] = jnp.where(right, moved, flat[row:row + lines, :])
            if shift:
                left = (lane < shift) & (number < length)
                flat[row + 1:row + 1 + lines, :] = jnp.where(left, moved, flat[row + 1:row + 1 + lines, :])

        for weight, width in enumerate(self.widths):
            base = self.starts[weight]
            if weight >= 11:
                put(r[self.base_enc + weight - 11:self.base_enc + weight - 10, :], base, width)
                continue
            _, deep, tiles = self.place[weight]
            if weight == 8:
                for c in range(tiles):
                    at = self.tile(weight, c)
                    work[pl.ds(c, deep, stride=tiles), :] = r[at:at + deep, :]
                offset = lax.rem(group * width, self.plan.width)
                need = -(-width // 128)
                value = jnp.where(offset >= 128, work[1:need + 2, :], work[0:need + 1, :])
                turned = pltpu.roll(value, 64, 1)
                after = jnp.where(lane < 64, turned[:need], turned[1:])
                put(jnp.where(lax.rem(offset, 128) >= 64, after, value[:need]), base, width)
            elif weight in (9, 10):
                for c in range(tiles):
                    at = self.tile(weight, c)
                    work[pl.ds(c, deep, stride=tiles), :] = r[at:at + deep, :]
                for i in range(deep):
                    put(work[tiles * i:tiles * (i + 1), :], base + self.plan.vocab * i, self.plan.vocab)
            else:
                count = width // 128 // tiles
                for c in range(tiles):
                    at = self.tile(weight, c)
                    flat[pl.ds(base // 128 + c, count, stride=tiles), :] = r[at:at + count, :]


def tail_kernel(geo, plan, layout, total, utterances, counts, *refs):
    fused = geo.share == 1
    refs = list(refs)

    def take(count):
        out = refs[:count]
        del refs[:count]
        return out

    len_ref, count_ref, target_ref, enc, gain, bias, gg_in, gb_in, att = take(9)
    if fused:
        keep = take(9)
        names = ["dff1", "dff2", "cross", "self"]
    else:
        denc_in, row_in = take(2)
        names = []
    names += ["head", "bank", "perm", "attn", "ff1", "ff2", "h0", "qkv", "ctx", "h1", "h2"]
    names += ["master", "moment1", "moment2"] if fused else []
    far = take(len(names))
    pair = take(1)[0]
    g_far = None if fused else take(1)[0]
    out_ref, info_ref = take(2)
    near = dict(zip(names, take(len(far))))
    sems, g_ctc, g_enc, denc, gg, gb = take(6)
    g_dec = take(1)[0] if fused else None
    ctc_scratch, enc_scratch = take(counts[0]), take(counts[1])
    fused_scratch = take(counts[2])
    optimizer = [near[name] for name in ("master", "moment1", "moment2")] if fused else None
    here = Here(geo)
    r_ref = fused_scratch[0] if fused else out_ref
    dims = (2 * geo.ny, geo.ns * geo.gf)
    arrays = (pair, g_dec.reshape(*dims, plan.dec_rows, 128) if fused else g_far, g_ctc.reshape(*dims, plan.ctc_rows, 128),
              g_enc.reshape(*dims, plan.enc_rows, 128))
    total.bind(here, arrays, refs, r_ref, (0, layout.base_dec, layout.base_ctc, layout.base_enc, layout.base_embed))
    beside = Beside(sems)
    first = names.index("head")

    def load(some):
        for name in some:
            beside.start(name, far[names.index(name)], near[name])

    load(names[:first])
    here.greet()
    total.tick("begin")
    gg[...], gb[...] = gg_in[...], gb_in[...]
    if fused:
        beside.wait("dff1", "dff2")

        def tick(name):
            if name in ("cross", "self"):
                beside.wait(name)
            total.tick(name)
            if name == "dff1":
                load(names[first:])

        rows = dec_bwd_part(plan, tick, len_ref, target_ref, enc, near["self"], near["cross"], near["dff1"], near["dff2"], gain, bias,
                            keep, g_dec, gg, gb, denc)
    else:
        load(names)
        for name in ("dff0", "dff1", "cross", "self", "dself"):
            total.tick(name)
        rows = row_in[...]
        denc[...] = denc_in[...]
    total.row_stream.fill(rows, input_tokens(plan, target_ref))
    total.tick("rows")
    beside.wait("head")
    loss = ctc_part(plan, utterances, total.tick, len_ref, count_ref, target_ref, enc, near["head"], g_ctc, denc, *ctc_scratch)
    beside.wait(*names[names.index("bank"):])
    enc_bwd_part(plan, total.tick, len_ref, *[near[name] for name in ("bank", "perm", "attn", "ff1", "ff2")], gain, bias,
                 *[near[name] for name in ("h0", "qkv", "ctx", "h1", "h2")], denc, gg, gb, g_enc, *enc_scratch)
    if fused:
        weight_squares = square_sums(layout, optimizer, fused_scratch)
    total.tick("end")
    total.tick("drain")
    row = jnp.zeros((1, 128), F32) + (loss + att[0:1, :])
    if fused:
        group = ((here.at["y"] * 2 + here.at["c"]) * geo.ns + here.at["s"]) * geo.gf + here.at["f"]
        layout.in_kernel(r_ref, out_ref, fused_scratch[1], group)
        norms(geo, layout, here, out_ref, weight_squares, row, info_ref, fused_scratch)
    else:
        info_ref[0:1, :] = row
        info_ref[1:2, :] = row


def tail(geo, plan, layout, utterances, now, later, summed, ctc_scratch, enc_scratch, optimizer):
    fused = geo.share == 1
    total = Sum(geo, plan)
    extra = norm_scratch(geo, plan, layout) if fused else []
    later = list(later) + (list(optimizer) if fused else [])
    scratch = [pltpu.VMEM(x.shape, x.dtype) for x in later]
    scratch += [pltpu.SemaphoreType.DMA((len(later),)), pltpu.VMEM((GROUPS, plan.ctc_rows, 128), F32),
                pltpu.VMEM((GROUPS, plan.enc_rows, 128), F32), pltpu.VMEM((plan.rows, plan.width), F32),
                pltpu.VMEM((8, plan.width), F32), pltpu.VMEM((8, plan.width), F32)]
    scratch += [pltpu.VMEM((GROUPS, plan.dec_rows, 128), F32)] if fused else []
    scratch += ctc_scratch + enc_scratch + extra + total.scratch()
    lines = layout.lines if fused else layout.rows
    return pl.pallas_call(
        functools.partial(tail_kernel, geo, plan, layout, total, utterances, (len(ctc_scratch), len(enc_scratch), len(extra))),
        out_shape=[shape(lines, 128), shape(8, 128)],
        in_specs=[SM] * 2 + [VM] * (len(now) - 2) + [ANY] * (len(later) + len(summed)),
        out_specs=[VM] * 2,
        scratch_shapes=scratch,
        name="tail",
        compiler_params=pltpu.CompilerParams(vmem_limit_bytes=VMEM_LIMIT, collective_id=0, has_side_effects=True),
    )(*now, *later, *summed)


def share_sum(here, row, block, recv, sems, turn):
    devices, own = here.devices, here.index
    block[turn] = row
    recv[turn, pl.ds(own, 1)] = row.reshape(1, 1, 128)

    def copy(p, sender):
        other = lax.rem(own + 1 + p, devices)
        slot = own if sender else other
        return pltpu.make_async_remote_copy(
            src_ref=block.at[turn], dst_ref=recv.at[turn, slot], send_sem=sems.at[turn, 0, p], recv_sem=sems.at[turn, 1, slot],
            device_id=here.other(other), device_id_type=MESH)

    for p in range(devices - 1):
        copy(p, True).start()
    for p in range(devices - 1):
        copy(p, False).wait_recv()
    for p in range(devices - 1):
        copy(p, True).wait_send()
    return jnp.sum(recv[turn].reshape(devices, 128), axis=0, keepdims=True)


def edges(layout):
    full = layout.part // 128
    return full, layout.part - full * 128


def load_flat(layout, source, target):
    full, edge = edges(layout)
    target[0:full, :] = source[pl.ds(0, full * 128)].reshape(full, 128)
    if edge:
        target[full:full + 1, :] = jnp.zeros((1, 128), F32)
        target[full:full + 1, 0:edge] = source[pl.ds(full * 128, edge)].reshape(1, edge)


def store_flat(layout, target, value):
    full, edge = edges(layout)
    target[pl.ds(0, full * 128)] = value[0:full, :].reshape(full * 128).astype(target.dtype)
    if edge:
        target[pl.ds(full * 128, edge)] = value[full:full + 1, 0:edge].reshape(edge).astype(target.dtype)


def pieces(layout, m):
    lo, hi = layout.starts[m], layout.starts[m + 1]
    shared = []
    for at in sorted({lo // 128, hi // 128}):
        left, right = max(lo, at * 128) - at * 128, min(hi, at * 128 + 128) - at * 128
        if left < right and not (left == 0 and right == 128):
            shared.append((at, left, right))
    return (-(-lo // 128), hi // 128), shared


def matrix_sums(layout, ref):
    lane = iota((1, 128), 1)
    out = jnp.zeros((1, 128), F32)
    for m in range(len(layout.widths)):
        (r0, r1), shared = pieces(layout, m)
        total = jnp.zeros((1, 128), F32)
        if r1 > r0:
            total = total + jnp.sum(ref[r0:r1, :], axis=0, keepdims=True)
        for at, left, right in shared:
            total = total + jnp.where((lane >= left) & (lane < right), ref[at:at + 1, :], 0.0)
        out = jnp.where(lane == m, jnp.sum(total, axis=1, keepdims=True), out)
    return out


def norm_scratch(geo, plan, layout):
    devices = 2 * geo.ny * geo.ns * geo.nf
    flat = pltpu.VMEM((layout.lines, 128), F32)
    return [pltpu.VMEM((layout.rows, 128), F32), pltpu.VMEM((plan.embed_rows * plan.width // 128, 128), F32), flat, flat, flat, flat,
            pltpu.VMEM((2, 1, 128), F32), pltpu.VMEM((2, devices, 1, 128), F32), pltpu.SemaphoreType.DMA((2, 2, devices))]


def square_sums(layout, optimizer, scratch):
    w, a, b, sq = scratch[2:6]
    lines = sum(1 if x else 0 for x in edges(layout)[1:]) + edges(layout)[0]
    for source, target in zip(optimizer, (w, a, b)):
        load_flat(layout, source, target)
    sq[0:lines, :] = w[0:lines, :] * w[0:lines, :]
    return matrix_sums(layout, sq)


def adam(g, clip, w, a, b):
    scaled = g * jnp.minimum(1.0, 1.0 / clip)
    first = 0.5 * a + 0.5 * scaled
    second = 0.5 * b + 0.5 * scaled * scaled
    correct = 1.0 - 0.5**STEP
    return first, second, first / correct / (jnp.sqrt(second / correct) + 1e-06) + 0.01 * w


def norms(geo, layout, here, g_ref, weight_squares, loss, info_ref, scratch):
    w, a, b, sq, block, recv, sems = scratch[2:9]
    full, edge = edges(layout)
    lines = full + (1 if edge else 0)
    lane = iota((1, 128), 1)
    g = g_ref[0:lines, :]
    squares = jnp.sum(jnp.sum(g * g, axis=0, keepdims=True), axis=1, keepdims=True)
    row = jnp.where(lane == 120, squares, jnp.where(lane == 121, loss, weight_squares))
    row = share_sum(here, row, block, recv, sems, 0)
    info_ref[0:1, :] = row
    clip = jnp.sqrt(jnp.sum(jnp.where(lane == 120, row, 0.0), axis=1, keepdims=True))
    _, _, direction = adam(g, clip, w[0:lines, :], a[0:lines, :], b[0:lines, :])
    sq[0:lines, :] = direction * direction
    row = share_sum(here, matrix_sums(layout, sq), block, recv, sems, 1)
    info_ref[1:2, :] = row


def norm_kernel(geo, layout, g_ref, master, moment1, moment2, loss_ref, info_ref, *scratch):
    here = Here(geo)
    here.greet()
    weight_squares = square_sums(layout, (master, moment1, moment2), scratch)
    norms(geo, layout, here, g_ref, weight_squares, loss_ref[0:1, :], info_ref, scratch)


def update_kernel(layout, utterances, g_ref, master, moment1, moment2, info_ref,
                  loss_ref, clip_ref, first_ref, second_ref, fresh_ref, low_ref, wn_ref, un_ref, w, a, b):
    full, edge = edges(layout)
    lines, count = full + (1 if edge else 0), len(layout.widths)
    lane = iota((1, 128), 1)
    for source, target in ((master, w), (moment1, a), (moment2, b)):
        load_flat(layout, source, target)
    row = info_ref[0:1, :]
    clip = jnp.sqrt(jnp.sum(jnp.where(lane == 120, row, 0.0), axis=1, keepdims=True))
    loss_ref[0] = jnp.sum(jnp.where(lane == 121, row, 0.0)) / utterances
    clip_ref[0] = jnp.sum(clip)
    weight_norms, update_norms = jnp.sqrt(row), jnp.sqrt(info_ref[1:2, :])
    wn_ref[...] = weight_norms[:, 0:count].reshape(count)
    un_ref[...] = update_norms[:, 0:count].reshape(count)
    ratio = 0.5 * weight_norms / update_norms
    first, second, direction = adam(g_ref[0:lines, :], clip, w[0:lines, :], a[0:lines, :], b[0:lines, :])
    store_flat(layout, first_ref, first)
    store_flat(layout, second_ref, second)
    a[0:lines, :] = direction
    for m in range(count):
        scale = jnp.sum(jnp.where(lane == m, ratio, 0.0), axis=1, keepdims=True)
        (r0, r1), shared = pieces(layout, m)
        if r1 > r0:
            w[r0:r1, :] -= scale * a[r0:r1, :]
        for at, left, right in shared:
            w[at:at + 1, :] -= jnp.where((lane >= left) & (lane < right), scale * a[at:at + 1, :], 0.0)
    fresh = w[0:lines, :]
    store_flat(layout, fresh_ref, fresh)
    store_flat(layout, low_ref, fresh)


def update(layout, utterances, g, optimizer, info):
    part, lines, count = layout.part, layout.lines, len(layout.widths)
    loss, clip, *rest = pl.pallas_call(
        functools.partial(update_kernel, layout, utterances),
        out_shape=[shape(1), shape(1), shape(part), shape(part), shape(part), shape(part, dtype=BF), shape(count), shape(count)],
        in_specs=[VM] * 5,
        out_specs=[SM, SM] + [VM] * 6,
        scratch_shapes=[pltpu.VMEM((lines, 128), F32)] * 3,
        name="update",
        compiler_params=pltpu.CompilerParams(vmem_limit_bytes=VMEM_LIMIT),
    )(g, *optimizer, info)
    return (loss[0], clip[0], *rest)


def solution(mesh):
    n_bucket, n_dp = mesh.shape["bucket"], mesh.shape["dp"]
    geo = Geometry(n_bucket, n_dp)

    def body(filter_bank, frame_len, tok_len, targets, *rest):
        weights, optimizer = rest[:13], rest[13:]
        utterances = frame_len.shape[0] * n_bucket * n_dp
        plan, *rest = front(geo, n_bucket, utterances, filter_bank, frame_len, tok_len, targets, weights)
        layout = Layout(plan, geo, [w.size for w in weights])
        out, info = tail(geo, plan, layout, utterances, *rest, optimizer)
        if geo.share == 1:
            return update(layout, utterances, out, optimizer, info)
        g = layout.in_xla(out, lax.axis_index("bucket"), lax.axis_index("dp"), n_dp)
        info = pl.pallas_call(
            functools.partial(norm_kernel, geo, layout),
            out_shape=shape(8, 128), in_specs=[VM] * 5, out_specs=VM, scratch_shapes=norm_scratch(geo, plan, layout), name="norms",
            compiler_params=pltpu.CompilerParams(vmem_limit_bytes=VMEM_LIMIT, collective_id=2, has_side_effects=True),
        )(g, *optimizer, info)
        return update(layout, utterances, g, optimizer, info)

    both = P(("bucket", "dp"))
    in_specs = (P(("bucket", "dp"), None, None), both, both, P(("bucket", "dp"), None)) + (P(),) * 13 + (both,) * 3
    out_specs = (P(), P(), both, both, both, both, P(), P())
    return jax.shard_map(body, mesh=mesh, in_specs=in_specs, out_specs=out_specs, check_vma=False)
```
